32 devices in a mesh: dp: 8 (over z, y), fsdp: 4 (over x, core).
Axes of the slice: x: 2, y: 2, z: 4, core: 2. Of those that a mesh axis runs over, the one named last changes fastest.
Arguments:
- block_input: bfloat16 [64, 128, 1536], P(('dp', 'fsdp')), may hold values from -6 to 6
- caption: bfloat16 [64, 256, 4096], P(('dp', 'fsdp')), may hold values from -6 to 6
- modulation: float32 [64, 4, 1536], P(('dp', 'fsdp')), may hold values from -2.5 to 2.5
- segment_ids: int32 [64, 128], P(('dp', 'fsdp')), may hold values from 0 to 127, as said below
- pos_row: int32 [64, 128], P(('dp', 'fsdp')), may hold values from 0 to 63
- pos_col: int32 [64, 128], P(('dp', 'fsdp')), may hold values from 0 to 10
- caption_len: int32 [64], P(('dp', 'fsdp')), may hold values from 64 to 256, as said below
- gain_attn: bfloat16 [1536], P('fsdp'), may hold values from 0.25 to 1.75
- w_query: bfloat16 [1536, 1536], P('fsdp'), may hold values from -0.15625 to 0.15625
- w_key: bfloat16 [1536, 1536], P('fsdp'), may hold values from -0.15625 to 0.15625
- w_value: bfloat16 [1536, 1536], P('fsdp'), may hold values from -0.15625 to 0.15625
- gain_query: bfloat16 [64], P('fsdp'), may hold values from 0.25 to 1.75
- gain_key: bfloat16 [64], P('fsdp'), may hold values from 0.25 to 1.75
- w_cap_key: bfloat16 [4096, 1536], P('fsdp'), may hold values from -0.09375 to 0.09375
- w_cap_value: bfloat16 [4096, 1536], P('fsdp'), may hold values from -0.09375 to 0.09375
- gain_cap_key: bfloat16 [64], P('fsdp'), may hold values from 0.25 to 1.75
- head_gate: bfloat16 [24], P('fsdp'), may hold values from -3 to 3
- w_out: bfloat16 [1536, 1536], P('fsdp'), may hold values from -0.625 to 0.625
- gain_ffn: bfloat16 [1536], P('fsdp'), may hold values from 0.25 to 1.75
- w_gate: bfloat16 [1536, 4096], P('fsdp'), may hold values from -0.15625 to 0.15625
- w_up: bfloat16 [1536, 4096], P('fsdp'), may hold values from -0.15625 to 0.15625
- w_down: bfloat16 [4096, 1536], P('fsdp'), may hold values from -0.09375 to 0.09375
- cotangent: bfloat16 [64, 128, 1536], P(('dp', 'fsdp')), may hold values from -6 to 6
Outputs:
- block_out: bfloat16 [64, 128, 1536], P(('dp', 'fsdp'))
- input_grad: bfloat16 [64, 128, 1536], P(('dp', 'fsdp'))
- modulation_grad: float32 [64, 4, 1536], P(('dp', 'fsdp'))
- grad_gain_attn: float32 [1536], P('fsdp')
- grad_w_query: float32 [1536, 1536], P('fsdp', 'dp')
- grad_w_key: float32 [1536, 1536], P('fsdp', 'dp')
- grad_w_value: float32 [1536, 1536], P('fsdp', 'dp')
- grad_gain_query: float32 [64], P('fsdp')
- grad_gain_key: float32 [64], P('fsdp')
- grad_w_cap_key: float32 [4096, 1536], P('fsdp', 'dp')
- grad_w_cap_value: float32 [4096, 1536], P('fsdp', 'dp')
- grad_gain_cap_key: float32 [64], P('fsdp')
- grad_head_gate: float32 [24], P('fsdp')
- grad_w_out: float32 [1536, 1536], P('fsdp', 'dp')
- grad_gain_ffn: float32 [1536], P('fsdp')
- grad_w_gate: float32 [1536, 4096], P('fsdp', 'dp')
- grad_w_up: float32 [1536, 4096], P('fsdp', 'dp')
- grad_w_down: float32 [4096, 1536], P('fsdp', 'dp')
The draws below stay inside these ranges and needn't reach their ends.
Inputs may be any that keep to these rules, and one draw needn't show every extreme that they name: `segment_ids`: within a row the ids start at 0 and rise by at most one from token to token; each image, a run of equal ids, lays its tokens out in raster order on a grid 2 to 11 columns wide, which pos_row and pos_col give. Caption positions from caption_len on are padding.
All inputs are finite; a program needn't handle non-finite values.
Results may differ from the reference program's by a relative error of at most 0.018.
Values may be sent and summed in bfloat16 or wider, within the bound.
No kernel may reach another device: no remote copies, remote signals or barrier semaphores. Data moves between devices by JAX's collectives and lax.ppermute only.
A program may use at most 384 MiB of HBM per device.

```python
import math
import jax
import jax.numpy as jnp
from jax import lax

D = 1536
HEADS = 24
HEAD = 64
FF = 4096
CAP = 4096
CAP_TOK = 256
SEQ = 128
HD = 1536
ROWS = 64


def image_layout(key):
    mark_key, shape_key, pick_key = jax.random.split(key, 3)
    boundary_draw = jax.random.randint(mark_key, (ROWS, SEQ), 0, max(SEQ // 4, 2)) == 0
    widths = jax.random.randint(shape_key, (ROWS, SEQ), 2, 12)
    first_row = jax.random.randint(pick_key, (), 0, ROWS)
    row_index = jnp.arange(ROWS, dtype=jnp.int32)[:, None]
    narrow_row = row_index == first_row
    split_row = row_index == (first_row + 1) % ROWS
    wide_row = row_index == (first_row + 2) % ROWS
    single_image = jnp.logical_or(narrow_row, wide_row)
    boundary_draw = jnp.where(single_image, False, boundary_draw)
    boundary_draw = jnp.where(split_row, True, boundary_draw)
    widths = jnp.where(narrow_row, 2, widths)
    widths = jnp.where(wide_row, 11, widths)
    positions = jnp.arange(SEQ, dtype=jnp.int32)[None, :]
    starts_here = jnp.logical_or(boundary_draw, positions == 0)
    start_of = lax.cummax(jnp.where(starts_here, positions, 0), axis=1)
    segment = jnp.cumsum(starts_here.astype(jnp.int32), axis=1) - 1
    image_width = jnp.take_along_axis(widths, start_of, axis=1)
    offset = positions - start_of
    return (segment, offset // image_width, offset % image_width)


def draw_segment_ids(key, part):
    layout = image_layout(key)
    return layout[0].astype(jnp.int32)


def draw_pos_row(key, part):
    layout = image_layout(key)
    return layout[1].astype(jnp.int32)


def draw_pos_col(key, part):
    layout = image_layout(key)
    return layout[2].astype(jnp.int32)


def draw_caption_len(key, part):
    key = jax.random.fold_in(key, 14)
    length_key, first_key, second_key = jax.random.split(key, 3)
    lengths = jax.random.randint(length_key, (ROWS,), CAP_TOK // 4, CAP_TOK + 1)
    first_row = jax.random.randint(first_key, (), 0, ROWS)
    second_row = (first_row + jax.random.randint(second_key, (), 1, ROWS)) % ROWS
    lengths = lengths.at[first_row].set(CAP_TOK).at[second_row].set(CAP_TOK // 4)
    return lengths.astype(jnp.int32)


def level_of(key, extent, cuts, smallest, largest):
    level, own = 1.0, jax.random.fold_in(key, 6)
    for dim, parts in cuts:
        steps = jnp.exp(jax.random.uniform(jax.random.fold_in(own, dim), (parts,), jnp.float32, smallest / len(cuts), largest / len(cuts)))
        level = level * jnp.repeat(steps, extent[dim] // parts).reshape([-1 if axis == dim else 1 for axis in range(len(extent))])
    return level


def scatter_about(rng, shape, width, most, cuts=(), kind=jnp.bfloat16):
    array = width * jax.random.normal(rng, shape, jnp.float32)
    if cuts:
        array = array * level_of(rng, shape, cuts, -0.22, 0.18)
    return jnp.clip(array, -most, most).astype(kind)


def setup_inputs(seed: int = 0) -> dict:
    key_list = jax.random.split(jax.random.key(seed), 24)
    return {
        "block_input": scatter_about(key_list[0], (ROWS, SEQ, D), 1.0, 6.0, ((0, 32),)),
        "caption": scatter_about(key_list[1], (ROWS, CAP_TOK, CAP), 1.0, 6.0, ((0, 32),)),
        "modulation": scatter_about(key_list[2], (ROWS, 4, D), 0.5, 2.5, ((0, 32),), jnp.float32),
        "segment_ids": draw_segment_ids(jax.random.fold_in(key_list[23], 71), 0),
        "pos_row": draw_pos_row(jax.random.fold_in(key_list[23], 71), 0),
        "pos_col": draw_pos_col(jax.random.fold_in(key_list[23], 71), 0),
        "caption_len": draw_caption_len(jax.random.fold_in(key_list[23], 71), 0),
        "gain_attn": jnp.clip(1.0 + 0.15 * jax.random.normal(key_list[7], (D,), jnp.float32), 0.25, 1.75).astype(jnp.bfloat16),
        "w_query": scatter_about(key_list[8], (D, HD), D ** -0.5, 0.15625, ((0, 4),)),
        "w_key": scatter_about(key_list[9], (D, HD), D ** -0.5, 0.15625, ((0, 4),)),
        "w_value": scatter_about(key_list[10], (D, HD), D ** -0.5, 0.15625, ((0, 4),)),
        "gain_query": jnp.clip(1.0 + 0.15 * jax.random.normal(key_list[11], (HEAD,), jnp.float32), 0.25, 1.75).astype(jnp.bfloat16),
        "gain_key": jnp.clip(1.0 + 0.15 * jax.random.normal(key_list[12], (HEAD,), jnp.float32), 0.25, 1.75).astype(jnp.bfloat16),
        "w_cap_key": scatter_about(key_list[13], (CAP, HD), CAP ** -0.5, 0.09375, ((0, 4),)),
        "w_cap_value": scatter_about(key_list[14], (CAP, HD), CAP ** -0.5, 0.09375, ((0, 4),)),
        "gain_cap_key": jnp.clip(1.0 + 0.15 * jax.random.normal(key_list[15], (HEAD,), jnp.float32), 0.25, 1.75).astype(jnp.bfloat16),
        "head_gate": scatter_about(key_list[16], (HEADS,), 1.0, 3.0, ((0, 4),)),
        "w_out": scatter_about(key_list[17], (HD, D), (HD // 16) ** -0.5, 0.625, ((0, 4),)),
        "gain_ffn": jnp.clip(1.0 + 0.15 * jax.random.normal(key_list[18], (D,), jnp.float32), 0.25, 1.75).astype(jnp.bfloat16),
        "w_gate": scatter_about(key_list[19], (D, FF), D ** -0.5, 0.15625, ((0, 4),)),
        "w_up": scatter_about(key_list[20], (D, FF), D ** -0.5, 0.15625, ((0, 4),)),
        "w_down": scatter_about(key_list[21], (FF, D), FF ** -0.5, 0.09375, ((0, 4),)),
        "cotangent": scatter_about(key_list[22], (ROWS, SEQ, D), 1.0, 6.0, ((0, 32),)),
    }


EPSILON = 1e-06
NEGATIVE = -1e+30
HIGHEST = lax.Precision.HIGHEST

@jax.custom_vjp
def low(v):
    return lax.optimization_barrier(v.astype(jnp.bfloat16)).astype(jnp.float32)

@jax.custom_vjp
def low_back(v):
    return v

def low_keep(v):
    return (low(v), None)

def low_pass(kept, grad):
    return (grad,)

def back_keep(v):
    return (v, None)

def back_low(kept, grad):
    return (low(grad),)
low.defvjp(low_keep, low_pass)
low_back.defvjp(back_keep, back_low)

def angle_tables(rows_pos, cols_pos, head_size):
    quarter = head_size // 4
    frequency = jnp.exp(jnp.arange(quarter, dtype=jnp.float32) * (-math.log(10000.0) / quarter))
    row_angle = rows_pos.astype(jnp.float32)[..., None] * frequency
    col_angle = cols_pos.astype(jnp.float32)[..., None] * frequency
    angles = jnp.concatenate([row_angle, row_angle, col_angle, col_angle], axis=-1)[:, :, None, :]
    return (jnp.cos(angles), jnp.sin(angles))

def quarter_turn(values):
    shaped = values.reshape(values.shape[:-1] + (2, 2, values.shape[-1] // 4))
    turned = jnp.stack([-shaped[..., 1, :], shaped[..., 0, :]], axis=-2)
    return turned.reshape(values.shape)

def rotary(values, cos_table, sin_table):
    return values * cos_table + quarter_turn(values) * sin_table

def rms_scale(values):
    return values * lax.rsqrt(lax.optimization_barrier(jnp.mean(values * values, axis=-1, keepdims=True)) + EPSILON)

def head_split(values, head_size):
    return values.reshape(values.shape[:-1] + (values.shape[-1] // head_size, head_size))

def project(operand, weight_matrix):
    return jnp.einsum('...c,ce->...e', operand, weight_matrix, precision=HIGHEST)

def attend(queries, keys, values, allowed, scaling):
    scores = low_back(jnp.einsum('rqhd,rkhd->rhqk', queries, keys, precision=HIGHEST) * scaling)
    weights = jax.nn.softmax(jnp.where(allowed, scores, NEGATIVE), axis=-1)
    return jnp.einsum('rhqk,rkhd->rqhd', low(weights), values, precision=HIGHEST)

def forward(params, inputs, modulation, caption, same_segment, caption_mask, cos_table, sin_table):
    gain_attn, w_query, w_key, w_value, gain_query, gain_key, w_cap_key, w_cap_value, gain_cap_key, head_gate, w_out, gain_ffn, w_gate, w_up, w_down = params
    head_size = gain_query.shape[0]
    scaling = 1.0 / math.sqrt(head_size)
    attn_in = low(rms_scale(inputs) * gain_attn * (1.0 + modulation[:, 0][:, None, :]))
    query_raw = low_back(project(attn_in, w_query))
    key_raw = low_back(project(attn_in, w_key))
    value_heads = head_split(low(low_back(project(attn_in, w_value))), head_size)
    queries = low(rotary(rms_scale(head_split(query_raw, head_size)) * gain_query, cos_table, sin_table))
    keys = low(rotary(rms_scale(head_split(key_raw, head_size)) * gain_key, cos_table, sin_table))
    cap_key_raw = low_back(project(caption, w_cap_key))
    cap_keys = low(rms_scale(head_split(cap_key_raw, head_size)) * gain_cap_key)
    cap_values = head_split(low(low_back(project(caption, w_cap_value))), head_size)
    self_out = attend(queries, keys, value_heads, same_segment[:, None, :, :], scaling)
    cross_out = attend(queries, cap_keys, cap_values, caption_mask[:, None, None, :], scaling)
    gate_heads = jnp.tanh(head_gate)[:, None]
    mixed = low(low_back(self_out + gate_heads * low_back(cross_out)))
    mixed = mixed.reshape(mixed.shape[:2] + (-1,))
    attn_branch = low_back(project(mixed, w_out))
    hidden = inputs + jnp.tanh(modulation[:, 1])[:, None, :] * attn_branch
    ffn_in = low(rms_scale(hidden) * gain_ffn * (1.0 + modulation[:, 2][:, None, :]))
    gate_proj = low_back(project(ffn_in, w_gate))
    up_proj = low_back(project(ffn_in, w_up))
    ffn_branch = low_back(project(low(jax.nn.silu(gate_proj) * up_proj), w_down))
    return hidden + jnp.tanh(modulation[:, 3])[:, None, :] * ffn_branch

def reference(block_input, caption, modulation, segment_ids, pos_row, pos_col, caption_len, gain_attn, w_query, w_key, w_value, gain_query, gain_key, w_cap_key, w_cap_value, gain_cap_key, head_gate, w_out, gain_ffn, w_gate, w_up, w_down, cotangent):
    params = tuple((weight_array.astype(jnp.float32) for weight_array in (gain_attn, w_query, w_key, w_value, gain_query, gain_key, w_cap_key, w_cap_value, gain_cap_key, head_gate, w_out, gain_ffn, w_gate, w_up, w_down)))
    block_rows = math.gcd(ROWS, 32)
    block_count = ROWS // block_rows

    def by_block(values):
        return values.reshape((block_count, block_rows) + values.shape[1:])
    blocked = (by_block(block_input), by_block(caption), by_block(modulation), by_block(segment_ids), by_block(pos_row), by_block(pos_col), by_block(caption_len), by_block(cotangent))

    def block_step(running, pieces):
        input_block, caption_block, mod_block, segment_block, row_block, col_block, length_block, cot_block = pieces
        cos_table, sin_table = angle_tables(row_block, col_block, HEAD)
        caption_mask = jnp.arange(CAP_TOK, dtype=jnp.int32)[None, :] < length_block[:, None]
        same_segment = segment_block[:, :, None] == segment_block[:, None, :]
        caption_float = caption_block.astype(jnp.float32)

        def layer_fn(param_set, input_float, mod_float):
            return forward(param_set, input_float, mod_float, caption_float, same_segment, caption_mask, cos_table, sin_table)
        result, pullback = jax.vjp(layer_fn, params, input_block.astype(jnp.float32), mod_block)
        grad_params, grad_inputs, grad_mod = pullback(cot_block.astype(jnp.float32))
        running = jax.tree.map(jnp.add, running, grad_params)
        return (running, (result.astype(jnp.bfloat16), grad_inputs.astype(jnp.bfloat16), grad_mod))
    zeros = tuple((jnp.zeros_like(weight_array) for weight_array in params))
    running, (results, input_grads, mod_grads) = lax.scan(block_step, zeros, blocked)
    return (results.reshape(ROWS, SEQ, D), input_grads.reshape(ROWS, SEQ, D), mod_grads.reshape(ROWS, 4, D), running[0], running[1], running[2], running[3], running[4], running[5], running[6], running[7], running[8], running[9], running[10], running[11], running[12], running[13], running[14])
```

```python
import math

import jax
import jax.numpy as jnp
from jax import lax
from jax.sharding import PartitionSpec as P

EPSILON = 1e-06
NEGATIVE = -1e30
BF16 = jnp.bfloat16
F32 = jnp.float32


def angle_tables(rows_pos, cols_pos, head_size):
    quarter = head_size // 4
    frequency = jnp.exp(jnp.arange(quarter, dtype=F32) * (-math.log(10000.0) / quarter))
    row_angle = rows_pos.astype(F32)[..., None] * frequency
    col_angle = cols_pos.astype(F32)[..., None] * frequency
    angles = jnp.concatenate([row_angle, row_angle, col_angle, col_angle], axis=-1)[:, :, None, :]
    return (jnp.cos(angles), jnp.sin(angles))


def quarter_turn(values):
    shaped = values.reshape(values.shape[:-1] + (2, 2, values.shape[-1] // 4))
    turned = jnp.stack([-shaped[..., 1, :], shaped[..., 0, :]], axis=-2)
    return turned.reshape(values.shape)


def rms_scale(values):
    inverse = lax.rsqrt(jnp.mean(values * values, axis=-1, keepdims=True) + EPSILON)
    return (values * inverse, inverse)


def rms_back(incoming, normed, inverse):
    return inverse * (incoming - normed * jnp.mean(incoming * normed, axis=-1, keepdims=True))


def dot(left, right):
    return jnp.einsum("tc,ce->te", left, right, preferred_element_type=F32)


def dot_back(incoming, weight):
    return jnp.einsum("te,ce->tc", incoming, weight, preferred_element_type=F32)


def dot_tokens(left, right):
    return jnp.einsum("tc,te->ce", left, right, preferred_element_type=F32)


def head_norm(projected, gain_vec, head_size):
    per_head = projected.reshape(
        projected.shape[:-1] + (projected.shape[-1] // head_size, head_size)
    )
    normed, inverse = rms_scale(per_head)
    return (normed * gain_vec, normed, inverse)


def head_norm_back(incoming, normed, inverse, gain_vec):
    grad_gain = jnp.sum(incoming * normed, axis=(0, 1, 2))
    grad_projected = rms_back(incoming * gain_vec, normed, inverse)
    return (
        grad_gain,
        grad_projected.reshape(-1, grad_projected.shape[2] * grad_projected.shape[3]).astype(BF16),
    )


def attend_weights(queries, keys, allowed, scaling):
    scores = jnp.einsum("rqhd,rkhd->rhqk", queries, keys, preferred_element_type=F32) * scaling
    return jax.nn.softmax(jnp.where(allowed, scores, NEGATIVE), axis=-1)


def attend_back(weights, grad_output, values, queries, keys, scaling):
    grad_weights = jnp.einsum("rqhd,rkhd->rhqk", grad_output, values, preferred_element_type=F32)
    centre = jnp.sum(grad_weights * weights, axis=-1, keepdims=True)
    grad_scores = (weights * (grad_weights - centre)).astype(BF16)
    grad_values = jnp.einsum(
        "rhqk,rqhd->rkhd", weights.astype(BF16), grad_output, preferred_element_type=F32
    ).astype(BF16)
    grad_queries = (
        jnp.einsum("rhqk,rkhd->rqhd", grad_scores, keys, preferred_element_type=F32) * scaling
    )
    grad_keys = (
        jnp.einsum("rhqk,rqhd->rkhd", grad_scores, queries, preferred_element_type=F32) * scaling
    )
    return (grad_queries, grad_keys, grad_values)


def unrotate(incoming, cos_table, sin_table):
    return incoming * cos_table - quarter_turn(incoming * sin_table)


class Place:
    def __init__(self, mesh):
        self.copies = mesh.shape["dp"]
        self.shards = mesh.shape["fsdp"]
        self.top_step = self.copies // 2
        self.team_step = self.copies // 4
        self.low = self.copies // 4

    def locate(self):
        self.dp = lax.axis_index("dp")
        self.fsdp = lax.axis_index("fsdp")
        self.side = self.fsdp // 2
        self.core = self.fsdp % 2
        self.top = self.dp // self.top_step
        self.team = (self.dp // self.team_step) % 2
        self.lane = self.dp % 2
        self.quarter = 2 * self.core + self.team

    def swap(self, value, dp=0, fsdp=0):
        if not dp:
            pairs = [(i, i ^ fsdp) for i in range(self.shards)]
            return lax.ppermute(value, "fsdp", pairs)
        if not fsdp:
            pairs = [(i, i ^ dp) for i in range(self.copies)]
            return lax.ppermute(value, "dp", pairs)
        return self.route(value, lambda d, f: (d ^ dp, f ^ fsdp))

    def route(self, value, target):
        pairs = []
        for d in range(self.copies):
            for f in range(self.shards):
                to = target(d, f)
                if to is not None:
                    pairs.append((d * self.shards + f, to[0] * self.shards + to[1]))
        return lax.ppermute(value, ("dp", "fsdp"), pairs)

    def bits(self, d, f):
        return ((d // self.team_step) % 2, f // 2, f % 2, d % 2)


    def gather_tokens(self, block):
        mine = jnp.concatenate([block, self.swap(block, dp=self.team_step)], axis=0)
        return jnp.concatenate([mine, self.swap(mine, fsdp=1)], axis=0)

    def reduce_tokens(self, pairs, product):
        half = pairs[0][0].shape[0] // 2
        block = half // 2

        def part(start, stop):
            return sum(product(left[start:stop], right) for left, right in pairs)

        away = self.swap(part(half, 2 * half).astype(BF16), fsdp=1).astype(F32)
        other = self.swap((part(block, half) + away[block:]).astype(BF16), dp=self.team_step)
        return part(0, block) + away[:block] + other.astype(F32)


    def columns(self, shard):
        width = shard.shape[1] // 4

        def cut(quarter):
            return lax.dynamic_slice_in_dim(shard, quarter * width, width, axis=1)

        near = self.swap(cut(2 * (1 - self.core) + self.team), fsdp=1)
        sent = cut(2 * (self.core ^ self.lane) + self.team)
        across = self.route(sent, lambda d, f: (d, f ^ 2 ^ (d % 2)))
        far = self.swap(across, dp=1)
        full = jnp.zeros((4,) + near.shape, shard.dtype)
        full = lax.dynamic_update_index_in_dim(full, cut(self.quarter), self.fsdp, 0)
        full = lax.dynamic_update_index_in_dim(full, near, self.fsdp ^ 1, 0)
        full = lax.dynamic_update_index_in_dim(full, across, self.fsdp ^ 2 ^ self.lane, 0)
        full = lax.dynamic_update_index_in_dim(full, far, self.fsdp ^ 3 ^ self.lane, 0)
        return full.reshape(-1, width)

    def rows(self, shard):
        half = shard.shape[0] // 2

        def near_target(d, f):
            team, side, core, _ = self.bits(d, f)
            return (d, 2 * side + side) if core == team and side != team else None

        def far_target(d, f):
            team, side, core, _ = self.bits(d, f)
            return (d, 2 * (1 - side) + side) if core == team else None

        near = self.route(shard, near_target)
        piece = lax.dynamic_slice_in_dim(shard, self.lane * half, half, axis=0)
        across = self.route(piece, far_target)
        far = self.swap(across, dp=1)
        first = jnp.where(self.lane == 0, across, far)
        second = jnp.where(self.lane == 0, far, across)
        home = jnp.where(self.side == self.team, shard, near)
        return jnp.where(
            self.core == self.side, home, jnp.concatenate([first, second], axis=0)
        )


    def halve(self, value, axis, keep, dp=0, fsdp=0):
        sent = lax.dynamic_index_in_dim(value, 1 - keep, axis, keepdims=False)
        kept = lax.dynamic_index_in_dim(value, keep, axis, keepdims=False)
        got = self.swap(sent.astype(BF16), dp=dp, fsdp=fsdp)
        return kept.astype(F32) + got.astype(F32)

    def halve_low(self, value):
        step = self.low // 2
        while step:
            value = value.reshape((2, step) + value.shape[1:])
            value = self.halve(value, 0, (self.dp // step) % 2, dp=step)
            step //= 2
        return value[0]

    def columns_back(self, grad, side_first):
        columns, rows = grad.shape
        value = grad.reshape(self.low, columns // self.low, 2, rows // 2)
        if side_first:
            value = self.halve(value, 2, self.side, fsdp=2)
            value = self.halve_low(value)
        else:
            value = self.halve_low(value)
            value = self.halve(value, 1, self.side, fsdp=2)
        value = value.astype(BF16).reshape(columns // self.low, 2, rows // 4)
        own = lax.dynamic_index_in_dim(value, self.core, 1, keepdims=False)
        got = self.swap(
            lax.dynamic_index_in_dim(value, 1 - self.core, 1, keepdims=False), fsdp=1
        )
        straight = self.core == self.top
        sent = jnp.where(straight, got, own)
        kept = jnp.where(straight, own, got)
        total = kept.astype(F32) + self.swap(sent, dp=self.top_step).astype(F32)
        return total.T

    def rows_back(self, grad, side_first):
        columns, rows = grad.shape
        value = grad.astype(BF16).reshape(2, 2, self.low, columns // self.copies, rows)
        own = lax.dynamic_index_in_dim(value, self.core, 1, keepdims=False)
        got = self.swap(
            lax.dynamic_index_in_dim(value, 1 - self.core, 1, keepdims=False), fsdp=1
        )
        straight = self.core == self.side

        def cross(kept, sent):
            return kept.astype(F32) + self.swap(sent, fsdp=2).astype(F32)

        kept = jnp.where(straight, own, got)
        sent = jnp.where(straight, got, own)
        if side_first:
            value = self.halve_low(jnp.moveaxis(cross(kept, sent), 1, 0))
        else:
            both = jnp.stack([kept, sent], axis=0)
            both = self.halve_low(jnp.moveaxis(both, 2, 0))
            value = cross(both[0], both[1].astype(BF16))
        value = self.halve(value, 0, self.top, dp=self.top_step)

        def turn(d, f):
            team, _, core, _ = self.bits(d, f)
            return (d ^ self.team_step, f ^ 1) if core != team else (d, f)

        value = self.route(value.astype(BF16), turn)
        return value.astype(F32).T


def layer(
    place,
    block_input,
    caption,
    modulation,
    segment_ids,
    pos_row,
    pos_col,
    caption_len,
    gain_attn,
    w_query,
    w_key,
    w_value,
    gain_query,
    gain_key,
    w_cap_key,
    w_cap_value,
    gain_cap_key,
    head_gate,
    w_out,
    gain_ffn,
    w_gate,
    w_up,
    w_down,
    cotangent,
):
    place.locate()
    rows, tokens, width = block_input.shape
    cap_tokens = caption.shape[1]
    head_size = gain_query.shape[0] * place.shards
    scaling = 1.0 / math.sqrt(head_size)
    team_rows = 4 * rows

    small = (gain_attn, gain_ffn, gain_query, gain_key, gain_cap_key, head_gate)
    packed = lax.all_gather(jnp.concatenate(small), "fsdp", axis=0).astype(F32)
    full_small, at = [], 0
    for vector in small:
        full_small.append(packed[:, at : at + vector.shape[0]].reshape(-1))
        at += vector.shape[0]
    full_gain_attn, full_gain_ffn, query_gain, key_gain, cap_gain, full_head_gate = full_small
    heads = full_head_gate.shape[0] // 4

    inputs = block_input.astype(F32)
    scale_attn = 1.0 + modulation[:, 0][:, None, :]
    tanh_attn = jnp.tanh(modulation[:, 1])[:, None, :]
    scale_ffn = 1.0 + modulation[:, 2][:, None, :]
    tanh_ffn = jnp.tanh(modulation[:, 3])[:, None, :]
    normed_in, inverse_in = rms_scale(inputs)
    attn_in = (normed_in * full_gain_attn * scale_attn).astype(BF16).reshape(-1, width)
    upstream = cotangent.astype(F32)
    grad_ffn_branch = (upstream * tanh_ffn).astype(BF16).reshape(-1, width)

    attn_in = place.gather_tokens(attn_in)
    marks = jnp.concatenate(
        [segment_ids, pos_row, pos_col, jnp.broadcast_to(caption_len[:, None], (rows, 128))], axis=1
    )
    marks = place.gather_tokens(marks)
    segment_ids, pos_row, pos_col = (marks[:, i * tokens : (i + 1) * tokens] for i in range(3))
    caption_len = marks[:, 3 * tokens]
    caption = place.gather_tokens(caption.reshape(-1, caption.shape[-1]))
    grad_ffn_branch = place.gather_tokens(grad_ffn_branch)

    w_query, w_key, w_value = (place.columns(w) for w in (w_query, w_key, w_value))
    w_cap_key, w_cap_value = (place.columns(w) for w in (w_cap_key, w_cap_value))
    w_out = place.rows(w_out)
    w_gate, w_up = (place.columns(w) for w in (w_gate, w_up))
    w_down = place.rows(w_down)

    cos_table, sin_table = angle_tables(pos_row, pos_col, head_size)
    same_segment = (segment_ids[:, :, None] == segment_ids[:, None, :])[:, None, :, :]
    cap_positions = jnp.arange(cap_tokens, dtype=jnp.int32)
    caption_mask = (cap_positions[None, :] < caption_len[:, None])[:, None, None, :]

    def by_row(flat):
        return flat.reshape(team_rows, -1, flat.shape[-1])

    def by_head(flat):
        return flat.reshape(team_rows, -1, heads, head_size)

    query_raw = by_row(dot(attn_in, w_query))
    key_raw = by_row(dot(attn_in, w_key))
    value_heads = by_head(dot(attn_in, w_value).astype(BF16))
    query_scaled, query_normed, query_inverse = head_norm(query_raw, query_gain, head_size)
    queries = (query_scaled * cos_table + quarter_turn(query_scaled) * sin_table).astype(BF16)
    key_scaled, key_normed, key_inverse = head_norm(key_raw, key_gain, head_size)
    keys = (key_scaled * cos_table + quarter_turn(key_scaled) * sin_table).astype(BF16)
    cap_key_raw = by_row(dot(caption, w_cap_key))
    cap_scaled, cap_normed, cap_inverse = head_norm(cap_key_raw, cap_gain, head_size)
    cap_keys = cap_scaled.astype(BF16)
    cap_values = by_head(dot(caption, w_cap_value).astype(BF16))
    self_weights = attend_weights(queries, keys, same_segment, scaling)
    self_out = jnp.einsum(
        "rhqk,rkhd->rqhd", self_weights.astype(BF16), value_heads, preferred_element_type=F32
    )
    cross_weights = attend_weights(queries, cap_keys, caption_mask, scaling)
    cross_out = jnp.einsum(
        "rhqk,rkhd->rqhd", cross_weights.astype(BF16), cap_values, preferred_element_type=F32
    )
    head_tanh = jnp.tanh(
        lax.dynamic_slice_in_dim(full_head_gate, place.quarter * heads, heads)
    )[:, None]
    mixed = (self_out + head_tanh * cross_out).astype(BF16).reshape(-1, heads * head_size)
    attn_branch = place.reduce_tokens([(mixed, w_out)], dot).reshape(inputs.shape)
    hidden = inputs + tanh_attn * attn_branch

    normed_mid, inverse_mid = rms_scale(hidden)
    ffn_in = (normed_mid * full_gain_ffn * scale_ffn).astype(BF16).reshape(-1, width)
    ffn_in = place.gather_tokens(ffn_in)
    gate_proj = dot(ffn_in, w_gate)
    up_proj = dot(ffn_in, w_up)
    sigmoid_gate = jax.nn.sigmoid(gate_proj)
    silu_gate = gate_proj * sigmoid_gate
    activated = (silu_gate * up_proj).astype(BF16)
    grad_act = dot_back(grad_ffn_branch, w_down)
    grad_gate = (
        grad_act * up_proj * sigmoid_gate * (1.0 + gate_proj * (1.0 - sigmoid_gate))
    ).astype(BF16)
    grad_up = (grad_act * silu_gate).astype(BF16)
    grad_ffn_in = place.reduce_tokens([(grad_gate, w_gate), (grad_up, w_up)], dot_back)
    grad_ffn_in = grad_ffn_in.reshape(inputs.shape)
    grad_w_down = place.rows_back(dot_tokens(grad_ffn_branch, activated), False)
    grad_w_gate = place.columns_back(dot_tokens(grad_gate, ffn_in), True)
    grad_w_up = place.columns_back(dot_tokens(grad_up, ffn_in), False)
    ffn_branch = place.reduce_tokens([(activated, w_down)], dot).reshape(inputs.shape)
    block_out = (hidden + tanh_ffn * ffn_branch).astype(BF16)
    grad_mod_ffn_gate = jnp.sum(upstream * ffn_branch, axis=1) * (
        1.0 - tanh_ffn[:, 0] * tanh_ffn[:, 0]
    )
    grad_ffn_gain = jnp.sum(grad_ffn_in * normed_mid * scale_ffn, axis=(0, 1))
    grad_mod_ffn_scale = jnp.sum(grad_ffn_in * normed_mid * full_gain_ffn, axis=1)
    grad_hidden = upstream + rms_back(
        grad_ffn_in * full_gain_ffn * scale_ffn, normed_mid, inverse_mid
    )

    grad_attn_branch = (grad_hidden * tanh_attn).astype(BF16).reshape(-1, width)
    grad_attn_branch = place.gather_tokens(grad_attn_branch)
    grad_mod_attn_gate = jnp.sum(grad_hidden * attn_branch, axis=1) * (
        1.0 - tanh_attn[:, 0] * tanh_attn[:, 0]
    )
    grad_mixed = by_head(dot_back(grad_attn_branch, w_out).astype(BF16))
    grad_w_out = place.rows_back(dot_tokens(grad_attn_branch, mixed), True)
    grad_mixed_float = grad_mixed.astype(F32)
    grad_head_gate = jnp.sum(grad_mixed_float * cross_out, axis=(0, 1, 3)) * (
        1.0 - head_tanh[:, 0] * head_tanh[:, 0]
    )
    grad_cross = (head_tanh * grad_mixed_float).astype(BF16)
    grad_q_self, grad_keys_turned, grad_values = attend_back(
        self_weights, grad_mixed, value_heads, queries, keys, scaling
    )
    grad_q_cross, grad_cap_keys, grad_cap_values = attend_back(
        cross_weights, grad_cross, cap_values, queries, cap_keys, scaling
    )
    grad_queries = unrotate(grad_q_self + grad_q_cross, cos_table, sin_table)
    grad_keys_plain = unrotate(grad_keys_turned, cos_table, sin_table)
    grad_query_gain, grad_query = head_norm_back(
        grad_queries, query_normed, query_inverse, query_gain
    )
    grad_key_gain, grad_key = head_norm_back(grad_keys_plain, key_normed, key_inverse, key_gain)
    grad_cap_gain, grad_cap = head_norm_back(grad_cap_keys, cap_normed, cap_inverse, cap_gain)
    grad_value = grad_values.reshape(-1, heads * head_size)
    grad_cap_value = grad_cap_values.reshape(-1, heads * head_size)
    grad_w_cap_key = place.columns_back(dot_tokens(grad_cap, caption), True)
    grad_w_cap_value = place.columns_back(dot_tokens(grad_cap_value, caption), False)
    grad_w_query = place.columns_back(dot_tokens(grad_query, attn_in), True)
    grad_w_key = place.columns_back(dot_tokens(grad_key, attn_in), False)
    grad_w_value = place.columns_back(dot_tokens(grad_value, attn_in), True)
    grad_attn_in = place.reduce_tokens(
        [(grad_query, w_query), (grad_key, w_key), (grad_value, w_value)], dot_back
    ).reshape(inputs.shape)
    grad_gain_in = jnp.sum(grad_attn_in * normed_in * scale_attn, axis=(0, 1))
    grad_mod_attn_scale = jnp.sum(grad_attn_in * normed_in * full_gain_attn, axis=1)
    input_grad = (
        grad_hidden + rms_back(grad_attn_in * full_gain_attn * scale_attn, normed_in, inverse_in)
    ).astype(BF16)
    modulation_grad = jnp.stack(
        [grad_mod_attn_scale, grad_mod_attn_gate, grad_mod_ffn_scale, grad_mod_ffn_gate], axis=1
    )

    head_part = jnp.zeros_like(full_head_gate)
    head_part = lax.dynamic_update_slice_in_dim(
        head_part, grad_head_gate, place.quarter * heads, axis=0
    )
    parts = (
        grad_gain_in,
        grad_ffn_gain,
        grad_query_gain,
        grad_key_gain,
        grad_cap_gain,
        head_part,
    )
    summed = lax.psum(jnp.concatenate(parts), ("dp", "fsdp"))
    gains, at = [], 0
    for vector in parts:
        size = vector.shape[0] // place.shards
        gains.append(lax.dynamic_slice_in_dim(summed, at + place.fsdp * size, size))
        at += vector.shape[0]
    return (
        block_out,
        input_grad,
        modulation_grad,
        gains[0],
        grad_w_query,
        grad_w_key,
        grad_w_value,
        gains[2],
        gains[3],
        grad_w_cap_key,
        grad_w_cap_value,
        gains[4],
        gains[5],
        grad_w_out,
        gains[1],
        grad_w_gate,
        grad_w_up,
        grad_w_down,
    )


def solution(mesh):
    def shards(*arrays):
        return layer(Place(mesh), *arrays)

    rows = P(("dp", "fsdp"), None, None)
    marks = P(("dp", "fsdp"), None)
    vector = P("fsdp")
    weight = P("fsdp", None)
    grad = P("fsdp", "dp")
    return jax.shard_map(
        shards,
        mesh=mesh,
        in_specs=(
            (rows, rows, rows, marks, marks, marks, P(("dp", "fsdp")), vector)
            + (weight, weight, weight, vector, vector, weight, weight, vector, vector, weight)
            + (vector, weight, weight, weight, rows)
        ),
        out_specs=(
            (rows, rows, rows, vector, grad, grad, grad, vector, vector, grad, grad, vector)
            + (vector, grad, vector, grad, grad, grad)
        ),
        check_vma=False,
    )
```

```python
import functools
import math

import jax
import jax.numpy as jnp
from jax import lax
from jax.experimental import pallas as pl
from jax.experimental.pallas import tpu as pltpu
from jax.sharding import PartitionSpec as P

EPSILON = 1e-06
NEGATIVE = -1e30
BF16 = jnp.bfloat16
F32 = jnp.float32


def rms_scale(values):
    inverse = lax.rsqrt(jnp.mean(values * values, axis=-1, keepdims=True) + EPSILON)
    return (values * inverse, inverse)


def rms_back(incoming, normed, inverse):
    return inverse * (incoming - normed * jnp.mean(incoming * normed, axis=-1, keepdims=True))


def dot(left, right):
    return jnp.einsum("tc,ce->te", left, right, preferred_element_type=F32)


def dot_back(incoming, weight):
    return jnp.einsum("te,ce->tc", incoming, weight, preferred_element_type=F32)


def dot_tokens(left, right):
    return jnp.einsum("tc,te->ce", left, right, preferred_element_type=F32)


def after(value, *others):
    if not others:
        return value
    return lax.optimization_barrier((value,) + others)[0]


def quarter_turn(values):
    heads, size, tokens = values.shape
    parts = values.reshape(heads, 2, 2, size // 4, tokens)
    turned = jnp.concatenate([-parts[:, :, 1:], parts[:, :, :1]], axis=2)
    return turned.reshape(heads, size, tokens)


def head_norm(raw):
    inverse = lax.rsqrt(jnp.mean(raw * raw, axis=1, keepdims=True) + EPSILON)
    return raw * inverse, inverse


def head_norm_back(incoming, normed, inverse, gain):
    scaled = incoming * gain
    return inverse * (scaled - normed * jnp.mean(scaled * normed, axis=1, keepdims=True))


def dot00(left, right):
    return lax.dot_general(left, right, (((0,), (0,)), ((), ())), preferred_element_type=F32)


def dot11(left, right):
    return lax.dot_general(left, right, (((1,), (1,)), ((), ())), preferred_element_type=F32)


def dot10(left, right):
    return lax.dot_general(left, right, (((1,), (0,)), ((), ())), preferred_element_type=F32)


def softmax0(scores):
    top = jnp.max(scores, axis=0, keepdims=True)
    raised = jnp.exp(scores - top)
    return raised * (1.0 / jnp.sum(raised, axis=0, keepdims=True))


def row_state(qkv, cap, cos_table, sin_table, marks, gains, heads, size):
    tokens, cap_tokens = qkv.shape[0], cap.shape[0]
    across = heads * size
    qkv = qkv.T
    cap = cap.T

    def split(values, at):
        return values[at * across : (at + 1) * across].reshape(heads, size, -1)

    query_normed, query_inverse = head_norm(split(qkv, 0))
    key_normed, key_inverse = head_norm(split(qkv, 1))
    cap_normed, cap_inverse = head_norm(split(cap, 0))

    def rotate(values):
        return (values * cos_table + quarter_turn(values) * sin_table).astype(BF16)

    segment = marks[0:1]
    key_segment = jnp.broadcast_to(segment, (tokens, tokens)).T
    return {
        "queries": rotate(query_normed * gains[0]),
        "keys": rotate(key_normed * gains[1]),
        "values": split(qkv, 2).astype(BF16),
        "cap_keys": (cap_normed * gains[2][:, :1]).astype(BF16),
        "cap_values": split(cap, 1).astype(BF16),
        "norms": (query_normed, query_inverse, key_normed, key_inverse, cap_normed, cap_inverse),
        "same": key_segment == segment,
        "in_use": lax.broadcasted_iota(jnp.int32, (cap_tokens, tokens), 0).astype(F32)
        < marks[1:2],
    }


def forward_kernel(
    heads, size, qkv_ref, cap_ref, cos_ref, sin_ref, marks_ref, gains_ref, tanh_ref, mixed_ref, cross_ref
):
    state = row_state(
        qkv_ref[...], cap_ref[...], cos_ref[...], sin_ref[...], marks_ref[0], gains_ref[...], heads, size
    )
    scaling = 1.0 / math.sqrt(size)
    mixed = []
    for head in range(heads):
        queries = state["queries"][head]
        scores = dot00(state["keys"][head], queries) * scaling
        weights = softmax0(jnp.where(state["same"], scores, NEGATIVE)).astype(BF16)
        self_out = dot10(state["values"][head], weights)
        scores = dot00(state["cap_keys"][head], queries) * scaling
        weights = softmax0(jnp.where(state["in_use"], scores, NEGATIVE)).astype(BF16)
        cross_out = dot10(state["cap_values"][head], weights)
        cross_ref[head * size : (head + 1) * size, :] = cross_out
        mixed.append(self_out + tanh_ref[head] * cross_out)
    mixed_ref[...] = jnp.concatenate(mixed, axis=0).T.astype(BF16)


def backward_kernel(
    heads,
    size,
    qkv_ref,
    cap_ref,
    cos_ref,
    sin_ref,
    marks_ref,
    gains_ref,
    tanh_ref,
    cross_ref,
    grad_ref,
    turned_ref,
    plain_ref,
    cap_grad_ref,
    gain_grad_ref,
    gate_grad_ref,
):
    step = pl.program_id(0)
    cap = cap_ref[...]
    crossed = cross_ref[...]
    gains = gains_ref[...]
    cos_table, sin_table = cos_ref[...], sin_ref[...]
    state = row_state(qkv_ref[...], cap, cos_table, sin_table, marks_ref[0], gains, heads, size)
    scaling = 1.0 / math.sqrt(size)
    across = heads * size
    grad_q, grad_k, grad_cap_k, gate = [], [], [], []
    for head in range(heads):
        span = slice(head * size, (head + 1) * size)
        queries, keys, values = (state[name][head] for name in ("queries", "keys", "values"))
        cap_keys, cap_values = state["cap_keys"][head], state["cap_values"][head]
        grad_out = grad_ref[span, :]
        grad_float = grad_out.astype(F32)
        gate.append(jnp.sum(grad_float * crossed[span], axis=0, keepdims=True))
        grad_cross = (tanh_ref[head] * grad_float).astype(BF16)

        def back(weights, grad_output, held):
            grad_weights = dot00(held, grad_output)
            centre = jnp.sum(grad_weights * weights, axis=0, keepdims=True)
            return (weights * (grad_weights - centre)).astype(BF16)

        scores = dot00(keys, queries) * scaling
        weights = softmax0(jnp.where(state["same"], scores, NEGATIVE))
        grad_scores = back(weights, grad_out, values)
        grad_value = dot11(grad_out, weights.astype(BF16))
        at = 2 * across + head * size
        turned_ref[at : at + size, :] = grad_value.astype(BF16)
        grad_query = dot10(keys, grad_scores)
        grad_k.append(dot11(queries, grad_scores) * scaling)

        scores = dot00(cap_keys, queries) * scaling
        weights = softmax0(jnp.where(state["in_use"], scores, NEGATIVE))
        grad_scores = back(weights, grad_cross, cap_values)
        grad_cap_value = dot11(grad_cross, weights.astype(BF16))
        cap_grad_ref[across + head * size : across + (head + 1) * size, :] = grad_cap_value.astype(
            BF16
        )
        grad_q.append((grad_query + dot10(cap_keys, grad_scores)) * scaling)
        grad_cap_k.append(dot11(queries, grad_scores) * scaling)

    def stacked(parts):
        return jnp.concatenate(parts, axis=0).reshape(heads, size, -1)

    def unrotate(incoming):
        return incoming * cos_table - quarter_turn(incoming * sin_table)

    normed = state["norms"]
    grad_q, grad_k = unrotate(stacked(grad_q)), unrotate(stacked(grad_k))
    grad_cap_k = stacked(grad_cap_k)
    turned_ref[0:across, :] = (
        head_norm_back(grad_q, normed[0], normed[1], gains[0]).reshape(across, -1).astype(BF16)
    )
    turned_ref[across : 2 * across, :] = (
        head_norm_back(grad_k, normed[2], normed[3], gains[1]).reshape(across, -1).astype(BF16)
    )
    cap_grad_ref[0:across, :] = (
        head_norm_back(grad_cap_k, normed[4], normed[5], gains[2][:, :1])
        .reshape(across, -1)
        .astype(BF16)
    )
    plain_ref[...] = turned_ref[...].astype(F32).T.astype(BF16)
    tokens = grad_q.shape[-1]
    cap_part = jnp.sum(grad_cap_k * normed[4], axis=0)
    gain_part = jnp.stack(
        [
            jnp.sum(grad_q * normed[0], axis=0),
            jnp.sum(grad_k * normed[2], axis=0),
            sum(cap_part[:, i : i + tokens] for i in range(0, cap_part.shape[1], tokens)),
        ]
    )
    gate_part = jnp.stack(gate)

    @pl.when(step == 0)
    def _():
        gain_grad_ref[...] = gain_part
        gate_grad_ref[...] = gate_part

    @pl.when(step > 0)
    def _():
        gain_grad_ref[...] += gain_part
        gate_grad_ref[...] += gate_part


def row_specs(row_of, sizes, across):
    size, tokens, cap_tokens = sizes
    return [
        pl.BlockSpec((tokens, 3 * across), lambda i: (row_of(i), 0)),
        pl.BlockSpec((cap_tokens, 2 * across), lambda i: (i, 0)),
        pl.BlockSpec((size, tokens), lambda i: (0, row_of(i))),
        pl.BlockSpec((size, tokens), lambda i: (0, row_of(i))),
        pl.BlockSpec((1, 8, tokens), lambda i: (row_of(i), 0, 0)),
    ]


def whole(shape):
    return pl.BlockSpec(shape, lambda i: (0,) * len(shape))


def attend(row_of, heads, sizes, qkv, cap, cos_table, sin_table, marks, gains, tanh):
    size, tokens, cap_tokens = sizes
    rows = cap.shape[0] // cap_tokens
    across = heads * size
    return pl.pallas_call(
        functools.partial(forward_kernel, heads, size),
        grid=(rows,),
        in_specs=row_specs(row_of, sizes, across) + [whole(gains.shape), whole(tanh.shape)],
        out_specs=[
            pl.BlockSpec((tokens, across), lambda i: (i, 0)),
            pl.BlockSpec((across, tokens), lambda i: (0, i)),
        ],
        out_shape=[
            jax.ShapeDtypeStruct((rows * tokens, across), BF16),
            jax.ShapeDtypeStruct((across, rows * tokens), F32),
        ],
        compiler_params=pltpu.CompilerParams(vmem_limit_bytes=32 * 1024 * 1024),
        cost_estimate=pl.CostEstimate(
            flops=rows * across * tokens * (tokens + cap_tokens) * 16,
            bytes_accessed=rows * across * (tokens * 18 + cap_tokens * 8),
            transcendentals=rows * heads * tokens * (tokens + cap_tokens),
        ),
    )(qkv, cap, cos_table, sin_table, marks, gains, tanh)


def attend_back(row_of, first, heads, sizes, qkv, cap, cos_table, sin_table, marks, gains, tanh, crossed, grad):
    size, tokens, cap_tokens = sizes
    rows = cap.shape[0] // cap_tokens
    across = heads * size
    out_shape = [
        jax.ShapeDtypeStruct((3 * across, rows * tokens), BF16),
        jax.ShapeDtypeStruct((rows * tokens, 3 * across), BF16),
        jax.ShapeDtypeStruct((2 * across, rows * cap_tokens), BF16),
        jax.ShapeDtypeStruct((3, size, tokens), F32),
        jax.ShapeDtypeStruct((heads, 1, tokens), F32),
    ]
    return pl.pallas_call(
        functools.partial(backward_kernel, heads, size),
        grid=(rows,),
        in_specs=row_specs(row_of, sizes, across)
        + [
            whole(gains.shape),
            whole(tanh.shape),
            pl.BlockSpec((across, tokens), lambda i: (0, i)),
            pl.BlockSpec((across, tokens), lambda i: (0, row_of(i) - first)),
        ],
        out_specs=[
            pl.BlockSpec((3 * across, tokens), lambda i: (0, row_of(i) - first)),
            pl.BlockSpec((tokens, 3 * across), lambda i: (row_of(i) - first, 0)),
            pl.BlockSpec((2 * across, cap_tokens), lambda i: (0, i)),
            whole(out_shape[3].shape),
            whole(out_shape[4].shape),
        ],
        out_shape=out_shape,
        compiler_params=pltpu.CompilerParams(vmem_limit_bytes=40 * 1024 * 1024),
        cost_estimate=pl.CostEstimate(
            flops=rows * across * tokens * (tokens + cap_tokens) * 40,
            bytes_accessed=rows * across * (tokens * 30 + cap_tokens * 12),
            transcendentals=rows * heads * tokens * (tokens + cap_tokens),
        ),
    )(qkv, cap, cos_table, sin_table, marks, gains, tanh, crossed, grad)


def join_kernel(widths, rows, chunks, place_ref, *refs):
    shards = refs[: len(widths)]
    near = refs[len(widths)]
    pieces = refs[len(widths) + 1 : len(widths) + 1 + 2 * chunks]
    out, sems = refs[-2:]
    copies = []

    def copy(source, row, count, column, width):
        target = out.at[pl.ds(pl.multiple_of(row, 16), count), pl.ds(column, width)]
        copies.append(pltpu.make_async_copy(source, target, sems.at[len(copies)]))
        copies[-1].start()

    at = 0
    for shard, width in zip(shards, widths):
        begin = pl.multiple_of(place_ref[4] * width, 128)
        copy(shard.at[:, pl.ds(begin, width)], place_ref[0] * rows, rows, at, width)
        at += width
    copy(near, place_ref[1] * rows, rows, 0, at)
    part = rows // chunks
    for chunk in range(chunks):
        for kind in range(2):
            row = place_ref[2 + kind] * rows + chunk * part
            copy(pieces[2 * chunk + kind], row, part, 0, at)
    for item in copies:
        item.wait()


def join(place_index, shards, near, pieces):
    widths = tuple(shard.shape[1] // 4 for shard in shards)
    rows = near.shape[0]
    chunks = len(pieces) // 2
    count = len(shards) + 1 + len(pieces)
    return pl.pallas_call(
        functools.partial(join_kernel, widths, rows, chunks),
        grid_spec=pltpu.PrefetchScalarGridSpec(
            num_scalar_prefetch=1,
            grid=(1,),
            in_specs=[pl.BlockSpec(memory_space=pl.ANY)] * count,
            out_specs=pl.BlockSpec((4 * rows, sum(widths)), lambda i, place: (0, 0)),
            scratch_shapes=[pltpu.SemaphoreType.DMA((count,))],
        ),
        out_shape=jax.ShapeDtypeStruct((4 * rows, sum(widths)), near.dtype),
        compiler_params=pltpu.CompilerParams(vmem_limit_bytes=32 * 1024 * 1024),
        cost_estimate=pl.CostEstimate(
            flops=0, bytes_accessed=16 * rows * sum(widths), transcendentals=0
        ),
    )(place_index, *shards, near, *pieces)


class Flow:
    def __init__(self, steps):
        self.steps = steps
        self.sent = next(steps)
        self.result = None

    def step(self, *others):
        try:
            self.sent = self.steps.send(others)
        except StopIteration as stop:
            self.result = stop.value


class Place:
    def __init__(self, mesh):
        self.copies = mesh.shape["dp"]
        self.shards = mesh.shape["fsdp"]
        self.top_step = self.copies // 2
        self.team_step = self.copies // 4
        self.low = self.copies // 4
        self.last = {}
        self.wave, self.before = [], ()
        self.links = {"fsdp": "x", "dp": "y"}

    def locate(self):
        self.dp = lax.axis_index("dp")
        self.fsdp = lax.axis_index("fsdp")
        self.side = self.fsdp // 2
        self.core = self.fsdp % 2
        self.top = self.dp // self.top_step
        self.team = (self.dp // self.team_step) % 2
        self.lane = self.dp % 2
        self.quarter = 2 * self.core + self.team

    def swap(self, value, dp=0, fsdp=0, link=None):
        return self.route(value, lambda d, f: (d ^ dp, f ^ fsdp), link)

    def route(self, value, target, link=None):
        pairs = []
        for d in range(self.copies):
            for f in range(self.shards):
                to = target(d, f)
                if to is not None:
                    pairs.append((d * self.shards + f, to[0] * self.shards + to[1]))
        value = after(value, *self.before, *self.last.get(link, ()))
        self.operand = value
        value = lax.ppermute(value, ("dp", "fsdp"), pairs)
        if link is not None:
            self.last[link] = (value,)
        self.wave.append(value)
        return value

    def next_wave(self, *computed):
        self.before, self.wave = tuple(self.wave) + computed, []

    def hold(self, value):
        return after(value, *self.before)

    def end_waves(self):
        self.before, self.wave = (), []

    def bits(self, d, f):
        return ((d // self.team_step) % 2, f // 2, f % 2, d % 2)

    def team_swap(self, value):
        return self.swap(value, dp=self.team_step, link="z")

    def core_swap(self, value):
        return self.swap(value, fsdp=1, link="c")


    def gather_tokens(self, block):
        near = self.core_swap(block)
        far = self.team_swap(block)
        near = jnp.concatenate([block, near], axis=0)
        return near, jnp.concatenate([far, self.core_swap(far)], axis=0)

    def reduce_tokens(self, near, far, right, product):
        own, near = jnp.split(near, 2, axis=0)
        far, last = jnp.split(far, 2, axis=0)
        last = self.core_swap(product(last, right).astype(BF16))
        far = self.team_swap((product(far, right) + last.astype(F32)).astype(BF16))
        self.reducing = self.operand
        near = self.core_swap(product(near, right).astype(BF16))
        return product(own, right) + near.astype(F32) + far.astype(F32)


    def cut_columns(self, shards):
        def cut(quarter):
            parts = []
            for shard in shards:
                width = shard.shape[1] // 4
                parts.append(lax.dynamic_slice_in_dim(shard, quarter * width, width, axis=1))
            return jnp.concatenate(parts, axis=1)

        return cut(2 * (self.core ^ self.lane) + self.team), cut(2 * (1 - self.core) + self.team)

    def side_swap(self, piece):
        return self.route(piece, lambda d, f: (d, f ^ 2 ^ (d % 2)))

    def lane_swap(self, piece):
        return self.swap(piece, dp=1)

    def join_columns(self, shards, near, pieces):
        index = [self.fsdp, self.fsdp ^ 1, self.fsdp ^ 2 ^ self.lane, self.fsdp ^ 3 ^ self.lane]
        return join(jnp.stack(index + [self.quarter]).astype(jnp.int32), shards, near, pieces)

    def rows_side_swap(self, shard):
        def target(d, f):
            team, side, core, _ = self.bits(d, f)
            return (d, 2 * (1 - side) + side) if core == team else None

        return self.route(self.part(shard, self.lane, 0), target)

    def rows_lane_swap(self, piece):
        def target(d, f):
            _, side, core, _ = self.bits(d, f)
            return (d ^ 1, f) if core != side else None

        return self.route(piece, target)

    def rows_core_swap(self, shard):
        def target(d, f):
            team, side, core, _ = self.bits(d, f)
            return (d, 2 * side + side) if core == team and side != team else None

        return self.route(shard, target, "c")

    def join_rows(self, shard, near, across, far):
        first = jnp.where(self.lane == 0, across, far)
        second = jnp.where(self.lane == 0, far, across)
        home = jnp.where(self.side == self.team, shard, near)
        return jnp.where(self.core == self.side, home, jnp.concatenate([first, second], axis=0))


    def part(self, value, index, axis):
        if isinstance(value, tuple):
            return tuple(self.part(array, index, axis) for array in value)
        size = value.shape[axis] // 2
        return lax.dynamic_slice_in_dim(value, index * size, size, axis=axis)

    def summed(self, arrays):
        return sum(array.astype(F32) for array in arrays).astype(BF16)

    def halves(self, value, axis, keep):
        sent = self.summed([self.part(array, 1 - keep, axis) for array in value])
        return sent, [self.part(array, keep, axis) for array in value]

    def low_steps(self):
        step = self.low // 2
        while step:
            yield step, (self.dp // step) % 2
            step //= 2

    def both_ways(self, first, second, first_way, second_way):
        got_first = self.swap(first, link=self.links[first_way[0]], **dict([first_way]))
        sent = (self.operand,)
        got_second = self.swap(second, link=self.links[second_way[0]], **dict([second_way]))
        others = yield sent + (self.operand,)
        return after(got_first, *others), after(got_second, *others)

    def spread(self, first, second, place):
        (step, keep), *lows = self.low_steps()
        side, low = ("fsdp", 2), ("dp", step)
        sent = first[0](1 - place), second[0](1 - keep)
        first, second = [first[1](place)], [second[1](keep)]
        got = yield from self.both_ways(*sent, side, low)
        first.append(got[0])
        second.append(got[1])
        sent_first, first = self.halves(first, 0, keep)
        sent_second, second = self.halves(second, 1, place)
        got = yield from self.both_ways(sent_first, sent_second, low, side)
        first.append(got[0])
        second.append(got[1])
        for step, keep in lows:
            sent_first, first = self.halves(first, 0, keep)
            sent_second, second = self.halves(second, 0, keep)
            first.append(self.swap(sent_first, dp=step))
            second.append(self.swap(sent_second, dp=step))
        return first, second

    def finish(self, own, sent):
        got = self.core_swap(sent)
        others = yield (self.operand,)
        got = after(got, *others)
        straight = self.core == self.top
        sent = jnp.where(straight, got, own)
        kept = jnp.where(straight, own, got)
        got = self.swap(sent, dp=self.top_step, link="w")
        others = yield (self.operand,)
        return kept.astype(F32) + after(got, *others).astype(F32)

    def pair_back(self, product, lefts, left_axis, right):
        def by_side(index):
            return product(lefts[0], self.part(right, index, 1)).astype(BF16)

        def by_low(index):
            return product(self.part(lefts[1], index, left_axis), right).astype(BF16)

        first, second = yield from self.spread((by_side, by_side), (by_low, by_low), self.side)

        def both(index):
            return jnp.concatenate(
                [self.summed([self.part(array, index, 1) for array in value]) for value in (first, second)]
            )

        value = yield from self.finish(both(self.core), both(1 - self.core))
        return [part.T for part in jnp.split(value, 2, axis=0)]

    def split_rows(self, right):
        columns = right.shape[1] // 4

        def block(index):
            return lax.dynamic_slice_in_dim(right, index * columns, columns, axis=1)

        return (
            block(2 * self.side),
            block(2 * (1 - self.side)),
            jnp.concatenate([block(1), block(3)], axis=1),
        )

    def split_back(self, product, left, left_axis, right, count):
        this_side, other_side, low_rows = right

        def by_low(index):
            return product(self.part(left, index, left_axis), low_rows).astype(BF16)

        first, second = yield from self.spread(
            (
                lambda index: product(left, other_side).astype(BF16),
                lambda index: product(left, this_side).astype(BF16),
            ),
            (by_low, by_low),
            self.side,
        )
        first, second = self.summed(first), self.summed(second)
        own = jnp.where(self.core == 0, first, second)
        sent = jnp.where(self.core == 0, second, first)
        value = yield from self.finish(own, sent)
        return [part.T for part in jnp.split(value, count, axis=0)]

    def rows_back(self, grad):
        columns, rows = grad.shape
        value = grad.reshape(2, 2, columns // 4, rows)
        own = lax.dynamic_index_in_dim(value, self.core, 1, keepdims=False)
        sent = lax.dynamic_index_in_dim(value, 1 - self.core, 1, keepdims=False)
        got = self.core_swap(sent)
        others = yield (self.operand,)
        got = after(got, *others)
        straight = self.core == self.side
        kept = jnp.where(straight, own, got)
        sent = jnp.where(straight, got, own)
        wide = jnp.concatenate([kept[1], sent[1]], axis=1)
        pieces = sent[0], kept[0]

        def by_low(index):
            return self.part(wide, index, 0)

        first, second = yield from self.spread(
            (lambda index: pieces[0], lambda index: pieces[1]), (by_low, by_low), 0
        )
        first, second = self.summed(first), self.summed(second)
        sent = jnp.where(self.top == 0, second, first)
        got = self.swap(sent, dp=self.top_step, link="w")
        others = yield (self.operand,)
        value = self.summed([jnp.where(self.top == 0, first, second), after(got, *others)])

        def turn(d, f):
            team, _, core, _ = self.bits(d, f)
            return (d ^ self.team_step, f ^ 1) if core != team else (d, f)

        got = self.route(value, turn)
        others = yield (self.operand,)
        return after(got, *others).astype(F32).T

    def total(self, value):
        for bit in (1, 2):
            value = value + self.swap(value, fsdp=bit)
        step = 1
        while step < self.copies:
            value = value + self.swap(value, dp=step)
            step *= 2
        return value


def layer(
    place,
    block_input,
    caption,
    modulation,
    segment_ids,
    pos_row,
    pos_col,
    caption_len,
    gain_attn,
    w_query,
    w_key,
    w_value,
    gain_query,
    gain_key,
    w_cap_key,
    w_cap_value,
    gain_cap_key,
    head_gate,
    w_out,
    gain_ffn,
    w_gate,
    w_up,
    w_down,
    cotangent,
):
    place.locate()
    rows, tokens, width = block_input.shape
    cap_tokens = caption.shape[1]
    size = gain_query.shape[0] * place.shards
    team_rows = 4 * rows

    cap_flat = caption.reshape(-1, caption.shape[-1])
    cap_pieces = jnp.split(cap_flat, 4, axis=0)
    qkv_shards, cap_shards, ffn_shards = (w_query, w_key, w_value), (w_cap_key, w_cap_value), (w_gate, w_up)
    qkv_sent, qkv_near = place.cut_columns(qkv_shards)
    cap_sent, cap_w_near = place.cut_columns(cap_shards)
    ffn_sent, ffn_w_near = place.cut_columns(ffn_shards)
    cap_sent, ffn_sent = jnp.split(cap_sent, 2, axis=0), jnp.split(ffn_sent, 2, axis=0)
    qkv_side = place.side_swap(qkv_sent)
    far_pieces = [place.team_swap(cap_pieces[0])]

    small = (gain_attn, gain_ffn, gain_query, gain_key, gain_cap_key, head_gate)
    piece = jnp.concatenate(small)
    pair = jnp.stack([piece, place.core_swap(piece)])
    other = place.swap(pair, fsdp=2)
    packed = jnp.zeros((place.shards,) + piece.shape, piece.dtype)
    for part, index in ((pair[0], 0), (pair[1], 1), (other[0], 2), (other[1], 3)):
        packed = lax.dynamic_update_index_in_dim(packed, part, place.fsdp ^ index, 0)
    packed = packed.astype(F32)
    full_small, at = [], 0
    for vector in small:
        full_small.append(packed[:, at : at + vector.shape[0]].reshape(-1))
        at += vector.shape[0]
    full_gain_attn, full_gain_ffn, query_gain, key_gain, cap_gain, full_head_gate = full_small
    heads = full_head_gate.shape[0] // 4
    across = heads * size
    sizes = (size, tokens, cap_tokens)
    cap_core = place.core_swap(cap_flat)
    cap_near = jnp.concatenate([cap_flat, cap_core], axis=0)

    inputs = block_input.astype(F32)
    scale_attn = 1.0 + modulation[:, 0][:, None, :]
    tanh_attn = jnp.tanh(modulation[:, 1])[:, None, :]
    scale_ffn = 1.0 + modulation[:, 2][:, None, :]
    tanh_ffn = jnp.tanh(modulation[:, 3])[:, None, :]
    normed_in, inverse_in = rms_scale(inputs)
    attn_in = (normed_in * full_gain_attn * scale_attn).astype(BF16).reshape(-1, width)
    upstream = cotangent.astype(F32)
    grad_branch = (upstream * tanh_ffn).astype(BF16).reshape(-1, width)

    marks = jnp.stack(
        [segment_ids, pos_row, pos_col, jnp.broadcast_to(caption_len[:, None], (rows, tokens))],
        axis=-1,
    ).astype(BF16)
    marks = jnp.pad(marks.reshape(-1, 4), ((0, 0), (0, 124)))
    marked = jnp.concatenate([attn_in, marks], axis=1)

    place.next_wave()
    cap_side = [place.side_swap(cap_sent[0])]
    qkv_lane = place.lane_swap(qkv_side)
    far = place.team_swap(marked)
    qkv_near = place.core_swap(qkv_near)
    near = place.core_swap(marked)

    place.next_wave()
    cap_side.append(place.side_swap(cap_sent[1]))
    cap_lane = [place.lane_swap(cap_side[0])]
    far_pieces.append(place.team_swap(cap_pieces[1]))
    gathered = [
        jnp.concatenate([marked, near], axis=0),
        jnp.concatenate([far, place.core_swap(far)], axis=0),
    ]
    attn_near, attn_far = (part[:, :width] for part in gathered)
    marks = jnp.concatenate([part[:, width : width + 4] for part in gathered]).astype(F32)
    attn_all = jnp.concatenate([attn_near, attn_far], axis=0)
    cap_w_near = place.core_swap(cap_w_near)
    w_qkv = place.join_columns(qkv_shards, qkv_near, [place.hold(qkv_side), qkv_lane])

    place.next_wave(w_qkv)
    out_side = place.rows_side_swap(w_out)
    ffn_side = [place.side_swap(ffn_sent[0])]
    cap_lane.append(place.lane_swap(cap_side[1]))
    far_pieces.append(place.team_swap(cap_pieces[2]))
    cap_first = jnp.concatenate(far_pieces[:2], axis=0)
    cap_first = jnp.concatenate([cap_first, place.core_swap(cap_first)], axis=0)
    quarter_size = size // 4
    frequency = jnp.exp(
        jnp.arange(quarter_size, dtype=F32) * (-math.log(10000.0) / quarter_size)
    )
    marks = place.hold(marks)
    row_angle = frequency[:, None] * marks[:, 1][None, :]
    col_angle = frequency[:, None] * marks[:, 2][None, :]
    angles = jnp.concatenate([row_angle, row_angle, col_angle, col_angle], axis=0)
    cos_table, sin_table = jnp.cos(angles), jnp.sin(angles)
    marks = jnp.stack([marks[:, 0], marks[:, 3]]).reshape(2, team_rows, tokens)
    marks = jnp.pad(jnp.moveaxis(marks, 0, 1), ((0, 0), (0, 6), (0, 0)))
    gains = jnp.broadcast_to(
        jnp.stack([query_gain, key_gain, cap_gain])[:, :, None], (3, size, tokens)
    )
    head_tanh = jnp.tanh(lax.dynamic_slice_in_dim(full_head_gate, place.quarter * heads, heads))
    tanh_table = jnp.broadcast_to(head_tanh[:, None, None], (heads, 1, tokens))
    tables = (cos_table, sin_table, marks, gains, tanh_table)
    qkv_raw = dot(place.hold(attn_all), w_qkv)

    half = team_rows // 2

    def near_row(i):
        return i

    def far_row(i):
        return half + (i % 2) * rows + i // 2

    def second_row(i):
        return half + i * rows + 1

    place.next_wave(qkv_raw, cos_table)
    ffn_side.append(place.side_swap(ffn_sent[1]))
    out_lane = place.rows_lane_swap(out_side)
    ffn_lane = [place.lane_swap(ffn_side[0])]
    far_pieces.append(place.team_swap(cap_pieces[3]))
    ffn_w_near = place.core_swap(ffn_w_near)
    w_cap = place.join_columns(
        cap_shards, cap_w_near, [place.hold(cap_side[0]), cap_lane[0], cap_side[1], cap_lane[1]]
    )
    cap_raw_near = dot(cap_near, w_cap)
    mixed_near, cross_near = attend(near_row, heads, sizes, qkv_raw, cap_raw_near, *tables)

    place.next_wave(mixed_near)
    cap_second = jnp.concatenate(far_pieces[2:], axis=0)
    cap_second = jnp.concatenate([cap_second, place.core_swap(cap_second)], axis=0)
    down_side = place.rows_side_swap(w_down)
    ffn_lane.append(place.lane_swap(ffn_side[1]))
    far = place.team_swap(grad_branch)
    out_near = place.rows_core_swap(w_out)
    w_out = place.join_rows(w_out, out_near, place.hold(out_side), out_lane)
    branch_near = jnp.concatenate([grad_branch, place.core_swap(grad_branch)], axis=0)
    cap_raw_first = dot(place.hold(cap_first), w_cap)
    mixed_first, cross_first = attend(far_row, heads, sizes, qkv_raw, cap_raw_first, *tables)

    place.next_wave(mixed_first)
    down_lane = place.rows_lane_swap(down_side)
    place.end_waves()
    cap_raw_second = dot(cap_second, w_cap)
    mixed_second, cross_second = attend(second_row, heads, sizes, qkv_raw, cap_raw_second, *tables)
    mixed_far = jnp.concatenate(
        [mixed_first[:tokens], mixed_second[:tokens], mixed_first[tokens:], mixed_second[tokens:]]
    )
    cap_far = jnp.concatenate([cap_first, cap_second], axis=0)
    cap_raw_far = jnp.concatenate([cap_raw_first, cap_raw_second], axis=0)
    cross_far = jnp.concatenate([cross_first, cross_second], axis=1)
    attn_branch = place.reduce_tokens(mixed_near, mixed_far, w_out, dot).reshape(inputs.shape)
    down_near = place.rows_core_swap(w_down)
    w_down = place.join_rows(w_down, down_near, down_side, down_lane)
    w_ffn = place.join_columns(
        ffn_shards, ffn_w_near, [ffn_side[0], ffn_lane[0], ffn_side[1], ffn_lane[1]]
    )
    branch_far = jnp.concatenate([far, place.core_swap(far)], axis=0)
    hidden = inputs + tanh_attn * attn_branch

    normed_mid, inverse_mid = rms_scale(hidden)
    ffn_in = (normed_mid * full_gain_ffn * scale_ffn).astype(BF16).reshape(-1, width)
    ffn_near, ffn_far = place.gather_tokens(ffn_in)

    def middle(ffn_in, grad_branch):
        grad_act = dot_back(grad_branch, w_down)
        inner = grad_act.shape[1]
        gate_up = dot(ffn_in, w_ffn)
        gate_proj, up_proj = gate_up[:, :inner], gate_up[:, inner:]
        sigmoid_gate = jax.nn.sigmoid(gate_proj)
        silu_gate = gate_proj * sigmoid_gate
        activated = (silu_gate * up_proj).astype(BF16)
        grad_gate = (
            grad_act * up_proj * sigmoid_gate * (1.0 + gate_proj * (1.0 - sigmoid_gate))
        ).astype(BF16)
        grad_up = (grad_act * silu_gate).astype(BF16)
        return activated, jnp.concatenate([grad_gate, grad_up], axis=1)

    act_near, grad_near = middle(ffn_near, branch_near)
    act_far, grad_far = middle(ffn_far, branch_far)
    grad_ffn_in = place.reduce_tokens(grad_near, grad_far, w_ffn, dot_back)
    grad_ffn_in = grad_ffn_in.reshape(inputs.shape)
    inner = act_near.shape[1]
    grad_far, act_far = after(grad_far, place.reducing), after(act_far, place.reducing)

    def halves_product(left, right):
        return dot_tokens(left[0], right[0]) + dot_tokens(left[1], right[1])

    ffn = Flow(
        place.pair_back(
            halves_product,
            [(grad_near[:, at : at + inner], grad_far[:, at : at + inner]) for at in (0, inner)],
            1,
            (ffn_near, ffn_far),
        )
    )
    grad_down = halves_product((branch_near, branch_far), (act_near, act_far)).astype(BF16)
    down = Flow(place.rows_back(grad_down))
    grad_ffn_gain = jnp.sum(grad_ffn_in * normed_mid * scale_ffn, axis=(0, 1))
    grad_mod_ffn_scale = jnp.sum(grad_ffn_in * normed_mid * full_gain_ffn, axis=1)
    grad_hidden = upstream + rms_back(
        grad_ffn_in * full_gain_ffn * scale_ffn, normed_mid, inverse_mid
    )

    grad_attn_branch = (grad_hidden * tanh_attn).astype(BF16).reshape(-1, width)
    attn_grad_near, attn_grad_far = place.gather_tokens(grad_attn_branch)
    grad_mod_attn_gate = jnp.sum(grad_hidden * attn_branch, axis=1) * (
        1.0 - tanh_attn[:, 0] * tanh_attn[:, 0]
    )

    def heads_back(row_of, first, cap_raw, crossed, grad):
        grad_mixed = dot_back(w_out, grad).astype(BF16)
        return attend_back(
            row_of, first, heads, sizes, qkv_raw, cap_raw, *tables, crossed, grad_mixed
        )

    cap_all = jnp.concatenate([cap_near, cap_far], axis=0)
    cap_right = place.split_rows(cap_all)
    attn_right = place.split_rows(attn_all)
    near = heads_back(near_row, 0, cap_raw_near, cross_near, attn_grad_near)
    ffn.step(near[0])
    attn_grad_far = after(attn_grad_far, *ffn.sent)
    far = heads_back(far_row, half, cap_raw_far, cross_far, attn_grad_far)
    ffn.step(far[0])
    down.step(far[0])

    def mix(grads, count):
        grads = jnp.concatenate(grads, axis=1)
        shaped = grads.reshape(count, place.low, -1, grads.shape[1])
        return jnp.moveaxis(shaped, 0, 1).reshape(grads.shape)

    grad_cap = after(mix((near[2], far[2]), 2), *down.sent)
    cap = Flow(place.split_back(dot, grad_cap, 0, cap_right, 2))
    near_plain, far_plain = (after(part, *cap.sent) for part in (near[1], far[1]))
    grad_attn_in = place.reduce_tokens(near_plain, far_plain, w_qkv, dot_back).reshape(inputs.shape)
    attn_grad_all = jnp.concatenate([attn_grad_near, attn_grad_far], axis=0)
    mixed_all = after(jnp.concatenate([mixed_near, mixed_far], axis=0), *cap.sent)
    ffn.step()
    out = Flow(place.rows_back(dot_tokens(attn_grad_all, mixed_all).astype(BF16)))
    down.step()
    cap.step()
    qkv = Flow(place.split_back(dot, mix((near[0], far[0]), 3), 0, attn_right, 3))
    ffn.step()
    down.step()
    cap.step()
    out.step()
    qkv.step()
    down.step()
    out.step()
    ffn_branch = place.reduce_tokens(act_near, after(act_far, *cap.sent), w_down, dot)
    ffn_branch = ffn_branch.reshape(inputs.shape)
    flows = [down, cap, qkv, out]
    while any(flow.result is None for flow in flows):
        for flow in flows:
            if flow.result is None:
                flow.step()
    block_out = (hidden + tanh_ffn * ffn_branch).astype(BF16)
    grad_mod_ffn_gate = jnp.sum(upstream * ffn_branch, axis=1) * (
        1.0 - tanh_ffn[:, 0] * tanh_ffn[:, 0]
    )
    gate_parts = near[4] + far[4]
    gain_parts = jnp.sum(near[3] + far[3], axis=2)
    grad_head_gate = jnp.sum(gate_parts, axis=(1, 2)) * (1.0 - head_tanh * head_tanh)
    grad_gain_in = jnp.sum(grad_attn_in * normed_in * scale_attn, axis=(0, 1))
    grad_mod_attn_scale = jnp.sum(grad_attn_in * normed_in * full_gain_attn, axis=1)
    input_grad = (
        grad_hidden + rms_back(grad_attn_in * full_gain_attn * scale_attn, normed_in, inverse_in)
    ).astype(BF16)
    modulation_grad = jnp.stack(
        [grad_mod_attn_scale, grad_mod_attn_gate, grad_mod_ffn_scale, grad_mod_ffn_gate], axis=1
    )

    head_part = jnp.zeros_like(full_head_gate)
    head_part = lax.dynamic_update_slice_in_dim(
        head_part, grad_head_gate, place.quarter * heads, axis=0
    )
    parts = (
        grad_gain_in,
        grad_ffn_gain,
        gain_parts[0],
        gain_parts[1],
        gain_parts[2],
        head_part,
    )
    summed = place.total(jnp.concatenate(parts))
    vectors, at = [], 0
    for vector in parts:
        length = vector.shape[0] // place.shards
        vectors.append(lax.dynamic_slice_in_dim(summed, at + place.fsdp * length, length))
        at += vector.shape[0]
    return (
        block_out,
        input_grad,
        modulation_grad,
        vectors[0],
        qkv.result[0],
        qkv.result[1],
        qkv.result[2],
        vectors[2],
        vectors[3],
        cap.result[0],
        cap.result[1],
        vectors[4],
        vectors[5],
        out.result,
        vectors[1],
        ffn.result[0],
        ffn.result[1],
        down.result,
    )


def solution(mesh):
    def shards(*arrays):
        return layer(Place(mesh), *arrays)

    rows = P(("dp", "fsdp"), None, None)
    marks = P(("dp", "fsdp"), None)
    vector = P("fsdp")
    weight = P("fsdp", None)
    grad = P("fsdp", "dp")
    return jax.shard_map(
        shards,
        mesh=mesh,
        in_specs=(
            (rows, rows, rows, marks, marks, marks, P(("dp", "fsdp")), vector)
            + (weight, weight, weight, vector, vector, weight, weight, vector, vector, weight)
            + (vector, weight, weight, weight, rows)
        ),
        out_specs=(
            (rows, rows, rows, vector, grad, grad, grad, vector, vector, grad, grad, vector)
            + (vector, grad, vector, grad, grad, grad)
        ),
        check_vma=False,
    )
```

```python
import functools
import math

import jax
import jax.numpy as jnp
from jax import lax
from jax.experimental import pallas as pl
from jax.experimental.pallas import tpu as pltpu
from jax.sharding import PartitionSpec as P

EPSILON = 1e-06
NEGATIVE = -1e30
BF16 = jnp.bfloat16
F32 = jnp.float32
SMALL_COST = pl.CostEstimate(flops=1024, bytes_accessed=1024, transcendentals=0)


def rms_scale(values):
    inverse = lax.rsqrt(jnp.mean(values * values, axis=-1, keepdims=True) + EPSILON)
    return (values * inverse, inverse)


def rms_back(incoming, normed, inverse):
    return inverse * (incoming - normed * jnp.mean(incoming * normed, axis=-1, keepdims=True))


def dot(left, right):
    return jnp.einsum("tc,ce->te", left, right, preferred_element_type=F32)


def dot_back(incoming, weight):
    return jnp.einsum("te,ce->tc", incoming, weight, preferred_element_type=F32)


def dot_tokens(left, right):
    return jnp.einsum("tc,te->ce", left, right, preferred_element_type=F32)


def after(value, *others):
    if not others:
        return value
    return lax.optimization_barrier((value,) + others)[0]


def join_rows_kernel(place_ref, shard, near, across, far, out, sems):
    half = across.shape[0]
    source, lane = place_ref[0], place_ref[1]

    def copy(piece, row, count, sem):
        item = pltpu.make_async_copy(piece, out.at[pl.ds(row, count)], sem)
        item.start()
        return item

    @pl.when(source == 0)
    def _():
        copy(shard, 0, 2 * half, sems.at[0]).wait()

    @pl.when(source == 1)
    def _():
        copy(near, 0, 2 * half, sems.at[0]).wait()

    @pl.when(source == 2)
    def _():
        first = copy(across, pl.multiple_of(lane * half, 16), half, sems.at[0])
        second = copy(far, pl.multiple_of((1 - lane) * half, 16), half, sems.at[1])
        first.wait()
        second.wait()


def join_rows(index, shard, near, across, far):
    return pl.pallas_call(
        join_rows_kernel,
        grid_spec=pltpu.PrefetchScalarGridSpec(
            num_scalar_prefetch=1,
            grid=(1,),
            in_specs=[pl.BlockSpec(memory_space=pl.ANY)] * 4,
            out_specs=pl.BlockSpec(shard.shape, lambda i, place: (0, 0)),
            scratch_shapes=[pltpu.SemaphoreType.DMA((2,))],
        ),
        out_shape=jax.ShapeDtypeStruct(shard.shape, shard.dtype),
        compiler_params=pltpu.CompilerParams(vmem_limit_bytes=32 * 1024 * 1024),
        cost_estimate=SMALL_COST,
    )(index, shard, near, across, far)


def quarter_turn(values):
    heads, size, tokens = values.shape
    parts = values.reshape(heads, 2, 2, size // 4, tokens)
    turned = jnp.concatenate([-parts[:, :, 1:], parts[:, :, :1]], axis=2)
    return turned.reshape(heads, size, tokens)


def head_norm(raw):
    inverse = lax.rsqrt(jnp.mean(raw * raw, axis=1, keepdims=True) + EPSILON)
    return raw * inverse, inverse


def head_norm_back(incoming, normed, inverse, gain):
    scaled = incoming * gain
    return inverse * (scaled - normed * jnp.mean(scaled * normed, axis=1, keepdims=True))


def dot00(left, right):
    return lax.dot_general(left, right, (((0,), (0,)), ((), ())), preferred_element_type=F32)


def dot11(left, right):
    return lax.dot_general(left, right, (((1,), (1,)), ((), ())), preferred_element_type=F32)


def dot10(left, right):
    return lax.dot_general(left, right, (((1,), (0,)), ((), ())), preferred_element_type=F32)


def softmax0(scores):
    top = jnp.max(scores, axis=0, keepdims=True)
    raised = jnp.exp(scores - top)
    return raised * (1.0 / jnp.sum(raised, axis=0, keepdims=True))


def row_state(qkv, cap, cos_table, sin_table, marks, gains, heads, size):
    tokens, cap_tokens = qkv.shape[0], cap.shape[0]
    across = heads * size
    qkv = qkv.T
    cap = cap.T

    def split(values, at):
        return values[at * across : (at + 1) * across].reshape(heads, size, -1)

    query_normed, query_inverse = head_norm(split(qkv, 0))
    key_normed, key_inverse = head_norm(split(qkv, 1))
    cap_normed, cap_inverse = head_norm(split(cap, 0))

    def rotate(values):
        return (values * cos_table + quarter_turn(values) * sin_table).astype(BF16)

    segment = marks[0:1]
    key_segment = jnp.broadcast_to(segment, (tokens, tokens)).T
    return {
        "queries": rotate(query_normed * gains[0]),
        "keys": rotate(key_normed * gains[1]),
        "values": split(qkv, 2).astype(BF16),
        "cap_keys": (cap_normed * gains[2][:, :1]).astype(BF16),
        "cap_values": split(cap, 1).astype(BF16),
        "norms": (query_normed, query_inverse, key_normed, key_inverse, cap_normed, cap_inverse),
        "same": key_segment == segment,
        "in_use": lax.broadcasted_iota(jnp.int32, (cap_tokens, tokens), 0).astype(F32)
        < marks[1:2],
    }


def forward_kernel(
    heads,
    size,
    half,
    qkv_ref,
    first_ref,
    second_ref,
    weight_ref,
    cos_ref,
    sin_ref,
    marks_ref,
    gains_ref,
    tanh_ref,
    raw_ref,
    mixed_ref,
    cross_ref,
):
    step = pl.program_id(0)

    @pl.when(step < half)
    def _():
        raw_ref[...] = dot10(first_ref[...], weight_ref[...])

    @pl.when(step >= half)
    def _():
        raw_ref[...] = dot10(second_ref[...], weight_ref[...])

    state = row_state(
        qkv_ref[...], raw_ref[...], cos_ref[...], sin_ref[...], marks_ref[0], gains_ref[...], heads, size
    )
    scaling = 1.0 / math.sqrt(size)
    mixed = []
    for head in range(heads):
        queries = state["queries"][head]
        scores = dot00(state["keys"][head], queries) * scaling
        weights = softmax0(jnp.where(state["same"], scores, NEGATIVE)).astype(BF16)
        self_out = dot10(state["values"][head], weights)
        scores = dot00(state["cap_keys"][head], queries) * scaling
        weights = softmax0(jnp.where(state["in_use"], scores, NEGATIVE)).astype(BF16)
        cross_out = dot10(state["cap_values"][head], weights)
        cross_ref[head * size : (head + 1) * size, :] = cross_out
        mixed.append(self_out + tanh_ref[head] * cross_out)
    mixed_ref[...] = jnp.concatenate(mixed, axis=0).T.astype(BF16)


def backward_kernel(
    heads,
    size,
    qkv_ref,
    cap_ref,
    cos_ref,
    sin_ref,
    marks_ref,
    gains_ref,
    tanh_ref,
    cross_ref,
    grad_ref,
    turned_ref,
    plain_ref,
    cap_grad_ref,
    gain_grad_ref,
    gate_grad_ref,
):
    step = pl.program_id(0)
    cap = cap_ref[...]
    crossed = cross_ref[...]
    gains = gains_ref[...]
    cos_table, sin_table = cos_ref[...], sin_ref[...]
    state = row_state(qkv_ref[...], cap, cos_table, sin_table, marks_ref[0], gains, heads, size)
    scaling = 1.0 / math.sqrt(size)
    across = heads * size
    grad_q, grad_k, grad_cap_k, gate = [], [], [], []
    for head in range(heads):
        span = slice(head * size, (head + 1) * size)
        queries, keys, values = (state[name][head] for name in ("queries", "keys", "values"))
        cap_keys, cap_values = state["cap_keys"][head], state["cap_values"][head]
        grad_out = grad_ref[span, :]
        grad_float = grad_out.astype(F32)
        gate.append(jnp.sum(grad_float * crossed[span], axis=0, keepdims=True))
        grad_cross = (tanh_ref[head] * grad_float).astype(BF16)

        def back(weights, grad_output, held):
            grad_weights = dot00(held, grad_output)
            centre = jnp.sum(grad_weights * weights, axis=0, keepdims=True)
            return (weights * (grad_weights - centre)).astype(BF16)

        scores = dot00(keys, queries) * scaling
        weights = softmax0(jnp.where(state["same"], scores, NEGATIVE))
        grad_scores = back(weights, grad_out, values)
        grad_value = dot11(grad_out, weights.astype(BF16))
        at = 2 * across + head * size
        turned_ref[at : at + size, :] = grad_value.astype(BF16)
        grad_query = dot10(keys, grad_scores)
        grad_k.append(dot11(queries, grad_scores) * scaling)

        scores = dot00(cap_keys, queries) * scaling
        weights = softmax0(jnp.where(state["in_use"], scores, NEGATIVE))
        grad_scores = back(weights, grad_cross, cap_values)
        grad_cap_value = dot11(grad_cross, weights.astype(BF16))
        cap_grad_ref[across + head * size : across + (head + 1) * size, :] = grad_cap_value.astype(
            BF16
        )
        grad_q.append((grad_query + dot10(cap_keys, grad_scores)) * scaling)
        grad_cap_k.append(dot11(queries, grad_scores) * scaling)

    def stacked(parts):
        return jnp.concatenate(parts, axis=0).reshape(heads, size, -1)

    def unrotate(incoming):
        return incoming * cos_table - quarter_turn(incoming * sin_table)

    normed = state["norms"]
    grad_q, grad_k = unrotate(stacked(grad_q)), unrotate(stacked(grad_k))
    grad_cap_k = stacked(grad_cap_k)
    turned_ref[0:across, :] = (
        head_norm_back(grad_q, normed[0], normed[1], gains[0]).reshape(across, -1).astype(BF16)
    )
    turned_ref[across : 2 * across, :] = (
        head_norm_back(grad_k, normed[2], normed[3], gains[1]).reshape(across, -1).astype(BF16)
    )
    cap_grad_ref[0:across, :] = (
        head_norm_back(grad_cap_k, normed[4], normed[5], gains[2][:, :1])
        .reshape(across, -1)
        .astype(BF16)
    )
    plain_ref[...] = turned_ref[...].astype(F32).T.astype(BF16)
    tokens = grad_q.shape[-1]
    cap_part = jnp.sum(grad_cap_k * normed[4], axis=0)
    gain_part = jnp.stack(
        [
            jnp.sum(grad_q * normed[0], axis=0),
            jnp.sum(grad_k * normed[2], axis=0),
            sum(cap_part[:, i : i + tokens] for i in range(0, cap_part.shape[1], tokens)),
        ]
    )
    gate_part = jnp.stack(gate)

    @pl.when(step == 0)
    def _():
        gain_grad_ref[...] = gain_part
        gate_grad_ref[...] = gate_part

    @pl.when(step > 0)
    def _():
        gain_grad_ref[...] += gain_part
        gate_grad_ref[...] += gate_part


def row_specs(row_of, sizes, across):
    size, tokens, cap_tokens = sizes
    return [
        pl.BlockSpec((tokens, 3 * across), lambda i: (row_of(i), 0)),
        pl.BlockSpec((cap_tokens, 2 * across), lambda i: (i, 0)),
        pl.BlockSpec((size, tokens), lambda i: (0, row_of(i))),
        pl.BlockSpec((size, tokens), lambda i: (0, row_of(i))),
        pl.BlockSpec((1, 8, tokens), lambda i: (row_of(i), 0, 0)),
    ]


def whole(shape):
    return pl.BlockSpec(shape, lambda i: (0,) * len(shape))


def attend(row_of, heads, sizes, qkv, caps, weight, cos_table, sin_table, marks, gains, tanh):
    size, tokens, cap_tokens = sizes
    half = caps[0].shape[0] // cap_tokens
    rows = 2 * half
    across = heads * size
    width = caps[0].shape[1]
    specs = row_specs(row_of, sizes, across)
    return pl.pallas_call(
        functools.partial(forward_kernel, heads, size, half),
        grid=(rows,),
        in_specs=[
            specs[0],
            pl.BlockSpec((cap_tokens, width), lambda i: (jnp.minimum(i, half - 1), 0)),
            pl.BlockSpec((cap_tokens, width), lambda i: (jnp.maximum(i - half, 0), 0)),
            whole(weight.shape),
            *specs[2:],
            whole(gains.shape),
            whole(tanh.shape),
        ],
        out_specs=[
            pl.BlockSpec((cap_tokens, 2 * across), lambda i: (i, 0)),
            pl.BlockSpec((tokens, across), lambda i: (i, 0)),
            pl.BlockSpec((across, tokens), lambda i: (0, i)),
        ],
        out_shape=[
            jax.ShapeDtypeStruct((rows * cap_tokens, 2 * across), F32),
            jax.ShapeDtypeStruct((rows * tokens, across), BF16),
            jax.ShapeDtypeStruct((across, rows * tokens), F32),
        ],
        compiler_params=pltpu.CompilerParams(vmem_limit_bytes=48 * 1024 * 1024),
        cost_estimate=SMALL_COST,
    )(qkv, caps[0], caps[1], weight, cos_table, sin_table, marks, gains, tanh)


def attend_back(row_of, first, heads, sizes, qkv, cap, cos_table, sin_table, marks, gains, tanh, crossed, grad):
    size, tokens, cap_tokens = sizes
    rows = cap.shape[0] // cap_tokens
    across = heads * size
    out_shape = [
        jax.ShapeDtypeStruct((3 * across, rows * tokens), BF16),
        jax.ShapeDtypeStruct((rows * tokens, 3 * across), BF16),
        jax.ShapeDtypeStruct((2 * across, rows * cap_tokens), BF16),
        jax.ShapeDtypeStruct((3, size, tokens), F32),
        jax.ShapeDtypeStruct((heads, 1, tokens), F32),
    ]
    return pl.pallas_call(
        functools.partial(backward_kernel, heads, size),
        grid=(rows,),
        in_specs=row_specs(row_of, sizes, across)
        + [
            whole(gains.shape),
            whole(tanh.shape),
            pl.BlockSpec((across, tokens), lambda i: (0, i)),
            pl.BlockSpec((across, tokens), lambda i: (0, row_of(i) - first)),
        ],
        out_specs=[
            pl.BlockSpec((3 * across, tokens), lambda i: (0, row_of(i) - first)),
            pl.BlockSpec((tokens, 3 * across), lambda i: (row_of(i) - first, 0)),
            pl.BlockSpec((2 * across, cap_tokens), lambda i: (0, i)),
            whole(out_shape[3].shape),
            whole(out_shape[4].shape),
        ],
        out_shape=out_shape,
        compiler_params=pltpu.CompilerParams(vmem_limit_bytes=40 * 1024 * 1024),
        cost_estimate=SMALL_COST,
    )(qkv, cap, cos_table, sin_table, marks, gains, tanh, crossed, grad)


def outer_kernel(counts, place_ref, *refs):
    lefts, rights = refs[: len(counts)], refs[len(counts) : -1]
    total, at = None, 0
    for left, count in zip(lefts, counts):
        begin = 0
        for right in rights[at : at + count]:
            end = begin + right.shape[0]
            part = dot10(left[:, begin:end], right[...])
            total = part if total is None else total + part
            begin = end
        at += count
    refs[-1][...] = total.astype(BF16)


def outer(lefts, rights, left_index, left_blocks, column_blocks, width):
    counts = tuple(len(group) for group in rights)
    flat = [piece for group in rights for piece in group]
    rows = lefts[0].shape[0] // left_blocks
    count = len(column_blocks)
    index = jnp.stack([left_index] + list(column_blocks)).astype(jnp.int32)
    tokens = sum(left.shape[1] for left in lefts)
    return pl.pallas_call(
        functools.partial(outer_kernel, counts),
        grid_spec=pltpu.PrefetchScalarGridSpec(
            num_scalar_prefetch=1,
            grid=(count,),
            in_specs=[
                pl.BlockSpec((rows, left.shape[1]), lambda i, place: (place[0], 0)) for left in lefts
            ]
            + [pl.BlockSpec((right.shape[0], width), lambda i, place: (0, place[1 + i])) for right in flat],
            out_specs=pl.BlockSpec((rows, width), lambda i, place: (0, i)),
        ),
        out_shape=jax.ShapeDtypeStruct((rows, count * width), BF16),
        compiler_params=pltpu.CompilerParams(vmem_limit_bytes=40 * 1024 * 1024),
        cost_estimate=SMALL_COST,
    )(index, *lefts, *flat)


def middle_kernel(inner, ffn_ref, gate_ref, up_ref, branch_ref, down_ref, act_ref, grad_ref):
    block = gate_ref.shape[1]
    grad_act = dot11(branch_ref[...], down_ref[...])
    gate = dot10(ffn_ref[...], gate_ref[...])
    up = dot10(ffn_ref[...], up_ref[...])
    sigmoid = 1.0 / (1.0 + jnp.exp(-gate))
    silu = gate * sigmoid
    at = pl.multiple_of(pl.program_id(0) * block, 128)
    act_ref[...] = (silu * up).astype(BF16)
    grad_ref[:, pl.ds(at, block)] = (grad_act * up * sigmoid * (1.0 + gate * (1.0 - sigmoid))).astype(BF16)
    grad_ref[:, pl.ds(at + inner, block)] = (grad_act * silu).astype(BF16)


def middle(ffn_in, w_ffn, grad_branch, w_down):
    tokens, width = ffn_in.shape
    inner = w_down.shape[0]
    block = 256
    steps = inner // block

    def whole(shape):
        return pl.BlockSpec(shape, lambda i: (0,) * len(shape))

    return pl.pallas_call(
        functools.partial(middle_kernel, inner),
        grid=(steps,),
        in_specs=[
            whole((tokens, width)),
            pl.BlockSpec((width, block), lambda i: (0, i)),
            pl.BlockSpec((width, block), lambda i: (0, i + steps)),
            whole((tokens, width)),
            pl.BlockSpec((block, width), lambda i: (i, 0)),
        ],
        out_specs=[
            pl.BlockSpec((tokens, block), lambda i: (0, i)),
            whole((tokens, 2 * inner)),
        ],
        out_shape=[
            jax.ShapeDtypeStruct((tokens, inner), BF16),
            jax.ShapeDtypeStruct((tokens, 2 * inner), BF16),
        ],
        compiler_params=pltpu.CompilerParams(vmem_limit_bytes=40 * 1024 * 1024),
        cost_estimate=SMALL_COST,
    )(ffn_in, w_ffn, w_ffn, grad_branch, w_down)


def outer_tokens_kernel(count, place_ref, *refs):
    total = None
    for left, right in zip(refs[:count], refs[count:-1]):
        part = dot00(left[...], right[...])
        total = part if total is None else total + part
    refs[-1][...] = total.astype(BF16)


def outer_tokens(lefts, rights, left_block, blocks, right_block, right_blocks):
    block = 256
    columns = rights[0].shape[1] // right_blocks
    index = jnp.stack([jnp.asarray(left_block), jnp.asarray(right_block)]).astype(jnp.int32)
    return pl.pallas_call(
        functools.partial(outer_tokens_kernel, len(lefts)),
        grid_spec=pltpu.PrefetchScalarGridSpec(
            num_scalar_prefetch=1,
            grid=(blocks,),
            in_specs=[
                pl.BlockSpec((left.shape[0], block), lambda i, place: (0, place[0] + i)) for left in lefts
            ]
            + [
                pl.BlockSpec((right.shape[0], columns), lambda i, place: (0, place[1]))
                for right in rights
            ],
            out_specs=pl.BlockSpec((block, columns), lambda i, place: (i, 0)),
        ),
        out_shape=jax.ShapeDtypeStruct((blocks * block, columns), BF16),
        compiler_params=pltpu.CompilerParams(vmem_limit_bytes=40 * 1024 * 1024),
        cost_estimate=SMALL_COST,
    )(index, *lefts, *rights)


def join_kernel(widths, rows, chunks, place_ref, *refs):
    shards = refs[: len(widths)]
    near = refs[len(widths)]
    pieces = refs[len(widths) + 1 : len(widths) + 1 + 2 * chunks]
    out, sems = refs[-2:]
    copies = []

    def copy(source, row, count, column, width):
        target = out.at[pl.ds(pl.multiple_of(row, 16), count), pl.ds(column, width)]
        copies.append(pltpu.make_async_copy(source, target, sems.at[len(copies)]))
        copies[-1].start()

    at = 0
    for shard, width in zip(shards, widths):
        begin = pl.multiple_of(place_ref[4] * width, 128)
        copy(shard.at[:, pl.ds(begin, width)], place_ref[0] * rows, rows, at, width)
        at += width
    copy(near, place_ref[1] * rows, rows, 0, at)
    part = rows // chunks
    for chunk in range(chunks):
        for kind in range(2):
            row = place_ref[2 + kind] * rows + chunk * part
            copy(pieces[2 * chunk + kind], row, part, 0, at)
    for item in copies:
        item.wait()


def join(place_index, shards, near, pieces):
    widths = tuple(shard.shape[1] // 4 for shard in shards)
    rows = near.shape[0]
    chunks = len(pieces) // 2
    count = len(shards) + 1 + len(pieces)
    return pl.pallas_call(
        functools.partial(join_kernel, widths, rows, chunks),
        grid_spec=pltpu.PrefetchScalarGridSpec(
            num_scalar_prefetch=1,
            grid=(1,),
            in_specs=[pl.BlockSpec(memory_space=pl.ANY)] * count,
            out_specs=pl.BlockSpec((4 * rows, sum(widths)), lambda i, place: (0, 0)),
            scratch_shapes=[pltpu.SemaphoreType.DMA((count,))],
        ),
        out_shape=jax.ShapeDtypeStruct((4 * rows, sum(widths)), near.dtype),
        compiler_params=pltpu.CompilerParams(vmem_limit_bytes=32 * 1024 * 1024),
        cost_estimate=SMALL_COST,
    )(place_index, *shards, near, *pieces)


class Flow:
    def __init__(self, steps):
        self.steps = steps
        self.result = None
        self.waiting = next(steps)

    def step(self, values):
        if self.result is not None:
            return
        try:
            self.waiting = self.steps.send(values)
        except StopIteration as stop:
            self.waiting, self.result = (), stop.value


class Place:
    def __init__(self, mesh):
        self.copies = mesh.shape["dp"]
        self.shards = mesh.shape["fsdp"]
        self.top_step = self.copies // 2
        self.team_step = self.copies // 4
        self.low = self.copies // 4
        self.last = {}
        self.before, self.token = (), ()

    def locate(self):
        self.dp = lax.axis_index("dp")
        self.fsdp = lax.axis_index("fsdp")
        self.side = self.fsdp // 2
        self.core = self.fsdp % 2
        self.top = self.dp // self.top_step
        self.team = (self.dp // self.team_step) % 2
        self.lane = self.dp % 2
        self.quarter = 2 * self.core + self.team

    def swap(self, value, dp=0, fsdp=0, link=None):
        return self.route(value, lambda d, f: (d ^ dp, f ^ fsdp), link)

    def route(self, value, target, link=None):
        pairs = []
        for d in range(self.copies):
            for f in range(self.shards):
                to = target(d, f)
                if to is not None:
                    pairs.append((d * self.shards + f, to[0] * self.shards + to[1]))
        value = after(value, *self.before, *self.last.get(link, ()))
        self.operand = value
        value = lax.ppermute(value, ("dp", "fsdp"), pairs)
        if link is not None:
            self.last[link] = (value,)
        return value

    def next_wave(self, *others):
        self.before = others

    def arrive(self, *values):
        values = lax.optimization_barrier(values)
        self.before = values
        return values

    def meet(self, flows, *values):
        waiting = [array for flow in flows for array in flow.waiting]
        arrived = self.arrive(*waiting, *values)
        self.done(*arrived[len(waiting) :])
        at = 0
        for flow in flows:
            count = len(flow.waiting)
            flow.step(arrived[at : at + count])
            at += count
        return arrived[at:]

    def held(self, value):
        if isinstance(value, tuple):
            return tuple(self.held(part) for part in value)
        return after(value, *self.token)

    def done(self, *values):
        self.token = values

    def bits(self, d, f):
        return ((d // self.team_step) % 2, f // 2, f % 2, d % 2)

    def team_swap(self, value):
        return self.swap(value, dp=self.team_step, link="z")

    def core_swap(self, value):
        return self.swap(value, fsdp=1, link="c")


    def cut_columns(self, shards):
        def cut(quarter):
            parts = []
            for shard in shards:
                width = shard.shape[1] // 4
                parts.append(lax.dynamic_slice_in_dim(shard, quarter * width, width, axis=1))
            return jnp.concatenate(parts, axis=1)

        return cut(2 * (self.core ^ self.lane) + self.team), cut(2 * (1 - self.core) + self.team)

    def side_swap(self, piece):
        return self.route(piece, lambda d, f: (d, f ^ 2 ^ (d % 2)), "x")

    def lane_swap(self, piece):
        return self.swap(piece, dp=1, link="y")

    def join_columns(self, shards, near, pieces):
        index = [self.fsdp, self.fsdp ^ 1, self.fsdp ^ 2 ^ self.lane, self.fsdp ^ 3 ^ self.lane]
        return join(jnp.stack(index + [self.quarter]).astype(jnp.int32), shards, near, pieces)

    def rows_side_swap(self, shard):
        def target(d, f):
            team, side, core, _ = self.bits(d, f)
            return (d, 2 * (1 - side) + side) if core == team else None

        return self.route(shard, target, "x")

    def rows_lane_swap(self, piece):
        def target(d, f):
            _, side, core, _ = self.bits(d, f)
            return (d ^ 1, f) if core != side else None

        return self.route(piece, target, "y")

    def rows_core_swap(self, shard):
        def target(d, f):
            team, side, core, _ = self.bits(d, f)
            return (d, 2 * side + side) if core == team and side != team else None

        return self.route(shard, target, "c")

    def join_rows(self, shard, near, across, far):
        source = jnp.where(
            self.core != self.side, 2, jnp.where(self.side == self.team, 0, 1)
        )
        return join_rows(jnp.stack([source, self.lane]).astype(jnp.int32), shard, near, across, far)


    def part(self, value, index, axis):
        if isinstance(value, tuple):
            return tuple(self.part(array, index, axis) for array in value)
        size = value.shape[axis] // 2
        return lax.dynamic_slice_in_dim(value, index * size, size, axis=axis)

    def summed(self, arrays):
        return sum(array.astype(F32) for array in arrays).astype(BF16)

    def halves(self, value, axis, keep):
        sent = self.summed([self.part(array, 1 - keep, axis) for array in value])
        return sent, [self.part(array, keep, axis) for array in value]

    def low_steps(self):
        step = self.low // 2
        while step:
            yield step, (self.dp // step) % 2
            step //= 2

    def spread(self, first, second, place, chunks=1, ahead=False):
        (step, keep), *lows = self.low_steps()
        side, low, kept = [], [], ()
        sents = [(first[0](1 - place, i), second[0](1 - keep, i)) for i in range(chunks)]
        if chunks > 1:
            kept = tuple(first[1](place, i) for i in range(chunks))
            kept += tuple(second[1](keep, i) for i in range(chunks))
        if ahead:
            sents = [(yield sents[0])]
        for chunk in range(chunks):
            first_got = self.swap(sents[chunk][0], fsdp=2)
            operands = (self.operand,)
            second_got = self.swap(sents[chunk][1], dp=step)
            self.operands = operands + (self.operand,)
            rest = tuple(part for pair in sents[chunk + 1 :] for part in pair)
            if not kept:
                yield first_got, second_got
                kept = first[1](place, 0), second[1](keep, 0)
            arrived = yield (first_got, second_got) + kept + rest
            side.append(arrived[0])
            low.append(arrived[1])
            kept, rest = arrived[2 : 2 + len(kept)], arrived[2 + len(kept) :]
            sents[chunk + 1 :] = [rest[i : i + 2] for i in range(0, len(rest), 2)]

        def joined(parts):
            return parts[0] if chunks == 1 else jnp.concatenate(parts, axis=0)

        if chunks == 2 and not lows:
            pairs = (kept[:chunks], side)
            sent_first = self.summed([jnp.where(keep == 0, pair[1], pair[0]) for pair in pairs])
            first = [jnp.where(keep == 0, pair[0], pair[1]) for pair in pairs]
        else:
            sent_first, first = self.halves([joined(kept[:chunks]), joined(side)], 0, keep)
        second = [joined(kept[chunks:]), joined(low)]
        sent_second, second = self.halves(second, 1, place)
        got = yield self.swap(sent_first, dp=step), self.swap(sent_second, fsdp=2)
        first.append(got[0])
        second.append(got[1])
        for step, keep in lows:
            sent_first, first = self.halves(first, 0, keep)
            sent_second, second = self.halves(second, 0, keep)
            first.append(self.swap(sent_first, dp=step))
            second.append(self.swap(sent_second, dp=step))
        return first, second

    def finish(self, own, sent, parts, apart=False):
        got = self.core_swap(sent)
        if apart:
            (got,) = yield (got,)
        straight = self.core == self.top
        sent = jnp.split(jnp.where(straight, got, own), parts, axis=0)
        kept = jnp.split(jnp.where(straight, own, got), parts, axis=0)
        totals = []
        for part in range(parts):
            (got,) = yield (self.swap(sent[part], dp=self.top_step),)
            totals.append(kept[part].astype(F32) + got.astype(F32))
        return totals

    def pair_back(self, by_side, by_low):
        first, second = yield from self.spread((by_side, by_side), (by_low, by_low), self.side, 2)

        def both(index):
            return jnp.concatenate(
                [self.summed([self.part(array, index, 1) for array in value]) for value in (first, second)]
            )

        value = yield from self.finish(both(self.core), both(1 - self.core), 2, True)
        return [part.T for part in value]

    def split_back(self, by_side, by_low, count, parts, ahead=False):
        yield ()
        first, second = yield from self.spread(
            (by_side, by_side), (by_low, by_low), self.side, 1, ahead
        )
        first, second = self.summed(first), self.summed(second)
        own = jnp.where(self.core == 0, first, second)
        sent = jnp.where(self.core == 0, second, first)
        value = yield from self.finish(own, sent, parts)
        return [part.T for total in value for part in jnp.split(total, count // parts, axis=0)]

    def rows_back(self, grad):
        columns, rows = grad.shape
        value = grad.reshape(2, 2, columns // 4, rows)
        own = lax.dynamic_index_in_dim(value, self.core, 1, keepdims=False)
        sent = lax.dynamic_index_in_dim(value, 1 - self.core, 1, keepdims=False)
        got = self.core_swap(sent)
        straight = self.core == self.side
        kept = jnp.where(straight, own, got)
        sent = jnp.where(straight, got, own)
        wide = jnp.concatenate([kept[1], sent[1]], axis=1)
        pieces = sent[0], kept[0]
        *pieces, wide = yield (*pieces, wide)

        def by_low(index, _):
            return self.part(wide, index, 0)

        first, second = yield from self.spread(
            (lambda *_: pieces[0], lambda *_: pieces[1]), (by_low, by_low), 0
        )
        first, second = self.summed(first), self.summed(second)
        sent = jnp.where(self.top == 0, second, first)
        (got,) = yield (self.swap(sent, dp=self.top_step),)
        value = self.summed([jnp.where(self.top == 0, first, second), got])

        def turn(d, f):
            team, _, core, _ = self.bits(d, f)
            return (d ^ self.team_step, f ^ 1) if core != team else (d, f)

        (got,) = yield (self.route(value, turn),)
        return got.astype(F32).T

    def total(self, value):
        for bit in (1, 2):
            value = value + self.swap(value, fsdp=bit)
        step = 1
        while step < self.top_step:
            value = value + self.swap(value, dp=step)
            step *= 2
        got = self.swap(value, dp=step)
        return lambda: value + self.held(got)


def layer(
    place,
    block_input,
    caption,
    modulation,
    segment_ids,
    pos_row,
    pos_col,
    caption_len,
    gain_attn,
    w_query,
    w_key,
    w_value,
    gain_query,
    gain_key,
    w_cap_key,
    w_cap_value,
    gain_cap_key,
    head_gate,
    w_out,
    gain_ffn,
    w_gate,
    w_up,
    w_down,
    cotangent,
):
    place.locate()
    rows, tokens, width = block_input.shape
    cap_tokens = caption.shape[1]
    size = gain_query.shape[0] * place.shards
    team_rows = 4 * rows

    qkv_shards, cap_shards, ffn_shards = (w_query, w_key, w_value), (w_cap_key, w_cap_value), (w_gate, w_up)
    qkv_sent, qkv_near = place.cut_columns(qkv_shards)
    qkv_side = place.side_swap(qkv_sent)
    cap_pieces = [caption[0, : cap_tokens // 2], caption[0, cap_tokens // 2 :]]
    cap_pieces += [caption[1, : cap_tokens // 2], caption[1, cap_tokens // 2 :]]
    far_pieces = [place.team_swap(cap_pieces[0])]

    small = (gain_attn, gain_ffn, gain_query, gain_key, gain_cap_key, head_gate)
    piece = after(jnp.concatenate(small), qkv_sent)
    pair = jnp.stack([piece, place.core_swap(piece)])
    other = place.swap(pair, fsdp=2)
    packed = jnp.zeros((place.shards,) + piece.shape, piece.dtype)
    for part, index in ((pair[0], 0), (pair[1], 1), (other[0], 2), (other[1], 3)):
        packed = lax.dynamic_update_index_in_dim(packed, part, place.fsdp ^ index, 0)
    packed = packed.astype(F32)
    full_small, at = [], 0
    for vector in small:
        full_small.append(packed[:, at : at + vector.shape[0]].reshape(-1))
        at += vector.shape[0]
    full_gain_attn, full_gain_ffn, query_gain, key_gain, cap_gain, full_head_gate = full_small
    heads = full_head_gate.shape[0] // 4
    across = heads * size
    sizes = (size, tokens, cap_tokens)

    cap_own = caption.reshape(-1, caption.shape[-1])
    cap_core = place.core_swap(cap_own)
    cap_sent, cap_w_near = place.cut_columns(cap_shards)
    cap_sent = jnp.split(cap_sent, 2, axis=0)
    ffn_sent, ffn_w_near = place.cut_columns(ffn_shards)
    ffn_sent = jnp.split(ffn_sent, 2, axis=0)
    half_out, half_down = w_out.shape[0] // 2, w_down.shape[0] // 2
    rows_sent = jnp.concatenate(
        [place.part(w_out, place.lane, 0), place.part(w_down, place.lane, 0)], axis=0
    )

    inputs = block_input.astype(F32)
    scale_attn = 1.0 + modulation[:, 0][:, None, :]
    tanh_attn = jnp.tanh(modulation[:, 1])[:, None, :]
    scale_ffn = 1.0 + modulation[:, 2][:, None, :]
    tanh_ffn = jnp.tanh(modulation[:, 3])[:, None, :]
    upstream = cotangent.astype(F32)
    grad_branch = (upstream * tanh_ffn).astype(BF16).reshape(-1, width)
    normed_in, inverse_in = rms_scale(inputs)
    attn_in = (normed_in * full_gain_attn * scale_attn).astype(BF16).reshape(-1, width)

    own_tokens = rows * tokens
    marks = jnp.stack(
        [segment_ids, pos_row, pos_col, jnp.broadcast_to(caption_len[:, None], (rows, tokens))]
    )
    marks = marks.astype(BF16).reshape(4, own_tokens)
    marks = jnp.pad(marks, ((0, 12), (0, width - own_tokens)))
    marked = jnp.concatenate([attn_in, marks], axis=0)

    qkv_side, far_piece = place.arrive(qkv_side, far_pieces[0])
    far_pieces = [far_piece]
    cap_side = place.side_swap(cap_sent[0])
    qkv_lane = place.lane_swap(qkv_side)
    marked_far = place.team_swap(marked)
    place.before = ()
    qkv_near = place.core_swap(qkv_near)
    marked_near = place.core_swap(marked)

    cap_side, qkv_lane, marked_far = place.arrive(cap_side, qkv_lane, marked_far)
    cap_pairs = [cap_side]
    next_side = place.side_swap(cap_sent[1])
    cap_lane = place.lane_swap(cap_side)
    far_piece = place.team_swap(cap_pieces[1])
    place.before = ()
    marked_last = place.core_swap(marked_far)
    cap_w_near = place.core_swap(cap_w_near)
    blocks = (marked, marked_near, marked_far, marked_last)
    attn_all = jnp.concatenate([block[:own_tokens] for block in blocks], axis=0)
    marks = jnp.concatenate([block[own_tokens:, :own_tokens] for block in blocks], axis=1).astype(F32)
    w_qkv = place.join_columns(qkv_shards, qkv_near, [qkv_side, qkv_lane])

    next_side, cap_lane, far_piece, attn_all, w_qkv = place.arrive(
        next_side, cap_lane, far_piece, attn_all, w_qkv
    )
    cap_pairs += [cap_lane, next_side]
    far_pieces.append(far_piece)
    rows_side = place.rows_side_swap(rows_sent)
    cap_lane = place.lane_swap(next_side)
    far_piece = place.team_swap(cap_pieces[2])
    place.before = ()
    far_first = jnp.concatenate(far_pieces, axis=0)
    far_first_core = place.core_swap(far_first)
    ffn_w_near = place.core_swap(ffn_w_near)
    qkv_raw = dot(attn_all, w_qkv)

    quarter_size = size // 4
    frequency = jnp.exp(
        jnp.arange(quarter_size, dtype=F32) * (-math.log(10000.0) / quarter_size)
    )
    row_angle = frequency[:, None] * marks[1][None, :]
    col_angle = frequency[:, None] * marks[2][None, :]
    angles = jnp.concatenate([row_angle, row_angle, col_angle, col_angle], axis=0)
    cos_table, sin_table = jnp.cos(angles), jnp.sin(angles)
    marks = jnp.stack([marks[0], marks[3]]).reshape(2, team_rows, tokens)
    marks = jnp.pad(jnp.moveaxis(marks, 0, 1), ((0, 0), (0, 6), (0, 0)))
    gains = jnp.broadcast_to(
        jnp.stack([query_gain, key_gain, cap_gain])[:, :, None], (3, size, tokens)
    )
    head_tanh = jnp.tanh(lax.dynamic_slice_in_dim(full_head_gate, place.quarter * heads, heads))
    tanh_table = jnp.broadcast_to(head_tanh[:, None, None], (heads, 1, tokens))
    tables = (cos_table, sin_table, marks, gains, tanh_table)
    half = team_rows // 2

    def far_row(i):
        return half + (i % rows) * rows + i // rows

    def rows_from(first):
        return lambda i: first + i

    rows_side, cap_lane, far_piece, qkv_raw, cos_table = place.arrive(
        rows_side, cap_lane, far_piece, qkv_raw, cos_table
    )
    tables = (cos_table,) + tables[1:]
    cap_pairs.append(cap_lane)
    far_pieces = [far_piece]
    ffn_side = place.side_swap(ffn_sent[0])
    rows_lane = place.rows_lane_swap(rows_side)
    far_piece = place.team_swap(cap_pieces[3])
    w_cap = place.join_columns(cap_shards, cap_w_near, cap_pairs)
    out_near = place.rows_core_swap(w_out)
    branch_core = place.core_swap(grad_branch)
    place.before = ()
    near_raw, mixed_near, near_crossed = attend(
        rows_from(0), heads, sizes, qkv_raw, (cap_own, cap_core), w_cap, *tables
    )

    ffn_side, rows_lane, far_piece, mixed_near = place.arrive(ffn_side, rows_lane, far_piece, mixed_near)
    ffn_pairs = [ffn_side]
    far_pieces.append(far_piece)
    next_side = place.side_swap(ffn_sent[1])
    ffn_lane = place.lane_swap(ffn_side)
    branch_far = place.team_swap(grad_branch)
    place.before = ()
    far_second = jnp.concatenate(far_pieces, axis=0)
    far_second_core = place.core_swap(far_second)
    down_near = place.rows_core_swap(w_down)
    w_out = place.join_rows(w_out, out_near, rows_side[:half_out], rows_lane[:half_out])
    first_raw, mixed_first, first_crossed = attend(
        lambda i: half + i * rows, heads, sizes, qkv_raw, (far_first, far_first_core), w_cap, *tables
    )
    second_raw, mixed_second, second_crossed = attend(
        lambda i: half + 1 + i * rows,
        heads,
        sizes,
        qkv_raw,
        (far_second, far_second_core),
        w_cap,
        *tables,
    )
    next_side, ffn_lane, branch_far, mixed_second = place.arrive(
        next_side, ffn_lane, branch_far, mixed_second
    )
    ffn_pairs += [ffn_lane, next_side]
    place.before = ()
    place.done(mixed_second)
    far_raw = jnp.concatenate([first_raw, second_raw], axis=0)
    far_crossed = jnp.concatenate([first_crossed, second_crossed], axis=1)
    mixed_blocks = (
        *jnp.split(mixed_near, 2, axis=0),
        jnp.concatenate([mixed_first[:tokens], mixed_second[:tokens]], axis=0),
        jnp.concatenate([mixed_first[tokens:], mixed_second[tokens:]], axis=0),
    )
    def far_sum(blocks, right, product):
        last = place.core_swap(product(place.held(blocks[3]), right).astype(BF16))
        far = product(place.held(blocks[2]), right) + last.astype(F32)
        return place.team_swap(far.astype(BF16))

    def near_sum(blocks, right, product):
        got = place.core_swap(product(place.held(blocks[1]), right).astype(BF16))
        return product(place.held(blocks[0]), right) + got.astype(F32)

    attn_far_sum = far_sum(mixed_blocks, w_out, dot)
    ffn_pairs.append(place.lane_swap(next_side))
    w_down = place.join_rows(w_down, down_near, rows_side[half_out:], rows_lane[half_out:])
    branch_near = jnp.concatenate([grad_branch, branch_core], axis=0)
    branch_far = jnp.concatenate([branch_far, place.core_swap(branch_far)], axis=0)
    w_ffn = place.join_columns(ffn_shards, ffn_w_near, ffn_pairs)
    attn_near_sum = near_sum(mixed_blocks, w_out, dot)
    attn_far_sum, attn_near_sum, w_ffn, w_down = place.arrive(
        attn_far_sum, attn_near_sum, w_ffn, w_down
    )
    place.before = ()
    attn_branch = (attn_near_sum + attn_far_sum.astype(F32)).reshape(inputs.shape)
    hidden = inputs + tanh_attn * attn_branch

    normed_mid, inverse_mid = rms_scale(hidden)
    ffn_in = (normed_mid * full_gain_ffn * scale_ffn).astype(BF16).reshape(-1, width)

    ffn_far = place.team_swap(ffn_in)
    ffn_near = jnp.concatenate([ffn_in, place.core_swap(ffn_in)], axis=0)
    act_near, grad_near = middle(ffn_near, w_ffn, branch_near, w_down)
    place.done(act_near, grad_near)
    ffn_far = place.held(ffn_far)
    ffn_far = jnp.concatenate([ffn_far, place.core_swap(ffn_far)], axis=0)
    act_far, grad_far = middle(ffn_far, w_ffn, branch_far, w_down)
    place.done(act_far, grad_far)
    grad_blocks = (*jnp.split(grad_near, 2, axis=0), *jnp.split(grad_far, 2, axis=0))
    act_blocks = (*jnp.split(act_near, 2, axis=0), *jnp.split(act_far, 2, axis=0))
    blocks = act_near.shape[1] // 256

    def gate_by_side(side, chunk):
        lefts = place.held((grad_near, grad_far))
        each = blocks // 2
        return outer_tokens(lefts, (ffn_near, ffn_far), chunk * each, each, side, 2)

    def up_by_low(index, chunk):
        lefts = place.held((grad_near, grad_far))
        each = blocks // 4
        first = blocks + index * (blocks // 2) + chunk * each
        return outer_tokens(lefts, (ffn_near, ffn_far), first, each, 0, 1)

    ffn_far_sum = far_sum(grad_blocks, w_ffn, dot_back)
    ffn = Flow(place.pair_back(gate_by_side, up_by_low))
    ffn_near_sum = near_sum(grad_blocks, w_ffn, dot_back)
    ffn_far_sum, ffn_near_sum = place.meet([ffn], ffn_far_sum, ffn_near_sum)
    place.before = ()
    grad_ffn_in = (ffn_near_sum + ffn_far_sum.astype(F32)).reshape(inputs.shape)
    grad_ffn_gain = jnp.sum(grad_ffn_in * normed_mid * scale_ffn, axis=(0, 1))
    grad_mod_ffn_scale = jnp.sum(grad_ffn_in * normed_mid * full_gain_ffn, axis=1)
    grad_hidden = upstream + rms_back(
        grad_ffn_in * full_gain_ffn * scale_ffn, normed_mid, inverse_mid
    )

    grad_attn_branch = (grad_hidden * tanh_attn).astype(BF16).reshape(-1, width)
    grad_mod_attn_gate = jnp.sum(grad_hidden * attn_branch, axis=1) * (
        1.0 - tanh_attn[:, 0] * tanh_attn[:, 0]
    )
    attn_grad_far = place.team_swap(grad_attn_branch)
    attn_grad_near = jnp.concatenate([grad_attn_branch, place.core_swap(grad_attn_branch)], axis=0)

    def heads_back(row_of, first, cap_raw, crossed, grad):
        grad_mixed = dot_back(w_out, grad).astype(BF16)
        result = attend_back(
            row_of, first, heads, sizes, qkv_raw, cap_raw, *tables, crossed, grad_mixed
        )
        return list(result)

    near = heads_back(rows_from(0), 0, near_raw, near_crossed, attn_grad_near)
    attn_grad_far, near[0] = place.meet([ffn], attn_grad_far, near[0])
    place.before = ()
    place.done(place.operand)
    attn_grad_far = jnp.concatenate([attn_grad_far, place.core_swap(attn_grad_far)], axis=0)
    grad_down = outer_tokens(
        (branch_near, branch_far), place.held((act_near, act_far)), 0, width // 256, 0, 1
    )
    down = Flow(place.rows_back(grad_down))
    far = heads_back(far_row, half, far_raw, far_crossed, attn_grad_far)
    attn_grad_all = jnp.concatenate([attn_grad_near, attn_grad_far], axis=0)
    mixed_all = jnp.concatenate(mixed_blocks, axis=0)

    def mix(grads, count):
        shaped = grads.reshape(count, place.low, -1, grads.shape[1])
        return jnp.moveaxis(shaped, 0, 1).reshape(grads.shape)

    cap_lefts = []
    cap_rights = (cap_own, cap_core), (far_first, far_first_core, far_second, far_second_core)
    block = min(512, caption.shape[2] // 4)
    per = caption.shape[2] // 4 // block

    def cap_by_side(side, _):
        lefts = place.held(tuple(cap_lefts))
        return outer(lefts, cap_rights, 0, 1, [2 * per * side + i for i in range(per)], block)

    def cap_by_low(index, _):
        lefts = place.held(tuple(cap_lefts))
        columns = [start * per + i for start in (1, 3) for i in range(per)]
        return outer(lefts, cap_rights, index, 2, columns, block)

    far[0], far[2] = place.meet([ffn, down], far[0], far[2])
    down.step(())
    cap_lefts += [mix(near[2], 2), mix(far[2], 2)]
    cap = Flow(place.split_back(cap_by_side, cap_by_low, 2, 2))
    cap.step(())
    place.meet([ffn, down], *place.operands)
    place.done(place.before[0])
    place.before = ()
    cap.step(())
    cap_kept = cap.waiting[2:]
    branch_far_sum = far_sum(act_blocks, w_down, dot)
    branch_near_sum = near_sum(act_blocks, w_down, dot)
    out = Flow(place.rows_back(dot_tokens(attn_grad_all, place.held(mixed_all)).astype(BF16)))
    branch_near_sum, *_ = place.meet([ffn, cap, out], branch_near_sum, *cap_kept)
    out.step(())
    place.before = ()
    plain = (*jnp.split(near[1], 2, axis=0), *jnp.split(far[1], 2, axis=0))
    plain = place.held(plain)
    attn_far_sum = far_sum(plain, w_qkv, dot_back)
    attn_near_sum = near_sum(plain, w_qkv, dot_back)
    turned = mix(jnp.concatenate([near[0], far[0]], axis=1), 3)
    columns = width // 4
    low_rows = jnp.concatenate([attn_all[:, i * columns : (i + 1) * columns] for i in (1, 3)], axis=1)

    def qkv_by_side(side, _):
        right = lax.dynamic_slice_in_dim(attn_all, 2 * side * columns, columns, axis=1)
        return dot(place.held(turned), right).astype(BF16)

    def qkv_by_low(index, _):
        return dot(place.part(place.held(turned), index, 0), low_rows).astype(BF16)

    qkv = Flow(place.split_back(qkv_by_side, qkv_by_low, 3, 1, True))
    qkv.step(())
    branch_far_sum, attn_near_sum = place.meet(
        [ffn, cap, down, qkv], branch_far_sum, attn_near_sum
    )
    qkv.step(())
    (attn_far_sum,) = place.meet([qkv, out], attn_far_sum)
    grad_attn_in = (attn_near_sum + attn_far_sum.astype(F32)).reshape(inputs.shape)
    grad_gain_in = jnp.sum(grad_attn_in * normed_in * scale_attn, axis=(0, 1))
    grad_mod_attn_scale = jnp.sum(grad_attn_in * normed_in * full_gain_attn, axis=1)
    input_grad = (
        grad_hidden + rms_back(grad_attn_in * full_gain_attn * scale_attn, normed_in, inverse_in)
    ).astype(BF16)
    gate_parts = near[4] + far[4]
    gain_parts = jnp.sum(near[3] + far[3], axis=2)
    grad_head_gate = jnp.sum(gate_parts, axis=(1, 2)) * (1.0 - head_tanh * head_tanh)
    ffn_branch = (branch_near_sum + branch_far_sum.astype(F32)).reshape(inputs.shape)
    block_out = (hidden + tanh_ffn * ffn_branch).astype(BF16)
    grad_mod_ffn_gate = jnp.sum(upstream * ffn_branch, axis=1) * (
        1.0 - tanh_ffn[:, 0] * tanh_ffn[:, 0]
    )
    grad_gain_in, input_grad, block_out = place.meet(
        [cap, out, down, qkv], grad_gain_in, input_grad, block_out
    )
    place.before = ()
    head_part = jnp.zeros_like(full_head_gate)
    head_part = lax.dynamic_update_slice_in_dim(
        head_part, grad_head_gate, place.quarter * heads, axis=0
    )
    parts = (
        grad_gain_in,
        grad_ffn_gain,
        gain_parts[0],
        gain_parts[1],
        gain_parts[2],
        head_part,
    )
    small_grads = jnp.concatenate(parts)
    summed = place.total(after(small_grads, place.operand))
    for flow in (ffn, down, cap, out, qkv):
        for _ in range(4):
            flow.step(flow.waiting)
    summed = summed()
    modulation_grad = jnp.stack(
        [grad_mod_attn_scale, grad_mod_attn_gate, grad_mod_ffn_scale, grad_mod_ffn_gate], axis=1
    )

    vectors, at = [], 0
    for vector in parts:
        length = vector.shape[0] // place.shards
        vectors.append(lax.dynamic_slice_in_dim(summed, at + place.fsdp * length, length))
        at += vector.shape[0]
    return (
        block_out,
        input_grad,
        modulation_grad,
        vectors[0],
        qkv.result[0],
        qkv.result[1],
        qkv.result[2],
        vectors[2],
        vectors[3],
        cap.result[0],
        cap.result[1],
        vectors[4],
        vectors[5],
        out.result,
        vectors[1],
        ffn.result[0],
        ffn.result[1],
        down.result,
    )


def solution(mesh):
    def shards(*arrays):
        return layer(Place(mesh), *arrays)

    rows = P(("dp", "fsdp"), None, None)
    marks = P(("dp", "fsdp"), None)
    vector = P("fsdp")
    weight = P("fsdp", None)
    grad = P("fsdp", "dp")
    return jax.shard_map(
        shards,
        mesh=mesh,
        in_specs=(
            (rows, rows, rows, marks, marks, marks, P(("dp", "fsdp")), vector)
            + (weight, weight, weight, vector, vector, weight, weight, vector, vector, weight)
            + (vector, weight, weight, weight, rows)
        ),
        out_specs=(
            (rows, rows, rows, vector, grad, grad, grad, vector, vector, grad, grad, vector)
            + (vector, grad, vector, grad, grad, grad)
        ),
        check_vma=False,
    )
```

```python
import functools
import math

import jax
import jax.numpy as jnp
from jax import lax
from jax.experimental import pallas as pl
from jax.experimental.pallas import tpu as pltpu
from jax.sharding import PartitionSpec as P

EPSILON = 1e-06
NEGATIVE = -1e30
BF16 = jnp.bfloat16
F32 = jnp.float32
SMALL_COST = pl.CostEstimate(flops=1024, bytes_accessed=1024, transcendentals=0)


def rms_scale(values):
    inverse = lax.rsqrt(jnp.mean(values * values, axis=-1, keepdims=True) + EPSILON)
    return (values * inverse, inverse)


def rms_back(incoming, normed, inverse):
    return inverse * (incoming - normed * jnp.mean(incoming * normed, axis=-1, keepdims=True))


def dot(left, right):
    return jnp.einsum("tc,ce->te", left, right, preferred_element_type=F32)


def dot_back(incoming, weight):
    return jnp.einsum("te,ce->tc", incoming, weight, preferred_element_type=F32)


def dot_tokens(left, right):
    return jnp.einsum("tc,te->ce", left, right, preferred_element_type=F32)


def after(value, *others):
    if not others:
        return value
    return lax.optimization_barrier((value,) + others)[0]


def join_rows_kernel(place_ref, shard, near, across, far, out, sems):
    half = across.shape[0]
    source, lane = place_ref[0], place_ref[1]

    def copy(piece, row, count, sem):
        item = pltpu.make_async_copy(piece, out.at[pl.ds(row, count)], sem)
        item.start()
        return item

    @pl.when(source == 0)
    def _():
        copy(shard, 0, 2 * half, sems.at[0]).wait()

    @pl.when(source == 1)
    def _():
        copy(near, 0, 2 * half, sems.at[0]).wait()

    @pl.when(source == 2)
    def _():
        first = copy(across, pl.multiple_of(lane * half, 16), half, sems.at[0])
        second = copy(far, pl.multiple_of((1 - lane) * half, 16), half, sems.at[1])
        first.wait()
        second.wait()


def join_rows(index, shard, near, across, far):
    return pl.pallas_call(
        join_rows_kernel,
        grid_spec=pltpu.PrefetchScalarGridSpec(
            num_scalar_prefetch=1,
            grid=(1,),
            in_specs=[pl.BlockSpec(memory_space=pl.ANY)] * 4,
            out_specs=pl.BlockSpec(shard.shape, lambda i, place: (0, 0)),
            scratch_shapes=[pltpu.SemaphoreType.DMA((2,))],
        ),
        out_shape=jax.ShapeDtypeStruct(shard.shape, shard.dtype),
        compiler_params=pltpu.CompilerParams(vmem_limit_bytes=50 * 1024 * 1024),
        cost_estimate=SMALL_COST,
    )(index, shard, near, across, far)


def quarter_turn(values):
    heads, size, tokens = values.shape
    parts = values.reshape(heads, 2, 2, size // 4, tokens)
    turned = jnp.concatenate([-parts[:, :, 1:], parts[:, :, :1]], axis=2)
    return turned.reshape(heads, size, tokens)


def head_norm(raw):
    inverse = lax.rsqrt(jnp.mean(raw * raw, axis=1, keepdims=True) + EPSILON)
    return raw * inverse, inverse


def head_norm_back(incoming, normed, inverse, gain):
    scaled = incoming * gain
    return inverse * (scaled - normed * jnp.mean(scaled * normed, axis=1, keepdims=True))


def dot00(left, right):
    return lax.dot_general(left, right, (((0,), (0,)), ((), ())), preferred_element_type=F32)


def dot11(left, right):
    return lax.dot_general(left, right, (((1,), (1,)), ((), ())), preferred_element_type=F32)


def dot10(left, right):
    return lax.dot_general(left, right, (((1,), (0,)), ((), ())), preferred_element_type=F32)


def softmax0(scores):
    top = jnp.max(scores, axis=0, keepdims=True)
    raised = jnp.exp(scores - top)
    return raised * (1.0 / jnp.sum(raised, axis=0, keepdims=True))


def row_state(qkv, cap, cos_table, sin_table, marks, gains, heads, size):
    tokens, cap_tokens = qkv.shape[0], cap.shape[0]
    across = heads * size
    qkv = qkv.T
    cap = cap.T

    def split(values, at):
        return values[at * across : (at + 1) * across].reshape(heads, size, -1)

    query_normed, query_inverse = head_norm(split(qkv, 0))
    key_normed, key_inverse = head_norm(split(qkv, 1))
    cap_normed, cap_inverse = head_norm(split(cap, 0))

    def rotate(values):
        return (values * cos_table + quarter_turn(values) * sin_table).astype(BF16)

    segment = marks[0:1]
    key_segment = jnp.broadcast_to(segment, (tokens, tokens)).T
    return {
        "queries": rotate(query_normed * gains[0]),
        "keys": rotate(key_normed * gains[1]),
        "values": split(qkv, 2).astype(BF16),
        "cap_keys": (cap_normed * gains[2][:, :1]).astype(BF16),
        "cap_values": split(cap, 1).astype(BF16),
        "norms": (query_normed, query_inverse, key_normed, key_inverse, cap_normed, cap_inverse),
        "same": key_segment == segment,
        "in_use": lax.broadcasted_iota(jnp.int32, (cap_tokens, tokens), 0).astype(F32)
        < marks[1:2],
    }


def forward_kernel(
    heads,
    size,
    half,
    qkv_ref,
    first_ref,
    second_ref,
    weight_ref,
    cos_ref,
    sin_ref,
    marks_ref,
    gains_ref,
    tanh_ref,
    raw_ref,
    mixed_ref,
    cross_ref,
):
    step = pl.program_id(0)

    @pl.when(step < half)
    def _():
        raw_ref[...] = dot10(first_ref[...], weight_ref[...])

    @pl.when(step >= half)
    def _():
        raw_ref[...] = dot10(second_ref[...], weight_ref[...])

    state = row_state(
        qkv_ref[...], raw_ref[...], cos_ref[...], sin_ref[...], marks_ref[0], gains_ref[...], heads, size
    )
    scaling = 1.0 / math.sqrt(size)
    mixed = []
    for head in range(heads):
        queries = state["queries"][head]
        scores = dot00(state["keys"][head], queries) * scaling
        weights = softmax0(jnp.where(state["same"], scores, NEGATIVE)).astype(BF16)
        self_out = dot10(state["values"][head], weights)
        scores = dot00(state["cap_keys"][head], queries) * scaling
        weights = softmax0(jnp.where(state["in_use"], scores, NEGATIVE)).astype(BF16)
        cross_out = dot10(state["cap_values"][head], weights)
        cross_ref[head * size : (head + 1) * size, :] = cross_out
        mixed.append(self_out + tanh_ref[head] * cross_out)
    mixed_ref[...] = jnp.concatenate(mixed, axis=0).T.astype(BF16)


def backward_kernel(
    heads,
    size,
    qkv_ref,
    cap_ref,
    cos_ref,
    sin_ref,
    marks_ref,
    gains_ref,
    tanh_ref,
    cross_ref,
    grad_ref,
    turned_ref,
    plain_ref,
    cap_grad_ref,
    gain_grad_ref,
    gate_grad_ref,
):
    step = pl.program_id(0)
    cap = cap_ref[...]
    crossed = cross_ref[...]
    gains = gains_ref[...]
    cos_table, sin_table = cos_ref[...], sin_ref[...]
    state = row_state(qkv_ref[...], cap, cos_table, sin_table, marks_ref[0], gains, heads, size)
    scaling = 1.0 / math.sqrt(size)
    across = heads * size
    grad_q, grad_k, grad_cap_k, gate = [], [], [], []
    for head in range(heads):
        span = slice(head * size, (head + 1) * size)
        queries, keys, values = (state[name][head] for name in ("queries", "keys", "values"))
        cap_keys, cap_values = state["cap_keys"][head], state["cap_values"][head]
        grad_out = grad_ref[span, :]
        grad_float = grad_out.astype(F32)
        gate.append(jnp.sum(grad_float * crossed[span], axis=0, keepdims=True))
        grad_cross = (tanh_ref[head] * grad_float).astype(BF16)

        def back(weights, grad_output, held):
            grad_weights = dot00(held, grad_output)
            centre = jnp.sum(grad_weights * weights, axis=0, keepdims=True)
            return (weights * (grad_weights - centre)).astype(BF16)

        scores = dot00(keys, queries) * scaling
        weights = softmax0(jnp.where(state["same"], scores, NEGATIVE))
        grad_scores = back(weights, grad_out, values)
        grad_value = dot11(grad_out, weights.astype(BF16))
        at = 2 * across + head * size
        turned_ref[at : at + size, :] = grad_value.astype(BF16)
        grad_query = dot10(keys, grad_scores)
        grad_k.append(dot11(queries, grad_scores) * scaling)

        scores = dot00(cap_keys, queries) * scaling
        weights = softmax0(jnp.where(state["in_use"], scores, NEGATIVE))
        grad_scores = back(weights, grad_cross, cap_values)
        grad_cap_value = dot11(grad_cross, weights.astype(BF16))
        cap_grad_ref[across + head * size : across + (head + 1) * size, :] = grad_cap_value.astype(
            BF16
        )
        grad_q.append((grad_query + dot10(cap_keys, grad_scores)) * scaling)
        grad_cap_k.append(dot11(queries, grad_scores) * scaling)

    def stacked(parts):
        return jnp.concatenate(parts, axis=0).reshape(heads, size, -1)

    def unrotate(incoming):
        return incoming * cos_table - quarter_turn(incoming * sin_table)

    normed = state["norms"]
    grad_q, grad_k = unrotate(stacked(grad_q)), unrotate(stacked(grad_k))
    grad_cap_k = stacked(grad_cap_k)
    turned_ref[0:across, :] = (
        head_norm_back(grad_q, normed[0], normed[1], gains[0]).reshape(across, -1).astype(BF16)
    )
    turned_ref[across : 2 * across, :] = (
        head_norm_back(grad_k, normed[2], normed[3], gains[1]).reshape(across, -1).astype(BF16)
    )
    cap_grad_ref[0:across, :] = (
        head_norm_back(grad_cap_k, normed[4], normed[5], gains[2][:, :1])
        .reshape(across, -1)
        .astype(BF16)
    )
    plain_ref[...] = turned_ref[...].astype(F32).T.astype(BF16)
    tokens = grad_q.shape[-1]
    cap_part = jnp.sum(grad_cap_k * normed[4], axis=0)
    gain_part = jnp.stack(
        [
            jnp.sum(grad_q * normed[0], axis=0),
            jnp.sum(grad_k * normed[2], axis=0),
            sum(cap_part[:, i : i + tokens] for i in range(0, cap_part.shape[1], tokens)),
        ]
    )
    gate_part = jnp.stack(gate)

    @pl.when(step == 0)
    def _():
        gain_grad_ref[...] = gain_part
        gate_grad_ref[...] = gate_part

    @pl.when(step > 0)
    def _():
        gain_grad_ref[...] += gain_part
        gate_grad_ref[...] += gate_part


def row_specs(row_of, sizes, across):
    size, tokens, cap_tokens = sizes
    return [
        pl.BlockSpec((tokens, 3 * across), lambda i: (row_of(i), 0)),
        pl.BlockSpec((cap_tokens, 2 * across), lambda i: (i, 0)),
        pl.BlockSpec((size, tokens), lambda i: (0, row_of(i))),
        pl.BlockSpec((size, tokens), lambda i: (0, row_of(i))),
        pl.BlockSpec((1, 8, tokens), lambda i: (row_of(i), 0, 0)),
    ]


def whole(shape):
    return pl.BlockSpec(shape, lambda i: (0,) * len(shape))


def attend(row_of, heads, sizes, qkv, caps, weight, cos_table, sin_table, marks, gains, tanh):
    size, tokens, cap_tokens = sizes
    half = caps[0].shape[0] // cap_tokens
    rows = 2 * half
    across = heads * size
    width = caps[0].shape[1]
    specs = row_specs(row_of, sizes, across)
    return pl.pallas_call(
        functools.partial(forward_kernel, heads, size, half),
        grid=(rows,),
        in_specs=[
            specs[0],
            pl.BlockSpec((cap_tokens, width), lambda i: (jnp.minimum(i, half - 1), 0)),
            pl.BlockSpec((cap_tokens, width), lambda i: (jnp.maximum(i - half, 0), 0)),
            whole(weight.shape),
            *specs[2:],
            whole(gains.shape),
            whole(tanh.shape),
        ],
        out_specs=[
            pl.BlockSpec((cap_tokens, 2 * across), lambda i: (i, 0)),
            pl.BlockSpec((tokens, across), lambda i: (i, 0)),
            pl.BlockSpec((across, tokens), lambda i: (0, i)),
        ],
        out_shape=[
            jax.ShapeDtypeStruct((rows * cap_tokens, 2 * across), F32),
            jax.ShapeDtypeStruct((rows * tokens, across), BF16),
            jax.ShapeDtypeStruct((across, rows * tokens), F32),
        ],
        compiler_params=pltpu.CompilerParams(vmem_limit_bytes=34 * 1024 * 1024),
        cost_estimate=SMALL_COST,
    )(qkv, caps[0], caps[1], weight, cos_table, sin_table, marks, gains, tanh)


def attend_back(row_of, first, heads, sizes, qkv, cap, cos_table, sin_table, marks, gains, tanh, crossed, grad):
    size, tokens, cap_tokens = sizes
    rows = cap.shape[0] // cap_tokens
    across = heads * size
    out_shape = [
        jax.ShapeDtypeStruct((3 * across, rows * tokens), BF16),
        jax.ShapeDtypeStruct((rows * tokens, 3 * across), BF16),
        jax.ShapeDtypeStruct((2 * across, rows * cap_tokens), BF16),
        jax.ShapeDtypeStruct((3, size, tokens), F32),
        jax.ShapeDtypeStruct((heads, 1, tokens), F32),
    ]
    return pl.pallas_call(
        functools.partial(backward_kernel, heads, size),
        grid=(rows,),
        in_specs=row_specs(row_of, sizes, across)
        + [
            whole(gains.shape),
            whole(tanh.shape),
            pl.BlockSpec((across, tokens), lambda i: (0, i)),
            pl.BlockSpec((across, tokens), lambda i: (0, row_of(i) - first)),
        ],
        out_specs=[
            pl.BlockSpec((3 * across, tokens), lambda i: (0, row_of(i) - first)),
            pl.BlockSpec((tokens, 3 * across), lambda i: (row_of(i) - first, 0)),
            pl.BlockSpec((2 * across, cap_tokens), lambda i: (0, i)),
            whole(out_shape[3].shape),
            whole(out_shape[4].shape),
        ],
        out_shape=out_shape,
        compiler_params=pltpu.CompilerParams(vmem_limit_bytes=24 * 1024 * 1024),
        cost_estimate=SMALL_COST,
    )(qkv, cap, cos_table, sin_table, marks, gains, tanh, crossed, grad)


def outer_kernel(counts, place_ref, *refs):
    lefts, rights = refs[: len(counts)], refs[len(counts) : -1]
    total, at = None, 0
    for left, count in zip(lefts, counts):
        begin = 0
        for right in rights[at : at + count]:
            end = begin + right.shape[0]
            part = dot10(left[:, begin:end], right[...])
            total = part if total is None else total + part
            begin = end
        at += count
    refs[-1][...] = total.astype(BF16)


def outer(lefts, rights, left_index, left_blocks, column_blocks, width):
    counts = tuple(len(group) for group in rights)
    flat = [piece for group in rights for piece in group]
    rows = lefts[0].shape[0] // left_blocks
    count = len(column_blocks)
    index = jnp.stack([left_index] + list(column_blocks)).astype(jnp.int32)
    tokens = sum(left.shape[1] for left in lefts)
    return pl.pallas_call(
        functools.partial(outer_kernel, counts),
        grid_spec=pltpu.PrefetchScalarGridSpec(
            num_scalar_prefetch=1,
            grid=(count,),
            in_specs=[
                pl.BlockSpec((rows, left.shape[1]), lambda i, place: (place[0], 0)) for left in lefts
            ]
            + [pl.BlockSpec((right.shape[0], width), lambda i, place: (0, place[1 + i])) for right in flat],
            out_specs=pl.BlockSpec((rows, width), lambda i, place: (0, i)),
        ),
        out_shape=jax.ShapeDtypeStruct((rows, count * width), BF16),
        compiler_params=pltpu.CompilerParams(vmem_limit_bytes=26 * 1024 * 1024),
        cost_estimate=SMALL_COST,
    )(index, *lefts, *flat)


def middle_kernel(inner, ffn_ref, gate_ref, up_ref, branch_ref, down_ref, act_ref, grad_ref):
    block = gate_ref.shape[1]
    grad_act = dot11(branch_ref[...], down_ref[...])
    gate = dot10(ffn_ref[...], gate_ref[...])
    up = dot10(ffn_ref[...], up_ref[...])
    sigmoid = 1.0 / (1.0 + jnp.exp(-gate))
    silu = gate * sigmoid
    at = pl.multiple_of(pl.program_id(0) * block, 128)
    act_ref[...] = (silu * up).astype(BF16)
    grad_ref[:, pl.ds(at, block)] = (grad_act * up * sigmoid * (1.0 + gate * (1.0 - sigmoid))).astype(BF16)
    grad_ref[:, pl.ds(at + inner, block)] = (grad_act * silu).astype(BF16)


def middle(ffn_in, w_ffn, grad_branch, w_down):
    tokens, width = ffn_in.shape
    inner = w_down.shape[0]
    block = 256
    steps = inner // block

    def whole(shape):
        return pl.BlockSpec(shape, lambda i: (0,) * len(shape))

    return pl.pallas_call(
        functools.partial(middle_kernel, inner),
        grid=(steps,),
        in_specs=[
            whole((tokens, width)),
            pl.BlockSpec((width, block), lambda i: (0, i)),
            pl.BlockSpec((width, block), lambda i: (0, i + steps)),
            whole((tokens, width)),
            pl.BlockSpec((block, width), lambda i: (i, 0)),
        ],
        out_specs=[
            pl.BlockSpec((tokens, block), lambda i: (0, i)),
            whole((tokens, 2 * inner)),
        ],
        out_shape=[
            jax.ShapeDtypeStruct((tokens, inner), BF16),
            jax.ShapeDtypeStruct((tokens, 2 * inner), BF16),
        ],
        compiler_params=pltpu.CompilerParams(vmem_limit_bytes=52 * 1024 * 1024),
        cost_estimate=SMALL_COST,
    )(ffn_in, w_ffn, w_ffn, grad_branch, w_down)


def outer_tokens_kernel(count, place_ref, *refs):
    total = None
    for left, right in zip(refs[:count], refs[count:-1]):
        part = dot00(left[...], right[...])
        total = part if total is None else total + part
    refs[-1][...] = total.astype(BF16)


def rows_kernel(*refs):
    *pieces, out_ref = refs
    at = 0
    for group in range(0, len(pieces), 4):
        near, far, near_right, far_right = pieces[group : group + 4]
        total = dot00(near[...], near_right[...]) + dot00(far[...], far_right[...])
        end = at + near_right.shape[1]
        out_ref[:, at:end] = total.astype(BF16)
        at = end


def outer_rows(*groups):
    block = 256
    columns = sum(group[2].shape[1] for group in groups)
    width = groups[0][0].shape[1]
    specs = []
    for near, far, near_right, far_right in groups:
        specs += [pl.BlockSpec((left.shape[0], block), lambda i: (0, i)) for left in (near, far)]
        specs += [pl.BlockSpec(right.shape, lambda i: (0, 0)) for right in (near_right, far_right)]
    return pl.pallas_call(
        rows_kernel,
        grid=(width // block,),
        in_specs=specs,
        out_specs=pl.BlockSpec((block, columns), lambda i: (i, 0)),
        out_shape=jax.ShapeDtypeStruct((width, columns), BF16),
        compiler_params=pltpu.CompilerParams(vmem_limit_bytes=18 * 1024 * 1024),
        cost_estimate=SMALL_COST,
    )(*[piece for group in groups for piece in group])


def outer_tokens(lefts, rights, left_block, blocks, right_block, right_blocks):
    block = 256
    columns = rights[0].shape[1] // right_blocks
    index = jnp.stack([jnp.asarray(left_block), jnp.asarray(right_block)]).astype(jnp.int32)
    return pl.pallas_call(
        functools.partial(outer_tokens_kernel, len(lefts)),
        grid_spec=pltpu.PrefetchScalarGridSpec(
            num_scalar_prefetch=1,
            grid=(blocks,),
            in_specs=[
                pl.BlockSpec((left.shape[0], block), lambda i, place: (0, place[0] + i)) for left in lefts
            ]
            + [
                pl.BlockSpec((right.shape[0], columns), lambda i, place: (0, place[1]))
                for right in rights
            ],
            out_specs=pl.BlockSpec((block, columns), lambda i, place: (i, 0)),
        ),
        out_shape=jax.ShapeDtypeStruct((blocks * block, columns), BF16),
        compiler_params=pltpu.CompilerParams(vmem_limit_bytes=18 * 1024 * 1024),
        cost_estimate=SMALL_COST,
    )(index, *lefts, *rights)


def join_kernel(widths, rows, chunks, place_ref, *refs):
    shards = refs[: len(widths)]
    near = refs[len(widths)]
    pieces = refs[len(widths) + 1 : len(widths) + 1 + 2 * chunks]
    out, sems = refs[-2:]
    copies = []

    def copy(source, row, count, column, width):
        target = out.at[pl.ds(pl.multiple_of(row, 16), count), pl.ds(column, width)]
        copies.append(pltpu.make_async_copy(source, target, sems.at[len(copies)]))
        copies[-1].start()

    at = 0
    for shard, width in zip(shards, widths):
        begin = pl.multiple_of(place_ref[4] * width, 128)
        copy(shard.at[:, pl.ds(begin, width)], place_ref[0] * rows, rows, at, width)
        at += width
    copy(near, place_ref[1] * rows, rows, 0, at)
    part = rows // chunks
    for chunk in range(chunks):
        for kind in range(2):
            row = place_ref[2 + kind] * rows + chunk * part
            copy(pieces[2 * chunk + kind], row, part, 0, at)
    for item in copies:
        item.wait()


def join(place_index, shards, near, pieces):
    widths = tuple(shard.shape[1] // 4 for shard in shards)
    rows = near.shape[0]
    chunks = len(pieces) // 2
    count = len(shards) + 1 + len(pieces)
    return pl.pallas_call(
        functools.partial(join_kernel, widths, rows, chunks),
        grid_spec=pltpu.PrefetchScalarGridSpec(
            num_scalar_prefetch=1,
            grid=(1,),
            in_specs=[pl.BlockSpec(memory_space=pl.ANY)] * count,
            out_specs=pl.BlockSpec((4 * rows, sum(widths)), lambda i, place: (0, 0)),
            scratch_shapes=[pltpu.SemaphoreType.DMA((count,))],
        ),
        out_shape=jax.ShapeDtypeStruct((4 * rows, sum(widths)), near.dtype),
        compiler_params=pltpu.CompilerParams(vmem_limit_bytes=50 * 1024 * 1024),
        cost_estimate=SMALL_COST,
    )(place_index, *shards, near, *pieces)


class Flow:
    def __init__(self, steps):
        self.steps = steps
        self.result = None
        self.waiting = next(steps)

    def step(self, values):
        if self.result is not None:
            return
        try:
            self.waiting = self.steps.send(values)
        except StopIteration as stop:
            self.waiting, self.result = (), stop.value


class Place:
    def __init__(self, mesh):
        self.copies = mesh.shape["dp"]
        self.shards = mesh.shape["fsdp"]
        self.top_step = self.copies // 2
        self.team_step = self.copies // 4
        self.low = self.copies // 4
        self.last = {}
        self.before, self.token = (), ()

    def locate(self):
        self.dp = lax.axis_index("dp")
        self.fsdp = lax.axis_index("fsdp")
        self.side = self.fsdp // 2
        self.core = self.fsdp % 2
        self.top = self.dp // self.top_step
        self.team = (self.dp // self.team_step) % 2
        self.lane = self.dp % 2
        self.quarter = 2 * self.core + self.team

    def swap(self, value, dp=0, fsdp=0, link=None):
        return self.route(value, lambda d, f: (d ^ dp, f ^ fsdp), link)

    def route(self, value, target, link=None):
        pairs = []
        for d in range(self.copies):
            for f in range(self.shards):
                to = target(d, f)
                if to is not None:
                    pairs.append((d * self.shards + f, to[0] * self.shards + to[1]))
        value = after(value, *self.before, *self.last.get(link, ()))
        self.operand = value
        value = lax.ppermute(value, ("dp", "fsdp"), pairs)
        if link is not None:
            self.last[link] = (value,)
        return value

    def next_wave(self, *others):
        self.before = others

    def arrive(self, *values):
        values = lax.optimization_barrier(values)
        self.before = values
        return values

    def meet(self, flows, *values):
        waiting = [array for flow in flows for array in flow.waiting]
        arrived = self.arrive(*waiting, *values)
        self.done(*(arrived[len(waiting) :] or arrived[:1]))
        at = 0
        for flow in flows:
            count = len(flow.waiting)
            flow.step(arrived[at : at + count])
            at += count
        return arrived[at:]

    def held(self, value):
        if isinstance(value, tuple):
            return tuple(self.held(part) for part in value)
        return after(value, *self.token)

    def done(self, *values):
        self.token = values

    def bits(self, d, f):
        return ((d // self.team_step) % 2, f // 2, f % 2, d % 2)

    def team_swap(self, value):
        return self.swap(value, dp=self.team_step, link="z")

    def core_swap(self, value):
        return self.swap(value, fsdp=1, link="c")


    def cut_columns(self, shards):
        def cut(quarter):
            parts = []
            for shard in shards:
                width = shard.shape[1] // 4
                parts.append(lax.dynamic_slice_in_dim(shard, quarter * width, width, axis=1))
            return jnp.concatenate(parts, axis=1)

        return cut(2 * (self.core ^ self.lane) + self.team), cut(2 * (1 - self.core) + self.team)

    def side_swap(self, piece):
        return self.route(piece, lambda d, f: (d, f ^ 2 ^ (d % 2)), "x")

    def lane_swap(self, piece):
        return self.swap(piece, dp=1, link="y")

    def join_columns(self, shards, near, pieces):
        index = [self.fsdp, self.fsdp ^ 1, self.fsdp ^ 2 ^ self.lane, self.fsdp ^ 3 ^ self.lane]
        return join(jnp.stack(index + [self.quarter]).astype(jnp.int32), shards, near, pieces)

    def rows_side_swap(self, shard):
        def target(d, f):
            team, side, core, _ = self.bits(d, f)
            return (d, 2 * (1 - side) + side) if core == team else None

        return self.route(shard, target, "x")

    def rows_lane_swap(self, piece):
        def target(d, f):
            _, side, core, _ = self.bits(d, f)
            return (d ^ 1, f) if core != side else None

        return self.route(piece, target, "y")

    def rows_core_swap(self, shard):
        def target(d, f):
            team, side, core, _ = self.bits(d, f)
            return (d, 2 * side + side) if core == team and side != team else None

        return self.route(shard, target, "c")

    def join_rows(self, shard, near, across, far):
        source = jnp.where(
            self.core != self.side, 2, jnp.where(self.side == self.team, 0, 1)
        )
        return join_rows(jnp.stack([source, self.lane]).astype(jnp.int32), shard, near, across, far)


    def part(self, value, index, axis):
        if isinstance(value, tuple):
            return tuple(self.part(array, index, axis) for array in value)
        size = value.shape[axis] // 2
        return lax.dynamic_slice_in_dim(value, index * size, size, axis=axis)

    def summed(self, arrays):
        return sum(array.astype(F32) for array in arrays).astype(BF16)

    def halves(self, value, axis, keep):
        sent = self.summed([self.part(array, 1 - keep, axis) for array in value])
        return sent, [self.part(array, keep, axis) for array in value]

    def low_steps(self):
        step = self.low // 2
        while step:
            yield step, (self.dp // step) % 2
            step //= 2

    def spread(self, first, second, place, chunks=1, ahead=False, hold=False):
        (step, keep), *lows = self.low_steps()
        side, low, kept = [], [], ()
        sents = [(first[0](1 - place, i), second[0](1 - keep, i)) for i in range(chunks)]
        if chunks > 1:
            kept = tuple(first[1](place, i) for i in range(chunks))
            kept += tuple(second[1](keep, i) for i in range(chunks))
        if ahead:
            sents = [(yield sents[0])]
        if ahead == 2:
            kept = first[1](place, 0), second[1](keep, 0)
            arrived = yield tuple(sents[0]) + kept
            sents, kept = [arrived[:2]], arrived[2:]
        for chunk in range(chunks):
            first_got = self.swap(sents[chunk][0], fsdp=2)
            operands = (self.operand,)
            second_got = self.swap(sents[chunk][1], dp=step)
            self.operands = operands + (self.operand,)
            rest = tuple(part for pair in sents[chunk + 1 :] for part in pair)
            if not kept:
                yield first_got, second_got
                kept = first[1](place, 0), second[1](keep, 0)
            arrived = yield (first_got, second_got) + kept + rest
            side.append(arrived[0])
            low.append(arrived[1])
            kept, rest = arrived[2 : 2 + len(kept)], arrived[2 + len(kept) :]
            sents[chunk + 1 :] = [rest[i : i + 2] for i in range(0, len(rest), 2)]

        def joined(parts):
            return parts[0] if chunks == 1 else jnp.concatenate(parts, axis=0)

        if chunks == 2 and not lows:
            pairs = (kept[:chunks], side)
            sent_first = self.summed([jnp.where(keep == 0, pair[1], pair[0]) for pair in pairs])
            first = [jnp.where(keep == 0, pair[0], pair[1]) for pair in pairs]
        else:
            sent_first, first = self.halves([joined(kept[:chunks]), joined(side)], 0, keep)
        second = [joined(kept[chunks:]), joined(low)]
        sent_second, second = self.halves(second, 1, place)
        if hold:
            sent_first, sent_second = yield sent_first, sent_second
        got = yield self.swap(sent_first, dp=step), self.swap(sent_second, fsdp=2)
        first.append(got[0])
        second.append(got[1])
        for step, keep in lows:
            sent_first, first = self.halves(first, 0, keep)
            sent_second, second = self.halves(second, 0, keep)
            first.append(self.swap(sent_first, dp=step))
            second.append(self.swap(sent_second, dp=step))
        return first, second

    def finish(self, own, sent, parts, apart=False):
        got = self.core_swap(sent)
        if apart:
            (got,) = yield (got,)
        straight = self.core == self.top
        sent = jnp.split(jnp.where(straight, got, own), parts, axis=0)
        kept = jnp.split(jnp.where(straight, own, got), parts, axis=0)
        totals = []
        for part in range(parts):
            (got,) = yield (self.swap(sent[part], dp=self.top_step),)
            totals.append(kept[part].astype(F32) + got.astype(F32))
        return totals

    def pair_back(self, by_side, by_low):
        first, second = yield from self.spread((by_side, by_side), (by_low, by_low), self.side, 2)

        def both(index):
            return jnp.concatenate(
                [self.summed([self.part(array, index, 1) for array in value]) for value in (first, second)]
            )

        (value,) = yield from self.finish(both(self.core), both(1 - self.core), 1, True)
        return [part.T for part in jnp.split(value, 2, axis=0)]

    def split_back(self, by_side, by_low, count, parts, ahead=False):
        yield ()
        first, second = yield from self.spread(
            (by_side, by_side), (by_low, by_low), self.side, 1, ahead
        )
        first, second = self.summed(first), self.summed(second)
        own = jnp.where(self.core == 0, first, second)
        sent = jnp.where(self.core == 0, second, first)
        value = yield from self.finish(own, sent, parts)
        return [part.T for total in value for part in jnp.split(total, count // parts, axis=0)]

    def rows_back(self, grad, hold=False):
        columns, rows = grad.shape
        value = grad.reshape(2, 2, columns // 4, rows)
        own = lax.dynamic_index_in_dim(value, self.core, 1, keepdims=False)
        sent = lax.dynamic_index_in_dim(value, 1 - self.core, 1, keepdims=False)
        got = self.core_swap(sent)
        straight = self.core == self.side
        kept = jnp.where(straight, own, got)
        sent = jnp.where(straight, got, own)
        wide = jnp.concatenate([kept[1], sent[1]], axis=1)
        pieces = sent[0], kept[0]
        *pieces, wide = yield (*pieces, wide)

        def by_low(index, _):
            return self.part(wide, index, 0)

        first, second = yield from self.spread(
            (lambda *_: pieces[0], lambda *_: pieces[1]), (by_low, by_low), 0, hold=hold
        )
        first, second = self.summed(first), self.summed(second)
        sent = jnp.where(self.top == 0, second, first)
        (got,) = yield (self.swap(sent, dp=self.top_step),)
        value = self.summed([jnp.where(self.top == 0, first, second), got])

        def turn(d, f):
            team, _, core, _ = self.bits(d, f)
            return (d ^ self.team_step, f ^ 1) if core != team else (d, f)

        (got,) = yield (self.route(value, turn),)
        return got.astype(F32).T

    def total(self, value):
        for bit in (1, 2):
            value = value + self.swap(value, fsdp=bit)
        step = 1
        while step < self.copies:
            value = value + self.swap(value, dp=step)
            step *= 2
        return value


def layer(
    place,
    block_input,
    caption,
    modulation,
    segment_ids,
    pos_row,
    pos_col,
    caption_len,
    gain_attn,
    w_query,
    w_key,
    w_value,
    gain_query,
    gain_key,
    w_cap_key,
    w_cap_value,
    gain_cap_key,
    head_gate,
    w_out,
    gain_ffn,
    w_gate,
    w_up,
    w_down,
    cotangent,
):
    place.locate()
    rows, tokens, width = block_input.shape
    cap_tokens = caption.shape[1]
    size = gain_query.shape[0] * place.shards
    team_rows = 4 * rows

    qkv_shards, cap_shards, ffn_shards = (w_query, w_key, w_value), (w_cap_key, w_cap_value), (w_gate, w_up)
    qkv_sent, qkv_near = place.cut_columns(qkv_shards)
    qkv_side = place.side_swap(qkv_sent)
    cap_pieces = [caption[0, : cap_tokens // 2], caption[0, cap_tokens // 2 :]]
    cap_pieces += [caption[1, : cap_tokens // 2], caption[1, cap_tokens // 2 :]]
    far_pieces = [place.team_swap(cap_pieces[0])]

    small = (gain_attn, gain_ffn, gain_query, gain_key, gain_cap_key, head_gate)
    piece = after(jnp.concatenate(small), qkv_sent)
    pair = jnp.stack([piece, place.core_swap(piece)])
    other = place.swap(pair, fsdp=2)
    packed = jnp.zeros((place.shards,) + piece.shape, piece.dtype)
    for part, index in ((pair[0], 0), (pair[1], 1), (other[0], 2), (other[1], 3)):
        packed = lax.dynamic_update_index_in_dim(packed, part, place.fsdp ^ index, 0)
    packed = packed.astype(F32)
    full_small, at = [], 0
    for vector in small:
        full_small.append(packed[:, at : at + vector.shape[0]].reshape(-1))
        at += vector.shape[0]
    full_gain_attn, full_gain_ffn, query_gain, key_gain, cap_gain, full_head_gate = full_small
    heads = full_head_gate.shape[0] // 4
    across = heads * size
    sizes = (size, tokens, cap_tokens)

    cap_own = caption.reshape(-1, caption.shape[-1])
    cap_core = place.core_swap(cap_own)
    cap_sent, cap_w_near = place.cut_columns(cap_shards)
    cap_sent = jnp.split(cap_sent, 2, axis=0)
    ffn_sent, ffn_w_near = place.cut_columns(ffn_shards)
    ffn_sent = jnp.split(ffn_sent, 2, axis=0)
    half_out, half_down = w_out.shape[0] // 2, w_down.shape[0] // 2
    rows_sent = jnp.concatenate(
        [place.part(w_out, place.lane, 0), place.part(w_down, place.lane, 0)], axis=0
    )

    inputs = block_input.astype(F32)
    scale_attn = 1.0 + modulation[:, 0][:, None, :]
    tanh_attn = jnp.tanh(modulation[:, 1])[:, None, :]
    scale_ffn = 1.0 + modulation[:, 2][:, None, :]
    tanh_ffn = jnp.tanh(modulation[:, 3])[:, None, :]
    upstream = cotangent.astype(F32)
    grad_branch = (upstream * tanh_ffn).astype(BF16).reshape(-1, width)
    normed_in, inverse_in = rms_scale(inputs)
    attn_in = (normed_in * full_gain_attn * scale_attn).astype(BF16).reshape(-1, width)

    own_tokens = rows * tokens
    marks = jnp.stack(
        [segment_ids, pos_row, pos_col, jnp.broadcast_to(caption_len[:, None], (rows, tokens))]
    )
    marks = marks.astype(BF16).reshape(4, own_tokens)
    marks = jnp.pad(marks, ((0, 12), (0, width - own_tokens)))
    marked = jnp.concatenate([attn_in, marks], axis=0)

    qkv_side, far_piece = place.arrive(qkv_side, far_pieces[0])
    far_pieces = [far_piece]
    cap_side = place.side_swap(cap_sent[0])
    qkv_lane = place.lane_swap(qkv_side)
    marked_far = place.team_swap(marked)
    place.before = ()
    qkv_near = place.core_swap(qkv_near)
    marked_near = place.core_swap(marked)

    cap_side, qkv_lane, marked_far = place.arrive(cap_side, qkv_lane, marked_far)
    cap_pairs = [cap_side]
    next_side = place.side_swap(cap_sent[1])
    cap_lane = place.lane_swap(cap_side)
    far_piece = place.team_swap(cap_pieces[1])
    place.before = ()
    marked_last = place.core_swap(marked_far)
    cap_w_near = place.core_swap(cap_w_near)
    blocks = (marked, marked_near, marked_far, marked_last)
    attn_all = jnp.concatenate([block[:own_tokens] for block in blocks], axis=0)
    marks = jnp.concatenate([block[own_tokens:, :own_tokens] for block in blocks], axis=1).astype(F32)
    w_qkv = place.join_columns(qkv_shards, qkv_near, [qkv_side, qkv_lane])

    next_side, cap_lane, far_piece, attn_all, w_qkv = place.arrive(
        next_side, cap_lane, far_piece, attn_all, w_qkv
    )
    cap_pairs += [cap_lane, next_side]
    far_pieces.append(far_piece)
    rows_side = place.rows_side_swap(rows_sent)
    cap_lane = place.lane_swap(next_side)
    far_piece = place.team_swap(cap_pieces[2])
    place.before = ()
    far_first = jnp.concatenate(far_pieces, axis=0)
    far_first_core = place.core_swap(far_first)
    ffn_w_near = place.core_swap(ffn_w_near)
    qkv_raw = dot(attn_all, w_qkv)

    quarter_size = size // 4
    frequency = jnp.exp(
        jnp.arange(quarter_size, dtype=F32) * (-math.log(10000.0) / quarter_size)
    )
    row_angle = frequency[:, None] * marks[1][None, :]
    col_angle = frequency[:, None] * marks[2][None, :]
    angles = jnp.concatenate([row_angle, row_angle, col_angle, col_angle], axis=0)
    cos_table, sin_table = jnp.cos(angles), jnp.sin(angles)
    marks = jnp.stack([marks[0], marks[3]]).reshape(2, team_rows, tokens)
    marks = jnp.pad(jnp.moveaxis(marks, 0, 1), ((0, 0), (0, 6), (0, 0)))
    gains = jnp.broadcast_to(
        jnp.stack([query_gain, key_gain, cap_gain])[:, :, None], (3, size, tokens)
    )
    head_tanh = jnp.tanh(lax.dynamic_slice_in_dim(full_head_gate, place.quarter * heads, heads))
    tanh_table = jnp.broadcast_to(head_tanh[:, None, None], (heads, 1, tokens))
    tables = (cos_table, sin_table, marks, gains, tanh_table)
    half = team_rows // 2

    def far_row(i):
        return half + (i % rows) * rows + i // rows

    def rows_from(first):
        return lambda i: first + i

    rows_side, cap_lane, far_piece, qkv_raw, cos_table = place.arrive(
        rows_side, cap_lane, far_piece, qkv_raw, cos_table
    )
    tables = (cos_table,) + tables[1:]
    cap_pairs.append(cap_lane)
    far_pieces = [far_piece]
    ffn_side = place.side_swap(ffn_sent[0])
    rows_lane = place.rows_lane_swap(rows_side)
    far_piece = place.team_swap(cap_pieces[3])
    w_cap = place.join_columns(cap_shards, cap_w_near, cap_pairs)
    out_near = place.rows_core_swap(w_out)
    branch_core = place.core_swap(grad_branch)
    place.before = ()
    near_raw, mixed_near, near_crossed = attend(
        rows_from(0), heads, sizes, qkv_raw, (cap_own, cap_core), w_cap, *tables
    )

    ffn_side, rows_lane, far_piece, mixed_near = place.arrive(ffn_side, rows_lane, far_piece, mixed_near)
    ffn_pairs = [ffn_side]
    far_pieces.append(far_piece)
    next_side = place.side_swap(ffn_sent[1])
    ffn_lane = place.lane_swap(ffn_side)
    branch_far = place.team_swap(grad_branch)
    place.before = ()
    far_second = jnp.concatenate(far_pieces, axis=0)
    far_second_core = place.core_swap(far_second)
    down_near = place.rows_core_swap(w_down)
    w_out = place.join_rows(w_out, out_near, rows_side[:half_out], rows_lane[:half_out])
    first_raw, mixed_first, first_crossed = attend(
        lambda i: half + i * rows, heads, sizes, qkv_raw, (far_first, far_first_core), w_cap, *tables
    )
    second_raw, mixed_second, second_crossed = attend(
        lambda i: half + 1 + i * rows,
        heads,
        sizes,
        qkv_raw,
        (far_second, far_second_core),
        w_cap,
        *tables,
    )
    next_side, ffn_lane, branch_far, mixed_second = place.arrive(
        next_side, ffn_lane, branch_far, mixed_second
    )
    ffn_pairs += [ffn_lane, next_side]
    place.before = ()
    place.done(mixed_second)
    far_raw = jnp.concatenate([first_raw, second_raw], axis=0)
    far_crossed = jnp.concatenate([first_crossed, second_crossed], axis=1)
    mixed_blocks = (
        *jnp.split(mixed_near, 2, axis=0),
        jnp.concatenate([mixed_first[:tokens], mixed_second[:tokens]], axis=0),
        jnp.concatenate([mixed_first[tokens:], mixed_second[tokens:]], axis=0),
    )
    def far_sum(blocks, right, product):
        last = place.core_swap(product(place.held(blocks[3]), right).astype(BF16))
        far = product(place.held(blocks[2]), right) + last.astype(F32)
        return place.team_swap(far.astype(BF16))

    def near_sum(blocks, right, product):
        got = place.core_swap(product(place.held(blocks[1]), right).astype(BF16))
        return product(place.held(blocks[0]), right) + got.astype(F32)

    attn_far_sum = far_sum(mixed_blocks, w_out, dot)
    ffn_pairs.append(place.lane_swap(next_side))
    w_down = place.join_rows(w_down, down_near, rows_side[half_out:], rows_lane[half_out:])
    branch_near = jnp.concatenate([grad_branch, branch_core], axis=0)
    branch_far = jnp.concatenate([branch_far, place.core_swap(branch_far)], axis=0)
    w_ffn = place.join_columns(ffn_shards, ffn_w_near, ffn_pairs)
    attn_near_sum = near_sum(mixed_blocks, w_out, dot)
    attn_far_sum, attn_near_sum, w_ffn, w_down = place.arrive(
        attn_far_sum, attn_near_sum, w_ffn, w_down
    )
    place.before = ()
    attn_branch = (attn_near_sum + attn_far_sum.astype(F32)).reshape(inputs.shape)
    hidden = inputs + tanh_attn * attn_branch

    normed_mid, inverse_mid = rms_scale(hidden)
    ffn_in = (normed_mid * full_gain_ffn * scale_ffn).astype(BF16).reshape(-1, width)

    ffn_far = place.team_swap(ffn_in)
    ffn_near = jnp.concatenate([ffn_in, place.core_swap(ffn_in)], axis=0)
    act_near, grad_near = middle(ffn_near, w_ffn, branch_near, w_down)
    place.done(act_near, grad_near)
    ffn_far = place.held(ffn_far)
    ffn_far = jnp.concatenate([ffn_far, place.core_swap(ffn_far)], axis=0)
    act_far, grad_far = middle(ffn_far, w_ffn, branch_far, w_down)
    place.done(act_far, grad_far)
    grad_blocks = (*jnp.split(grad_near, 2, axis=0), *jnp.split(grad_far, 2, axis=0))
    act_blocks = (*jnp.split(act_near, 2, axis=0), *jnp.split(act_far, 2, axis=0))
    blocks = act_near.shape[1] // 256

    def gate_by_side(side, chunk):
        lefts = place.held((grad_near, grad_far))
        each = blocks // 2
        return outer_tokens(lefts, (ffn_near, ffn_far), chunk * each, each, side, 2)

    def up_by_low(index, chunk):
        lefts = place.held((grad_near, grad_far))
        each = blocks // 4
        first = blocks + index * (blocks // 2) + chunk * each
        return outer_tokens(lefts, (ffn_near, ffn_far), first, each, 0, 1)

    ffn_far_sum = far_sum(grad_blocks, w_ffn, dot_back)
    ffn = Flow(place.pair_back(gate_by_side, up_by_low))
    ffn_near_sum = near_sum(grad_blocks, w_ffn, dot_back)
    ffn_far_sum, ffn_near_sum = place.meet([ffn], ffn_far_sum, ffn_near_sum)
    place.before = ()
    grad_ffn_in = (ffn_near_sum + ffn_far_sum.astype(F32)).reshape(inputs.shape)
    grad_ffn_gain = jnp.sum(grad_ffn_in * normed_mid * scale_ffn, axis=(0, 1))
    grad_mod_ffn_scale = jnp.sum(grad_ffn_in * normed_mid * full_gain_ffn, axis=1)
    grad_hidden = upstream + rms_back(
        grad_ffn_in * full_gain_ffn * scale_ffn, normed_mid, inverse_mid
    )

    grad_attn_branch = (grad_hidden * tanh_attn).astype(BF16).reshape(-1, width)
    grad_mod_attn_gate = jnp.sum(grad_hidden * attn_branch, axis=1) * (
        1.0 - tanh_attn[:, 0] * tanh_attn[:, 0]
    )
    attn_grad_far = place.team_swap(grad_attn_branch)
    attn_grad_near = jnp.concatenate([grad_attn_branch, place.core_swap(grad_attn_branch)], axis=0)

    def heads_back(row_of, first, cap_raw, crossed, grad):
        grad_mixed = dot_back(w_out, grad).astype(BF16)
        result = attend_back(
            row_of, first, heads, sizes, qkv_raw, cap_raw, *tables, crossed, grad_mixed
        )
        return list(result)

    near = heads_back(rows_from(0), 0, near_raw, near_crossed, attn_grad_near)
    attn_grad_far, near[0] = place.meet([ffn], attn_grad_far, near[0])
    place.before = ()
    place.done(place.operand)
    attn_grad_far = jnp.concatenate([attn_grad_far, place.core_swap(attn_grad_far)], axis=0)
    grad_rows = outer_rows(
        (branch_near, branch_far, *place.held((act_near, act_far))),
        (
            attn_grad_near,
            attn_grad_far,
            mixed_near,
            jnp.concatenate(mixed_blocks[2:], axis=0),
        ),
    )
    down = Flow(place.rows_back(grad_rows))
    attn_grad_far = after(attn_grad_far, grad_rows)
    far = heads_back(far_row, half, far_raw, far_crossed, attn_grad_far)

    def mix(grads, count):
        shaped = grads.reshape(count, place.low, -1, grads.shape[1])
        return jnp.moveaxis(shaped, 0, 1).reshape(grads.shape)

    cap_lefts = []
    cap_rights = (cap_own, cap_core), (far_first, far_first_core, far_second, far_second_core)
    block = min(512, caption.shape[2] // 4)
    per = caption.shape[2] // 4 // block

    def cap_by_side(side, _):
        lefts = place.held(tuple(cap_lefts))
        return outer(lefts, cap_rights, 0, 1, [2 * per * side + i for i in range(per)], block)

    def cap_by_low(index, _):
        lefts = place.held(tuple(cap_lefts))
        columns = [start * per + i for start in (1, 3) for i in range(per)]
        return outer(lefts, cap_rights, index, 2, columns, block)

    far[0], far[2] = place.meet([ffn, down], far[0], far[2])
    down.step(())
    cap_lefts += [mix(near[2], 2), mix(far[2], 2)]
    cap = Flow(place.split_back(cap_by_side, cap_by_low, 2, 2, 2))
    cap.step(())
    place.meet([ffn, down, cap])
    place.meet([down, cap])
    place.done(place.before[0])
    place.before = ()
    branch_far_sum = far_sum(act_blocks, w_down, dot)
    branch_near_sum = near_sum(act_blocks, w_down, dot)
    branch_near_sum, branch_far_sum = place.meet([ffn, cap], branch_near_sum, branch_far_sum)
    place.before = ()
    plain = (*jnp.split(near[1], 2, axis=0), *jnp.split(far[1], 2, axis=0))
    plain = place.held(plain)
    attn_far_sum = far_sum(plain, w_qkv, dot_back)
    attn_near_sum = near_sum(plain, w_qkv, dot_back)
    turned = mix(jnp.concatenate([near[0], far[0]], axis=1), 3)
    columns = width // 4
    low_rows = jnp.concatenate([attn_all[:, i * columns : (i + 1) * columns] for i in (1, 3)], axis=1)

    def qkv_by_side(side, _):
        right = lax.dynamic_slice_in_dim(attn_all, 2 * side * columns, columns, axis=1)
        return dot(place.held(turned), right).astype(BF16)

    def qkv_by_low(index, _):
        return dot(place.part(place.held(turned), index, 0), low_rows).astype(BF16)

    qkv = Flow(place.split_back(qkv_by_side, qkv_by_low, 3, 1, True))
    qkv.step(())
    attn_far_sum, attn_near_sum = place.meet([cap, qkv, down], attn_far_sum, attn_near_sum)
    qkv.step(())
    grad_attn_in = (attn_near_sum + attn_far_sum.astype(F32)).reshape(inputs.shape)
    grad_gain_in = jnp.sum(grad_attn_in * normed_in * scale_attn, axis=(0, 1))
    grad_mod_attn_scale = jnp.sum(grad_attn_in * normed_in * full_gain_attn, axis=1)
    input_grad = (
        grad_hidden + rms_back(grad_attn_in * full_gain_attn * scale_attn, normed_in, inverse_in)
    ).astype(BF16)
    gate_parts = near[4] + far[4]
    gain_parts = jnp.sum(near[3] + far[3], axis=2)
    grad_head_gate = jnp.sum(gate_parts, axis=(1, 2)) * (1.0 - head_tanh * head_tanh)
    ffn_branch = (branch_near_sum + branch_far_sum.astype(F32)).reshape(inputs.shape)
    block_out = (hidden + tanh_ffn * ffn_branch).astype(BF16)
    grad_mod_ffn_gate = jnp.sum(upstream * ffn_branch, axis=1) * (
        1.0 - tanh_ffn[:, 0] * tanh_ffn[:, 0]
    )
    head_part = jnp.zeros_like(full_head_gate)
    head_part = lax.dynamic_update_slice_in_dim(
        head_part, grad_head_gate, place.quarter * heads, axis=0
    )
    parts = (
        grad_gain_in,
        grad_ffn_gain,
        gain_parts[0],
        gain_parts[1],
        gain_parts[2],
        head_part,
    )
    small_grads = jnp.concatenate(parts)
    place.before = ()
    summed = place.total(small_grads)
    input_grad, block_out = place.meet([qkv, cap, down], input_grad, block_out)
    (summed,) = place.meet([qkv, cap, down], summed)
    for flow in (ffn, qkv, cap, down):
        for _ in range(5):
            flow.step(flow.waiting)
    modulation_grad = jnp.stack(
        [grad_mod_attn_scale, grad_mod_attn_gate, grad_mod_ffn_scale, grad_mod_ffn_gate], axis=1
    )

    vectors, at = [], 0
    for vector in parts:
        length = vector.shape[0] // place.shards
        vectors.append(lax.dynamic_slice_in_dim(summed, at + place.fsdp * length, length))
        at += vector.shape[0]
    return (
        block_out,
        input_grad,
        modulation_grad,
        vectors[0],
        qkv.result[0],
        qkv.result[1],
        qkv.result[2],
        vectors[2],
        vectors[3],
        cap.result[0],
        cap.result[1],
        vectors[4],
        vectors[5],
        down.result[w_down.shape[0] :],
        vectors[1],
        ffn.result[0],
        ffn.result[1],
        down.result[: w_down.shape[0]],
    )


def solution(mesh):
    def shards(*arrays):
        return layer(Place(mesh), *arrays)

    rows = P(("dp", "fsdp"), None, None)
    marks = P(("dp", "fsdp"), None)
    vector = P("fsdp")
    weight = P("fsdp", None)
    grad = P("fsdp", "dp")
    return jax.shard_map(
        shards,
        mesh=mesh,
        in_specs=(
            (rows, rows, rows, marks, marks, marks, P(("dp", "fsdp")), vector)
            + (weight, weight, weight, vector, vector, weight, weight, vector, vector, weight)
            + (vector, weight, weight, weight, rows)
        ),
        out_specs=(
            (rows, rows, rows, vector, grad, grad, grad, vector, vector, grad, grad, vector)
            + (vector, grad, vector, grad, grad, grad)
        ),
        check_vma=False,
    )
```

```python
import functools
import math

import jax
import jax.numpy as jnp
from jax import lax
from jax.experimental import pallas as pl
from jax.experimental.pallas import tpu as pltpu
from jax.sharding import PartitionSpec as P

EPSILON = 1e-06
NEGATIVE = -1e30
BF16 = jnp.bfloat16
F32 = jnp.float32
SMALL_COST = pl.CostEstimate(flops=1024, bytes_accessed=1024, transcendentals=0)


def rms_scale(values):
    inverse = lax.rsqrt(jnp.mean(values * values, axis=-1, keepdims=True) + EPSILON)
    return (values * inverse, inverse)


def rms_back(incoming, normed, inverse):
    return inverse * (incoming - normed * jnp.mean(incoming * normed, axis=-1, keepdims=True))


def dot(left, right):
    return jnp.einsum("tc,ce->te", left, right, preferred_element_type=F32)


def dot_back(incoming, weight):
    return jnp.einsum("te,ce->tc", incoming, weight, preferred_element_type=F32)


def dot_tokens(left, right):
    return jnp.einsum("tc,te->ce", left, right, preferred_element_type=F32)


def after(value, *others):
    if not others:
        return value
    return lax.optimization_barrier((value,) + others)[0]


def join_rows_kernel(place_ref, shard, near, across, far, out, sems):
    half = across.shape[0]
    source, lane = place_ref[0], place_ref[1]

    def copy(piece, row, count, sem):
        item = pltpu.make_async_copy(piece, out.at[pl.ds(row, count)], sem)
        item.start()
        return item

    @pl.when(source == 0)
    def _():
        copy(shard, 0, 2 * half, sems.at[0]).wait()

    @pl.when(source == 1)
    def _():
        copy(near, 0, 2 * half, sems.at[0]).wait()

    @pl.when(source == 2)
    def _():
        first = copy(across, pl.multiple_of(lane * half, 16), half, sems.at[0])
        second = copy(far, pl.multiple_of((1 - lane) * half, 16), half, sems.at[1])
        first.wait()
        second.wait()


def join_rows(index, shard, near, across, far):
    return pl.pallas_call(
        join_rows_kernel,
        grid_spec=pltpu.PrefetchScalarGridSpec(
            num_scalar_prefetch=1,
            grid=(1,),
            in_specs=[pl.BlockSpec(memory_space=pl.ANY)] * 4,
            out_specs=pl.BlockSpec(shard.shape, lambda i, place: (0, 0)),
            scratch_shapes=[pltpu.SemaphoreType.DMA((2,))],
        ),
        out_shape=jax.ShapeDtypeStruct(shard.shape, shard.dtype),
        compiler_params=pltpu.CompilerParams(vmem_limit_bytes=50 * 1024 * 1024),
        cost_estimate=SMALL_COST,
    )(index, shard, near, across, far)


def quarter_turn(values):
    heads, size, tokens = values.shape
    parts = values.reshape(heads, 2, 2, size // 4, tokens)
    turned = jnp.concatenate([-parts[:, :, 1:], parts[:, :, :1]], axis=2)
    return turned.reshape(heads, size, tokens)


def head_norm(raw):
    inverse = lax.rsqrt(jnp.mean(raw * raw, axis=1, keepdims=True) + EPSILON)
    return raw * inverse, inverse


def head_norm_back(incoming, normed, inverse, gain):
    scaled = incoming * gain
    return inverse * (scaled - normed * jnp.mean(scaled * normed, axis=1, keepdims=True))


def dot00(left, right):
    return lax.dot_general(left, right, (((0,), (0,)), ((), ())), preferred_element_type=F32)


def dot11(left, right):
    return lax.dot_general(left, right, (((1,), (1,)), ((), ())), preferred_element_type=F32)


def dot10(left, right):
    return lax.dot_general(left, right, (((1,), (0,)), ((), ())), preferred_element_type=F32)


def softmax0(scores):
    top = jnp.max(scores, axis=0, keepdims=True)
    raised = jnp.exp(scores - top)
    return raised * (1.0 / jnp.sum(raised, axis=0, keepdims=True))


def row_state(qkv, cap, cos_table, sin_table, marks, gains, heads, size):
    tokens, cap_tokens = qkv.shape[0], cap.shape[0]
    across = heads * size
    qkv = qkv.T
    cap = cap.T

    def split(values, at):
        return values[at * across : (at + 1) * across].reshape(heads, size, -1)

    query_normed, query_inverse = head_norm(split(qkv, 0))
    key_normed, key_inverse = head_norm(split(qkv, 1))
    cap_normed, cap_inverse = head_norm(split(cap, 0))

    def rotate(values):
        return (values * cos_table + quarter_turn(values) * sin_table).astype(BF16)

    segment = marks[0:1]
    key_segment = jnp.broadcast_to(segment, (tokens, tokens)).T
    return {
        "queries": rotate(query_normed * gains[0]),
        "keys": rotate(key_normed * gains[1]),
        "values": split(qkv, 2).astype(BF16),
        "cap_keys": (cap_normed * gains[2][:, :1]).astype(BF16),
        "cap_values": split(cap, 1).astype(BF16),
        "norms": (query_normed, query_inverse, key_normed, key_inverse, cap_normed, cap_inverse),
        "same": key_segment == segment,
        "in_use": lax.broadcasted_iota(jnp.int32, (cap_tokens, tokens), 0).astype(F32)
        < marks[1:2],
    }


def forward_kernel(
    heads,
    size,
    half,
    qkv_ref,
    first_ref,
    second_ref,
    weight_ref,
    cos_ref,
    sin_ref,
    marks_ref,
    gains_ref,
    tanh_ref,
    raw_ref,
    mixed_ref,
    cross_ref,
):
    step = pl.program_id(0)

    @pl.when(step < half)
    def _():
        raw_ref[...] = dot10(first_ref[...], weight_ref[...])

    @pl.when(step >= half)
    def _():
        raw_ref[...] = dot10(second_ref[...], weight_ref[...])

    state = row_state(
        qkv_ref[...], raw_ref[...], cos_ref[...], sin_ref[...], marks_ref[0], gains_ref[...], heads, size
    )
    scaling = 1.0 / math.sqrt(size)
    mixed = []
    for head in range(heads):
        queries = state["queries"][head]
        scores = dot00(state["keys"][head], queries) * scaling
        weights = softmax0(jnp.where(state["same"], scores, NEGATIVE)).astype(BF16)
        self_out = dot10(state["values"][head], weights)
        scores = dot00(state["cap_keys"][head], queries) * scaling
        weights = softmax0(jnp.where(state["in_use"], scores, NEGATIVE)).astype(BF16)
        cross_out = dot10(state["cap_values"][head], weights)
        cross_ref[head * size : (head + 1) * size, :] = cross_out
        mixed.append(self_out + tanh_ref[head] * cross_out)
    mixed_ref[...] = jnp.concatenate(mixed, axis=0).T.astype(BF16)


def backward_kernel(
    heads,
    size,
    qkv_ref,
    cap_ref,
    cos_ref,
    sin_ref,
    marks_ref,
    gains_ref,
    tanh_ref,
    cross_ref,
    grad_ref,
    turned_ref,
    plain_ref,
    cap_grad_ref,
    gain_grad_ref,
    gate_grad_ref,
):
    step = pl.program_id(0)
    cap = cap_ref[...]
    crossed = cross_ref[...]
    gains = gains_ref[...]
    cos_table, sin_table = cos_ref[...], sin_ref[...]
    state = row_state(qkv_ref[...], cap, cos_table, sin_table, marks_ref[0], gains, heads, size)
    scaling = 1.0 / math.sqrt(size)
    across = heads * size
    grad_q, grad_k, grad_cap_k, gate = [], [], [], []
    for head in range(heads):
        span = slice(head * size, (head + 1) * size)
        queries, keys, values = (state[name][head] for name in ("queries", "keys", "values"))
        cap_keys, cap_values = state["cap_keys"][head], state["cap_values"][head]
        grad_out = grad_ref[span, :]
        grad_float = grad_out.astype(F32)
        gate.append(jnp.sum(grad_float * crossed[span], axis=0, keepdims=True))
        grad_cross = (tanh_ref[head] * grad_float).astype(BF16)

        def back(weights, grad_output, held):
            grad_weights = dot00(held, grad_output)
            centre = jnp.sum(grad_weights * weights, axis=0, keepdims=True)
            return (weights * (grad_weights - centre)).astype(BF16)

        scores = dot00(keys, queries) * scaling
        weights = softmax0(jnp.where(state["same"], scores, NEGATIVE))
        grad_scores = back(weights, grad_out, values)
        grad_value = dot11(grad_out, weights.astype(BF16))
        at = 2 * across + head * size
        turned_ref[at : at + size, :] = grad_value.astype(BF16)
        grad_query = dot10(keys, grad_scores)
        grad_k.append(dot11(queries, grad_scores) * scaling)

        scores = dot00(cap_keys, queries) * scaling
        weights = softmax0(jnp.where(state["in_use"], scores, NEGATIVE))
        grad_scores = back(weights, grad_cross, cap_values)
        grad_cap_value = dot11(grad_cross, weights.astype(BF16))
        cap_grad_ref[across + head * size : across + (head + 1) * size, :] = grad_cap_value.astype(
            BF16
        )
        grad_q.append((grad_query + dot10(cap_keys, grad_scores)) * scaling)
        grad_cap_k.append(dot11(queries, grad_scores) * scaling)

    def stacked(parts):
        return jnp.concatenate(parts, axis=0).reshape(heads, size, -1)

    def unrotate(incoming):
        return incoming * cos_table - quarter_turn(incoming * sin_table)

    normed = state["norms"]
    grad_q, grad_k = unrotate(stacked(grad_q)), unrotate(stacked(grad_k))
    grad_cap_k = stacked(grad_cap_k)
    turned_ref[0:across, :] = (
        head_norm_back(grad_q, normed[0], normed[1], gains[0]).reshape(across, -1).astype(BF16)
    )
    turned_ref[across : 2 * across, :] = (
        head_norm_back(grad_k, normed[2], normed[3], gains[1]).reshape(across, -1).astype(BF16)
    )
    cap_grad_ref[0:across, :] = (
        head_norm_back(grad_cap_k, normed[4], normed[5], gains[2][:, :1])
        .reshape(across, -1)
        .astype(BF16)
    )
    plain_ref[...] = turned_ref[...].astype(F32).T.astype(BF16)
    tokens = grad_q.shape[-1]
    cap_part = jnp.sum(grad_cap_k * normed[4], axis=0)
    gain_part = jnp.stack(
        [
            jnp.sum(grad_q * normed[0], axis=0),
            jnp.sum(grad_k * normed[2], axis=0),
            sum(cap_part[:, i : i + tokens] for i in range(0, cap_part.shape[1], tokens)),
        ]
    )
    gate_part = jnp.stack(gate)

    @pl.when(step == 0)
    def _():
        gain_grad_ref[...] = gain_part
        gate_grad_ref[...] = gate_part

    @pl.when(step > 0)
    def _():
        gain_grad_ref[...] += gain_part
        gate_grad_ref[...] += gate_part


def row_specs(row_of, sizes, across):
    size, tokens, cap_tokens = sizes
    return [
        pl.BlockSpec((tokens, 3 * across), lambda i: (row_of(i), 0)),
        pl.BlockSpec((cap_tokens, 2 * across), lambda i: (i, 0)),
        pl.BlockSpec((size, tokens), lambda i: (0, row_of(i))),
        pl.BlockSpec((size, tokens), lambda i: (0, row_of(i))),
        pl.BlockSpec((1, 8, tokens), lambda i: (row_of(i), 0, 0)),
    ]


def whole(shape):
    return pl.BlockSpec(shape, lambda i: (0,) * len(shape))


def attend(row_of, heads, sizes, qkv, caps, weight, cos_table, sin_table, marks, gains, tanh):
    size, tokens, cap_tokens = sizes
    half = caps[0].shape[0] // cap_tokens
    rows = 2 * half
    across = heads * size
    width = caps[0].shape[1]
    specs = row_specs(row_of, sizes, across)
    return pl.pallas_call(
        functools.partial(forward_kernel, heads, size, half),
        grid=(rows,),
        in_specs=[
            specs[0],
            pl.BlockSpec((cap_tokens, width), lambda i: (jnp.minimum(i, half - 1), 0)),
            pl.BlockSpec((cap_tokens, width), lambda i: (jnp.maximum(i - half, 0), 0)),
            whole(weight.shape),
            *specs[2:],
            whole(gains.shape),
            whole(tanh.shape),
        ],
        out_specs=[
            pl.BlockSpec((cap_tokens, 2 * across), lambda i: (i, 0)),
            pl.BlockSpec((tokens, across), lambda i: (i, 0)),
            pl.BlockSpec((across, tokens), lambda i: (0, i)),
        ],
        out_shape=[
            jax.ShapeDtypeStruct((rows * cap_tokens, 2 * across), F32),
            jax.ShapeDtypeStruct((rows * tokens, across), BF16),
            jax.ShapeDtypeStruct((across, rows * tokens), F32),
        ],
        compiler_params=pltpu.CompilerParams(vmem_limit_bytes=34 * 1024 * 1024),
        cost_estimate=SMALL_COST,
    )(qkv, caps[0], caps[1], weight, cos_table, sin_table, marks, gains, tanh)


def attend_back(row_of, first, heads, sizes, qkv, cap, cos_table, sin_table, marks, gains, tanh, crossed, grad):
    size, tokens, cap_tokens = sizes
    rows = cap.shape[0] // cap_tokens
    across = heads * size
    out_shape = [
        jax.ShapeDtypeStruct((3 * across, rows * tokens), BF16),
        jax.ShapeDtypeStruct((rows * tokens, 3 * across), BF16),
        jax.ShapeDtypeStruct((2 * across, rows * cap_tokens), BF16),
        jax.ShapeDtypeStruct((3, size, tokens), F32),
        jax.ShapeDtypeStruct((heads, 1, tokens), F32),
    ]
    return pl.pallas_call(
        functools.partial(backward_kernel, heads, size),
        grid=(rows,),
        in_specs=row_specs(row_of, sizes, across)
        + [
            whole(gains.shape),
            whole(tanh.shape),
            pl.BlockSpec((across, tokens), lambda i: (0, i)),
            pl.BlockSpec((across, tokens), lambda i: (0, row_of(i) - first)),
        ],
        out_specs=[
            pl.BlockSpec((3 * across, tokens), lambda i: (0, row_of(i) - first)),
            pl.BlockSpec((tokens, 3 * across), lambda i: (row_of(i) - first, 0)),
            pl.BlockSpec((2 * across, cap_tokens), lambda i: (0, i)),
            whole(out_shape[3].shape),
            whole(out_shape[4].shape),
        ],
        out_shape=out_shape,
        compiler_params=pltpu.CompilerParams(vmem_limit_bytes=24 * 1024 * 1024),
        cost_estimate=SMALL_COST,
    )(qkv, cap, cos_table, sin_table, marks, gains, tanh, crossed, grad)


def outer_kernel(counts, place_ref, *refs):
    lefts, rights = refs[: len(counts)], refs[len(counts) : -1]
    total, at = None, 0
    for left, count in zip(lefts, counts):
        begin = 0
        for right in rights[at : at + count]:
            end = begin + right.shape[0]
            part = dot10(left[:, begin:end], right[...])
            total = part if total is None else total + part
            begin = end
        at += count
    refs[-1][...] = total.astype(BF16)


def outer(lefts, rights, left_index, left_blocks, column_blocks, width):
    counts = tuple(len(group) for group in rights)
    flat = [piece for group in rights for piece in group]
    rows = lefts[0].shape[0] // left_blocks
    count = len(column_blocks)
    index = jnp.stack([left_index] + list(column_blocks)).astype(jnp.int32)
    tokens = sum(left.shape[1] for left in lefts)
    return pl.pallas_call(
        functools.partial(outer_kernel, counts),
        grid_spec=pltpu.PrefetchScalarGridSpec(
            num_scalar_prefetch=1,
            grid=(count,),
            in_specs=[
                pl.BlockSpec((rows, left.shape[1]), lambda i, place: (place[0], 0)) for left in lefts
            ]
            + [pl.BlockSpec((right.shape[0], width), lambda i, place: (0, place[1 + i])) for right in flat],
            out_specs=pl.BlockSpec((rows, width), lambda i, place: (0, i)),
        ),
        out_shape=jax.ShapeDtypeStruct((rows, count * width), BF16),
        compiler_params=pltpu.CompilerParams(vmem_limit_bytes=26 * 1024 * 1024),
        cost_estimate=SMALL_COST,
    )(index, *lefts, *flat)


def middle_kernel(inner, ffn_ref, gate_ref, up_ref, branch_ref, down_ref, act_ref, grad_ref):
    block = gate_ref.shape[1]
    grad_act = dot11(branch_ref[...], down_ref[...])
    gate = dot10(ffn_ref[...], gate_ref[...])
    up = dot10(ffn_ref[...], up_ref[...])
    sigmoid = 1.0 / (1.0 + jnp.exp(-gate))
    silu = gate * sigmoid
    at = pl.multiple_of(pl.program_id(0) * block, 128)
    act_ref[...] = (silu * up).astype(BF16)
    grad_ref[:, pl.ds(at, block)] = (grad_act * up * sigmoid * (1.0 + gate * (1.0 - sigmoid))).astype(BF16)
    grad_ref[:, pl.ds(at + inner, block)] = (grad_act * silu).astype(BF16)


def middle(ffn_in, w_ffn, grad_branch, w_down):
    tokens, width = ffn_in.shape
    inner = w_down.shape[0]
    block = 256
    steps = inner // block

    def whole(shape):
        return pl.BlockSpec(shape, lambda i: (0,) * len(shape))

    return pl.pallas_call(
        functools.partial(middle_kernel, inner),
        grid=(steps,),
        in_specs=[
            whole((tokens, width)),
            pl.BlockSpec((width, block), lambda i: (0, i)),
            pl.BlockSpec((width, block), lambda i: (0, i + steps)),
            whole((tokens, width)),
            pl.BlockSpec((block, width), lambda i: (i, 0)),
        ],
        out_specs=[
            pl.BlockSpec((tokens, block), lambda i: (0, i)),
            whole((tokens, 2 * inner)),
        ],
        out_shape=[
            jax.ShapeDtypeStruct((tokens, inner), BF16),
            jax.ShapeDtypeStruct((tokens, 2 * inner), BF16),
        ],
        compiler_params=pltpu.CompilerParams(vmem_limit_bytes=52 * 1024 * 1024),
        cost_estimate=SMALL_COST,
    )(ffn_in, w_ffn, w_ffn, grad_branch, w_down)


def outer_tokens_kernel(count, place_ref, *refs):
    total = None
    for left, right in zip(refs[:count], refs[count:-1]):
        part = dot00(left[...], right[...])
        total = part if total is None else total + part
    refs[-1][...] = total.astype(BF16)


def rows_kernel(*refs):
    *pieces, out_ref = refs
    at = 0
    for group in range(0, len(pieces), 4):
        near, far, near_right, far_right = pieces[group : group + 4]
        total = dot00(near[...], near_right[...]) + dot00(far[...], far_right[...])
        end = at + near_right.shape[1]
        out_ref[:, at:end] = total.astype(BF16)
        at = end


def outer_rows(*groups):
    block = 256
    columns = sum(group[2].shape[1] for group in groups)
    width = groups[0][0].shape[1]
    specs = []
    for near, far, near_right, far_right in groups:
        specs += [pl.BlockSpec((left.shape[0], block), lambda i: (0, i)) for left in (near, far)]
        specs += [pl.BlockSpec(right.shape, lambda i: (0, 0)) for right in (near_right, far_right)]
    return pl.pallas_call(
        rows_kernel,
        grid=(width // block,),
        in_specs=specs,
        out_specs=pl.BlockSpec((block, columns), lambda i: (i, 0)),
        out_shape=jax.ShapeDtypeStruct((width, columns), BF16),
        compiler_params=pltpu.CompilerParams(vmem_limit_bytes=18 * 1024 * 1024),
        cost_estimate=SMALL_COST,
    )(*[piece for group in groups for piece in group])


def outer_tokens(lefts, rights, left_block, blocks, right_block, right_blocks):
    block = 256
    columns = rights[0].shape[1] // right_blocks
    index = jnp.stack([jnp.asarray(left_block), jnp.asarray(right_block)]).astype(jnp.int32)
    return pl.pallas_call(
        functools.partial(outer_tokens_kernel, len(lefts)),
        grid_spec=pltpu.PrefetchScalarGridSpec(
            num_scalar_prefetch=1,
            grid=(blocks,),
            in_specs=[
                pl.BlockSpec((left.shape[0], block), lambda i, place: (0, place[0] + i)) for left in lefts
            ]
            + [
                pl.BlockSpec((right.shape[0], columns), lambda i, place: (0, place[1]))
                for right in rights
            ],
            out_specs=pl.BlockSpec((block, columns), lambda i, place: (i, 0)),
        ),
        out_shape=jax.ShapeDtypeStruct((blocks * block, columns), BF16),
        compiler_params=pltpu.CompilerParams(vmem_limit_bytes=18 * 1024 * 1024),
        cost_estimate=SMALL_COST,
    )(index, *lefts, *rights)


def join_kernel(widths, rows, chunks, place_ref, *refs):
    shards = refs[: len(widths)]
    near = refs[len(widths)]
    pieces = refs[len(widths) + 1 : len(widths) + 1 + 2 * chunks]
    out, sems = refs[-2:]
    copies = []

    def copy(source, row, count, column, width):
        target = out.at[pl.ds(pl.multiple_of(row, 16), count), pl.ds(column, width)]
        copies.append(pltpu.make_async_copy(source, target, sems.at[len(copies)]))
        copies[-1].start()

    at = 0
    for shard, width in zip(shards, widths):
        begin = pl.multiple_of(place_ref[4] * width, 128)
        copy(shard.at[:, pl.ds(begin, width)], place_ref[0] * rows, rows, at, width)
        at += width
    copy(near, place_ref[1] * rows, rows, 0, at)
    part = rows // chunks
    for chunk in range(chunks):
        for kind in range(2):
            row = place_ref[2 + kind] * rows + chunk * part
            copy(pieces[2 * chunk + kind], row, part, 0, at)
    for item in copies:
        item.wait()


def join(place_index, shards, near, pieces):
    widths = tuple(shard.shape[1] // 4 for shard in shards)
    rows = near.shape[0]
    chunks = len(pieces) // 2
    count = len(shards) + 1 + len(pieces)
    return pl.pallas_call(
        functools.partial(join_kernel, widths, rows, chunks),
        grid_spec=pltpu.PrefetchScalarGridSpec(
            num_scalar_prefetch=1,
            grid=(1,),
            in_specs=[pl.BlockSpec(memory_space=pl.ANY)] * count,
            out_specs=pl.BlockSpec((4 * rows, sum(widths)), lambda i, place: (0, 0)),
            scratch_shapes=[pltpu.SemaphoreType.DMA((count,))],
        ),
        out_shape=jax.ShapeDtypeStruct((4 * rows, sum(widths)), near.dtype),
        compiler_params=pltpu.CompilerParams(vmem_limit_bytes=50 * 1024 * 1024),
        cost_estimate=SMALL_COST,
    )(place_index, *shards, near, *pieces)


class Flow:
    def __init__(self, steps):
        self.steps = steps
        self.result = None
        self.waiting = next(steps)

    def step(self, values):
        if self.result is not None:
            return
        try:
            self.waiting = self.steps.send(values)
        except StopIteration as stop:
            self.waiting, self.result = (), stop.value


class Place:
    def __init__(self, mesh):
        self.copies = mesh.shape["dp"]
        self.shards = mesh.shape["fsdp"]
        self.top_step = self.copies // 2
        self.team_step = self.copies // 4
        self.low = self.copies // 4
        self.last = {}
        self.before, self.token = (), ()

    def locate(self):
        self.dp = lax.axis_index("dp")
        self.fsdp = lax.axis_index("fsdp")
        self.side = self.fsdp // 2
        self.core = self.fsdp % 2
        self.top = self.dp // self.top_step
        self.team = (self.dp // self.team_step) % 2
        self.lane = self.dp % 2
        self.quarter = 2 * self.core + self.team

    def swap(self, value, dp=0, fsdp=0, link=None):
        return self.route(value, lambda d, f: (d ^ dp, f ^ fsdp), link)

    def route(self, value, target, link=None):
        pairs = []
        for d in range(self.copies):
            for f in range(self.shards):
                to = target(d, f)
                if to is not None:
                    pairs.append((d * self.shards + f, to[0] * self.shards + to[1]))
        value = after(value, *self.before, *self.last.get(link, ()))
        self.operand = value
        value = lax.ppermute(value, ("dp", "fsdp"), pairs)
        if link is not None:
            self.last[link] = (value,)
        return value

    def next_wave(self, *others):
        self.before = others

    def arrive(self, *values):
        values = lax.optimization_barrier(values)
        self.before = values
        return values

    def meet(self, flows, *values):
        waiting = [array for flow in flows for array in flow.waiting]
        arrived = self.arrive(*waiting, *values)
        self.done(*(arrived[len(waiting) :] or arrived[:1]))
        at = 0
        for flow in flows:
            count = len(flow.waiting)
            flow.step(arrived[at : at + count])
            at += count
        return arrived[at:]

    def held(self, value):
        if isinstance(value, tuple):
            return tuple(self.held(part) for part in value)
        return after(value, *self.token)

    def done(self, *values):
        self.token = values

    def bits(self, d, f):
        return ((d // self.team_step) % 2, f // 2, f % 2, d % 2)

    def team_swap(self, value):
        return self.swap(value, dp=self.team_step, link="z")

    def core_swap(self, value):
        return self.swap(value, fsdp=1, link="c")


    def cut_columns(self, shards):
        def cut(quarter):
            parts = []
            for shard in shards:
                width = shard.shape[1] // 4
                parts.append(lax.dynamic_slice_in_dim(shard, quarter * width, width, axis=1))
            return jnp.concatenate(parts, axis=1)

        return cut(2 * (self.core ^ self.lane) + self.team), cut(2 * (1 - self.core) + self.team)

    def side_swap(self, piece):
        return self.route(piece, lambda d, f: (d, f ^ 2 ^ (d % 2)), "x")

    def lane_swap(self, piece):
        return self.swap(piece, dp=1, link="y")

    def join_columns(self, shards, near, pieces):
        index = [self.fsdp, self.fsdp ^ 1, self.fsdp ^ 2 ^ self.lane, self.fsdp ^ 3 ^ self.lane]
        return join(jnp.stack(index + [self.quarter]).astype(jnp.int32), shards, near, pieces)

    def rows_side_swap(self, shard):
        def target(d, f):
            team, side, core, _ = self.bits(d, f)
            return (d, 2 * (1 - side) + side) if core == team else None

        return self.route(shard, target, "x")

    def rows_lane_swap(self, piece):
        def target(d, f):
            _, side, core, _ = self.bits(d, f)
            return (d ^ 1, f) if core != side else None

        return self.route(piece, target, "y")

    def rows_core_swap(self, shard):
        def target(d, f):
            team, side, core, _ = self.bits(d, f)
            return (d, 2 * side + side) if core == team and side != team else None

        return self.route(shard, target, "c")

    def join_rows(self, shard, near, across, far):
        source = jnp.where(
            self.core != self.side, 2, jnp.where(self.side == self.team, 0, 1)
        )
        return join_rows(jnp.stack([source, self.lane]).astype(jnp.int32), shard, near, across, far)


    def part(self, value, index, axis):
        if isinstance(value, tuple):
            return tuple(self.part(array, index, axis) for array in value)
        size = value.shape[axis] // 2
        return lax.dynamic_slice_in_dim(value, index * size, size, axis=axis)

    def summed(self, arrays):
        return sum(array.astype(F32) for array in arrays).astype(BF16)

    def halves(self, value, axis, keep):
        sent = self.summed([self.part(array, 1 - keep, axis) for array in value])
        return sent, [self.part(array, keep, axis) for array in value]

    def low_steps(self):
        step = self.low // 2
        while step:
            yield step, (self.dp // step) % 2
            step //= 2

    def spread(self, first, second, place, chunks=1, ahead=False, hold=False):
        (step, keep), *lows = self.low_steps()
        side, low, kept = [], [], ()
        sents = [(first[0](1 - place, i), second[0](1 - keep, i)) for i in range(chunks)]
        if chunks > 1:
            kept = tuple(first[1](place, i) for i in range(chunks))
            kept += tuple(second[1](keep, i) for i in range(chunks))
        if ahead:
            sents = [(yield sents[0])]
        if ahead == 2:
            kept = first[1](place, 0), second[1](keep, 0)
            arrived = yield tuple(sents[0]) + kept
            sents, kept = [arrived[:2]], arrived[2:]
        for chunk in range(chunks):
            first_got = self.swap(sents[chunk][0], fsdp=2)
            operands = (self.operand,)
            second_got = self.swap(sents[chunk][1], dp=step)
            self.operands = operands + (self.operand,)
            rest = tuple(part for pair in sents[chunk + 1 :] for part in pair)
            if not kept:
                yield first_got, second_got
                kept = first[1](place, 0), second[1](keep, 0)
            arrived = yield (first_got, second_got) + kept + rest
            side.append(arrived[0])
            low.append(arrived[1])
            kept, rest = arrived[2 : 2 + len(kept)], arrived[2 + len(kept) :]
            sents[chunk + 1 :] = [rest[i : i + 2] for i in range(0, len(rest), 2)]

        def joined(parts):
            return parts[0] if chunks == 1 else jnp.concatenate(parts, axis=0)

        if chunks == 2 and not lows:
            pairs = (kept[:chunks], side)
            sent_first = self.summed([jnp.where(keep == 0, pair[1], pair[0]) for pair in pairs])
            first = [jnp.where(keep == 0, pair[0], pair[1]) for pair in pairs]
        else:
            sent_first, first = self.halves([joined(kept[:chunks]), joined(side)], 0, keep)
        second = [joined(kept[chunks:]), joined(low)]
        sent_second, second = self.halves(second, 1, place)
        if hold:
            sent_first, sent_second = yield sent_first, sent_second
        got = yield self.swap(sent_first, dp=step), self.swap(sent_second, fsdp=2)
        first.append(got[0])
        second.append(got[1])
        for step, keep in lows:
            sent_first, first = self.halves(first, 0, keep)
            sent_second, second = self.halves(second, 0, keep)
            first.append(self.swap(sent_first, dp=step))
            second.append(self.swap(sent_second, dp=step))
        return first, second

    def finish(self, own, sent, parts, apart=False):
        got = self.core_swap(sent)
        if apart:
            (got,) = yield (got,)
        straight = self.core == self.top
        sent = jnp.split(jnp.where(straight, got, own), parts, axis=0)
        kept = jnp.split(jnp.where(straight, own, got), parts, axis=0)
        totals = []
        for part in range(parts):
            (got,) = yield (self.swap(sent[part], dp=self.top_step),)
            totals.append(kept[part].astype(F32) + got.astype(F32))
        return totals

    def pair_back(self, by_side, by_low):
        first, second = yield from self.spread((by_side, by_side), (by_low, by_low), self.side, 2)

        def both(index):
            return jnp.concatenate(
                [self.summed([self.part(array, index, 1) for array in value]) for value in (first, second)]
            )

        (value,) = yield from self.finish(both(self.core), both(1 - self.core), 1, True)
        return [part.T for part in jnp.split(value, 2, axis=0)]

    def split_back(self, by_side, by_low, count, parts, ahead=False):
        yield ()
        first, second = yield from self.spread(
            (by_side, by_side), (by_low, by_low), self.side, 1, ahead
        )
        first, second = self.summed(first), self.summed(second)
        own = jnp.where(self.core == 0, first, second)
        sent = jnp.where(self.core == 0, second, first)
        value = yield from self.finish(own, sent, parts)
        return [part.T for total in value for part in jnp.split(total, count // parts, axis=0)]

    def rows_back(self, grad, hold=False):
        columns, rows = grad.shape
        value = grad.reshape(2, 2, columns // 4, rows)
        own = lax.dynamic_index_in_dim(value, self.core, 1, keepdims=False)
        sent = lax.dynamic_index_in_dim(value, 1 - self.core, 1, keepdims=False)
        got = self.core_swap(sent)
        straight = self.core == self.side
        kept = jnp.where(straight, own, got)
        sent = jnp.where(straight, got, own)
        wide = jnp.concatenate([kept[1], sent[1]], axis=1)
        pieces = sent[0], kept[0]
        *pieces, wide = yield (*pieces, wide)

        def by_low(index, _):
            return self.part(wide, index, 0)

        first, second = yield from self.spread(
            (lambda *_: pieces[0], lambda *_: pieces[1]), (by_low, by_low), 0, hold=hold
        )
        first, second = self.summed(first), self.summed(second)
        sent = jnp.where(self.top == 0, second, first)
        (got,) = yield (self.swap(sent, dp=self.top_step),)
        value = self.summed([jnp.where(self.top == 0, first, second), got])

        def turn(d, f):
            team, _, core, _ = self.bits(d, f)
            return (d ^ self.team_step, f ^ 1) if core != team else (d, f)

        (got,) = yield (self.route(value, turn),)
        return got.astype(F32).T

    def total(self, value, axis, steps):
        for step in steps:
            value = value + self.swap(value, **{axis: step})
        return value


def layer(
    place,
    block_input,
    caption,
    modulation,
    segment_ids,
    pos_row,
    pos_col,
    caption_len,
    gain_attn,
    w_query,
    w_key,
    w_value,
    gain_query,
    gain_key,
    w_cap_key,
    w_cap_value,
    gain_cap_key,
    head_gate,
    w_out,
    gain_ffn,
    w_gate,
    w_up,
    w_down,
    cotangent,
):
    place.locate()
    rows, tokens, width = block_input.shape
    cap_tokens = caption.shape[1]
    size = gain_query.shape[0] * place.shards
    team_rows = 4 * rows

    qkv_shards, cap_shards, ffn_shards = (w_query, w_key, w_value), (w_cap_key, w_cap_value), (w_gate, w_up)
    qkv_sent, qkv_near = place.cut_columns(qkv_shards)
    qkv_side = place.side_swap(qkv_sent)
    later = after(caption, qkv_sent)
    cap_pieces = [caption[0, : cap_tokens // 2], later[0, cap_tokens // 2 :]]
    cap_pieces += [later[1, : cap_tokens // 2], later[1, cap_tokens // 2 :]]
    far_pieces = [place.team_swap(cap_pieces[0])]

    small = (gain_attn, gain_ffn, gain_query, gain_key, gain_cap_key, head_gate)
    piece = after(jnp.concatenate(small), qkv_sent)
    pair = jnp.stack([piece, place.core_swap(piece)])
    other = place.swap(pair, fsdp=2)
    packed = jnp.zeros((place.shards,) + piece.shape, piece.dtype)
    for part, index in ((pair[0], 0), (pair[1], 1), (other[0], 2), (other[1], 3)):
        packed = lax.dynamic_update_index_in_dim(packed, part, place.fsdp ^ index, 0)
    packed = packed.astype(F32)
    full_small, at = [], 0
    for vector in small:
        full_small.append(packed[:, at : at + vector.shape[0]].reshape(-1))
        at += vector.shape[0]
    full_gain_attn, full_gain_ffn, query_gain, key_gain, cap_gain, full_head_gate = full_small
    heads = full_head_gate.shape[0] // 4
    across = heads * size
    sizes = (size, tokens, cap_tokens)

    cap_own = caption.reshape(-1, caption.shape[-1])
    cap_core = place.core_swap(cap_own)
    cap_sent, cap_w_near = place.cut_columns(cap_shards)
    cap_sent = jnp.split(cap_sent, 2, axis=0)
    ffn_sent, ffn_w_near = place.cut_columns(ffn_shards)
    ffn_sent = jnp.split(ffn_sent, 2, axis=0)
    half_out, half_down = w_out.shape[0] // 2, w_down.shape[0] // 2
    rows_sent = jnp.concatenate(
        [place.part(w_out, place.lane, 0), place.part(w_down, place.lane, 0)], axis=0
    )

    inputs = block_input.astype(F32)
    scale_attn = 1.0 + modulation[:, 0][:, None, :]
    tanh_attn = jnp.tanh(modulation[:, 1])[:, None, :]
    scale_ffn = 1.0 + modulation[:, 2][:, None, :]
    tanh_ffn = jnp.tanh(modulation[:, 3])[:, None, :]
    upstream = cotangent.astype(F32)
    grad_branch = (upstream * tanh_ffn).astype(BF16).reshape(-1, width)
    normed_in, inverse_in = rms_scale(inputs)
    attn_in = (normed_in * full_gain_attn * scale_attn).astype(BF16).reshape(-1, width)

    own_tokens = rows * tokens
    marks = jnp.stack(
        [segment_ids, pos_row, pos_col, jnp.broadcast_to(caption_len[:, None], (rows, tokens))]
    )
    marks = marks.astype(BF16).reshape(4, own_tokens)
    marks = jnp.pad(marks, ((0, 12), (0, width - own_tokens)))
    marked = jnp.concatenate([attn_in, marks], axis=0)

    qkv_side, far_piece = place.arrive(qkv_side, far_pieces[0])
    far_pieces = [far_piece]
    cap_side = place.side_swap(cap_sent[0])
    qkv_lane = place.lane_swap(qkv_side)
    marked_far = place.team_swap(marked)
    place.before = ()
    qkv_near = place.core_swap(qkv_near)
    marked_near = place.core_swap(marked)

    cap_side, qkv_lane, marked_far = place.arrive(cap_side, qkv_lane, marked_far)
    cap_pairs = [cap_side]
    next_side = place.side_swap(cap_sent[1])
    cap_lane = place.lane_swap(cap_side)
    far_piece = place.team_swap(cap_pieces[1])
    place.before = ()
    marked_last = place.core_swap(marked_far)
    cap_w_near = place.core_swap(cap_w_near)
    blocks = (marked, marked_near, marked_far, marked_last)
    attn_all = jnp.concatenate([block[:own_tokens] for block in blocks], axis=0)
    marks = jnp.concatenate([block[own_tokens:, :own_tokens] for block in blocks], axis=1).astype(F32)
    w_qkv = place.join_columns(qkv_shards, qkv_near, [qkv_side, qkv_lane])

    next_side, cap_lane, far_piece, attn_all, w_qkv = place.arrive(
        next_side, cap_lane, far_piece, attn_all, w_qkv
    )
    cap_pairs += [cap_lane, next_side]
    far_pieces.append(far_piece)
    rows_side = place.rows_side_swap(rows_sent)
    cap_lane = place.lane_swap(next_side)
    far_piece = place.team_swap(cap_pieces[2])
    place.before = ()
    far_first = jnp.concatenate(far_pieces, axis=0)
    far_first_core = place.core_swap(far_first)
    ffn_w_near = place.core_swap(ffn_w_near)
    qkv_raw = dot(attn_all, w_qkv)

    quarter_size = size // 4
    frequency = jnp.exp(
        jnp.arange(quarter_size, dtype=F32) * (-math.log(10000.0) / quarter_size)
    )
    row_angle = frequency[:, None] * marks[1][None, :]
    col_angle = frequency[:, None] * marks[2][None, :]
    angles = jnp.concatenate([row_angle, row_angle, col_angle, col_angle], axis=0)
    cos_table, sin_table = jnp.cos(angles), jnp.sin(angles)
    marks = jnp.stack([marks[0], marks[3]]).reshape(2, team_rows, tokens)
    marks = jnp.pad(jnp.moveaxis(marks, 0, 1), ((0, 0), (0, 6), (0, 0)))
    gains = jnp.broadcast_to(
        jnp.stack([query_gain, key_gain, cap_gain])[:, :, None], (3, size, tokens)
    )
    head_tanh = jnp.tanh(lax.dynamic_slice_in_dim(full_head_gate, place.quarter * heads, heads))
    tanh_table = jnp.broadcast_to(head_tanh[:, None, None], (heads, 1, tokens))
    tables = (cos_table, sin_table, marks, gains, tanh_table)
    half = team_rows // 2

    def far_row(i):
        return half + (i % rows) * rows + i // rows

    def rows_from(first):
        return lambda i: first + i

    rows_side, cap_lane, far_piece, qkv_raw, cos_table = place.arrive(
        rows_side, cap_lane, far_piece, qkv_raw, cos_table
    )
    tables = (cos_table,) + tables[1:]
    cap_pairs.append(cap_lane)
    far_pieces = [far_piece]
    ffn_side = place.side_swap(ffn_sent[0])
    rows_lane = place.rows_lane_swap(rows_side)
    far_piece = place.team_swap(cap_pieces[3])
    w_cap = place.join_columns(cap_shards, cap_w_near, cap_pairs)
    out_near = place.rows_core_swap(w_out)
    branch_core = place.core_swap(grad_branch)
    place.before = ()
    near_raw, mixed_near, near_crossed = attend(
        rows_from(0), heads, sizes, qkv_raw, (cap_own, cap_core), w_cap, *tables
    )

    ffn_side, rows_lane, far_piece, mixed_near = place.arrive(ffn_side, rows_lane, far_piece, mixed_near)
    ffn_pairs = [ffn_side]
    far_pieces.append(far_piece)
    next_side = place.side_swap(ffn_sent[1])
    ffn_lane = place.lane_swap(ffn_side)
    branch_far = place.team_swap(grad_branch)
    place.before = ()
    far_second = jnp.concatenate(far_pieces, axis=0)
    far_second_core = place.core_swap(far_second)
    down_near = place.rows_core_swap(w_down)
    w_out = place.join_rows(w_out, out_near, rows_side[:half_out], rows_lane[:half_out])
    first_raw, mixed_first, first_crossed = attend(
        lambda i: half + i * rows, heads, sizes, qkv_raw, (far_first, far_first_core), w_cap, *tables
    )
    second_raw, mixed_second, second_crossed = attend(
        lambda i: half + 1 + i * rows,
        heads,
        sizes,
        qkv_raw,
        (far_second, far_second_core),
        w_cap,
        *tables,
    )
    next_side, ffn_lane, branch_far, mixed_second = place.arrive(
        next_side, ffn_lane, branch_far, mixed_second
    )
    ffn_pairs += [ffn_lane, next_side]
    place.before = ()
    place.done(mixed_second)
    far_raw = jnp.concatenate([first_raw, second_raw], axis=0)
    far_crossed = jnp.concatenate([first_crossed, second_crossed], axis=1)
    mixed_blocks = (
        *jnp.split(mixed_near, 2, axis=0),
        jnp.concatenate([mixed_first[:tokens], mixed_second[:tokens]], axis=0),
        jnp.concatenate([mixed_first[tokens:], mixed_second[tokens:]], axis=0),
    )
    def far_sum(blocks, right, product):
        last = place.core_swap(product(place.held(blocks[3]), right).astype(BF16))
        far = product(place.held(blocks[2]), right) + last.astype(F32)
        return place.team_swap(far.astype(BF16))

    def near_sum(blocks, right, product):
        got = place.core_swap(product(place.held(blocks[1]), right).astype(BF16))
        return product(place.held(blocks[0]), right) + got.astype(F32)

    attn_far_sum = far_sum(mixed_blocks, w_out, dot)
    ffn_pairs.append(place.lane_swap(next_side))
    w_down = place.join_rows(w_down, down_near, rows_side[half_out:], rows_lane[half_out:])
    branch_near = jnp.concatenate([grad_branch, branch_core], axis=0)
    branch_far = jnp.concatenate([branch_far, place.core_swap(branch_far)], axis=0)
    w_ffn = place.join_columns(ffn_shards, ffn_w_near, ffn_pairs)
    attn_near_sum = near_sum(mixed_blocks, w_out, dot)
    attn_far_sum, attn_near_sum, w_ffn, w_down = place.arrive(
        attn_far_sum, attn_near_sum, w_ffn, w_down
    )
    place.before = ()
    attn_branch = (attn_near_sum + attn_far_sum.astype(F32)).reshape(inputs.shape)
    hidden = inputs + tanh_attn * attn_branch

    normed_mid, inverse_mid = rms_scale(hidden)
    ffn_in = (normed_mid * full_gain_ffn * scale_ffn).astype(BF16).reshape(-1, width)

    ffn_far = place.team_swap(ffn_in)
    ffn_near = jnp.concatenate([ffn_in, place.core_swap(ffn_in)], axis=0)
    act_near, grad_near = middle(ffn_near, w_ffn, branch_near, w_down)
    place.done(act_near, grad_near)
    ffn_far = place.held(ffn_far)
    ffn_far = jnp.concatenate([ffn_far, place.core_swap(ffn_far)], axis=0)
    act_far, grad_far = middle(ffn_far, w_ffn, branch_far, w_down)
    place.done(act_far, grad_far)
    grad_blocks = (*jnp.split(grad_near, 2, axis=0), *jnp.split(grad_far, 2, axis=0))
    act_blocks = (*jnp.split(act_near, 2, axis=0), *jnp.split(act_far, 2, axis=0))
    blocks = act_near.shape[1] // 256

    def gate_by_side(side, chunk):
        lefts = place.held((grad_near, grad_far))
        each = blocks // 2
        return outer_tokens(lefts, (ffn_near, ffn_far), chunk * each, each, side, 2)

    def up_by_low(index, chunk):
        lefts = place.held((grad_near, grad_far))
        each = blocks // 4
        first = blocks + index * (blocks // 2) + chunk * each
        return outer_tokens(lefts, (ffn_near, ffn_far), first, each, 0, 1)

    ffn_far_sum = far_sum(grad_blocks, w_ffn, dot_back)
    ffn = Flow(place.pair_back(gate_by_side, up_by_low))
    ffn_near_sum = near_sum(grad_blocks, w_ffn, dot_back)
    ffn_far_sum, ffn_near_sum = place.meet([ffn], ffn_far_sum, ffn_near_sum)
    place.before = ()
    grad_ffn_in = (ffn_near_sum + ffn_far_sum.astype(F32)).reshape(inputs.shape)
    grad_ffn_gain = jnp.sum(grad_ffn_in * normed_mid * scale_ffn, axis=(0, 1))
    grad_mod_ffn_scale = jnp.sum(grad_ffn_in * normed_mid * full_gain_ffn, axis=1)
    grad_hidden = upstream + rms_back(
        grad_ffn_in * full_gain_ffn * scale_ffn, normed_mid, inverse_mid
    )

    grad_attn_branch = (grad_hidden * tanh_attn).astype(BF16).reshape(-1, width)
    grad_mod_attn_gate = jnp.sum(grad_hidden * attn_branch, axis=1) * (
        1.0 - tanh_attn[:, 0] * tanh_attn[:, 0]
    )
    attn_grad_far = place.team_swap(grad_attn_branch)
    attn_grad_near = jnp.concatenate([grad_attn_branch, place.core_swap(grad_attn_branch)], axis=0)

    def heads_back(row_of, first, cap_raw, crossed, grad):
        grad_mixed = dot_back(w_out, grad).astype(BF16)
        result = attend_back(
            row_of, first, heads, sizes, qkv_raw, cap_raw, *tables, crossed, grad_mixed
        )
        return list(result)

    near = heads_back(rows_from(0), 0, near_raw, near_crossed, attn_grad_near)
    attn_grad_far, near[0] = place.meet([ffn], attn_grad_far, near[0])
    place.before = ()
    place.done(place.operand)
    attn_grad_far = jnp.concatenate([attn_grad_far, place.core_swap(attn_grad_far)], axis=0)
    grad_rows = outer_rows(
        (branch_near, branch_far, *place.held((act_near, act_far))),
        (
            attn_grad_near,
            attn_grad_far,
            mixed_near,
            jnp.concatenate(mixed_blocks[2:], axis=0),
        ),
    )
    down = Flow(place.rows_back(grad_rows))
    attn_grad_far = after(attn_grad_far, grad_rows)
    far = heads_back(far_row, half, far_raw, far_crossed, attn_grad_far)

    def mix(grads, count):
        shaped = grads.reshape(count, place.low, -1, grads.shape[1])
        return jnp.moveaxis(shaped, 0, 1).reshape(grads.shape)

    cap_lefts = []
    cap_rights = (cap_own, cap_core), (far_first, far_first_core, far_second, far_second_core)
    block = min(512, caption.shape[2] // 4)
    per = caption.shape[2] // 4 // block

    def cap_by_side(side, _):
        lefts = place.held(tuple(cap_lefts))
        return outer(lefts, cap_rights, 0, 1, [2 * per * side + i for i in range(per)], block)

    def cap_by_low(index, _):
        lefts = place.held(tuple(cap_lefts))
        columns = [start * per + i for start in (1, 3) for i in range(per)]
        return outer(lefts, cap_rights, index, 2, columns, block)

    far[0], far[2] = place.meet([ffn, down], far[0], far[2])
    down.step(())
    cap_lefts += [mix(near[2], 2), mix(far[2], 2)]
    cap = Flow(place.split_back(cap_by_side, cap_by_low, 2, 2, 2))
    cap.step(())
    place.meet([ffn, down, cap])
    place.meet([down, cap])
    place.done(place.before[0])
    place.before = ()
    plain = (*jnp.split(near[1], 2, axis=0), *jnp.split(far[1], 2, axis=0))
    plain = place.held(plain)
    attn_far_sum = far_sum(plain, w_qkv, dot_back)
    attn_near_sum = near_sum(plain, w_qkv, dot_back)
    turned = mix(jnp.concatenate([near[0], far[0]], axis=1), 3)
    columns = width // 4
    low_rows = jnp.concatenate([attn_all[:, i * columns : (i + 1) * columns] for i in (1, 3)], axis=1)

    def qkv_by_side(side, _):
        right = lax.dynamic_slice_in_dim(attn_all, 2 * side * columns, columns, axis=1)
        return dot(place.held(turned), right).astype(BF16)

    def qkv_by_low(index, _):
        return dot(place.part(place.held(turned), index, 0), low_rows).astype(BF16)

    attn_near_sum, attn_far_sum = place.meet([ffn, cap], attn_near_sum, attn_far_sum)
    place.before = ()
    place.done(place.operand)
    attn_near_sum, attn_far_sum = place.held((attn_near_sum, attn_far_sum))
    qkv = Flow(place.split_back(qkv_by_side, qkv_by_low, 3, 1, True))
    qkv.step(())
    grad_attn_in = (attn_near_sum + attn_far_sum.astype(F32)).reshape(inputs.shape)
    grad_gain_in = jnp.sum(grad_attn_in * normed_in * scale_attn, axis=(0, 1))
    grad_mod_attn_scale = jnp.sum(grad_attn_in * normed_in * full_gain_attn, axis=1)
    input_grad = (
        grad_hidden + rms_back(grad_attn_in * full_gain_attn * scale_attn, normed_in, inverse_in)
    ).astype(BF16)
    gate_parts = near[4] + far[4]
    gain_parts = jnp.sum(near[3] + far[3], axis=2)
    grad_head_gate = jnp.sum(gate_parts, axis=(1, 2)) * (1.0 - head_tanh * head_tanh)
    head_part = jnp.zeros_like(full_head_gate)
    head_part = lax.dynamic_update_slice_in_dim(
        head_part, grad_head_gate, place.quarter * heads, axis=0
    )
    parts = (
        grad_gain_in,
        grad_ffn_gain,
        gain_parts[0],
        gain_parts[1],
        gain_parts[2],
        head_part,
    )
    summed = place.total(jnp.concatenate(parts), "fsdp", (1, 2))
    branch_far_sum = far_sum(act_blocks, w_down, dot)
    branch_near_sum = near_sum(act_blocks, w_down, dot)
    summed, input_grad = place.meet([down, qkv, cap], summed, input_grad)
    place.before = ()
    qkv.step(())
    steps = [1 << i for i in range(place.copies.bit_length() - 1)]
    summed = place.total(summed, "dp", steps[:-2])
    summed, branch_near_sum = place.meet([qkv, cap, down], summed, branch_near_sum)
    place.before = ()
    summed = place.total(summed, "dp", steps[-2:])
    summed, branch_far_sum = place.meet([qkv, cap, down], summed, branch_far_sum)
    ffn_branch = (branch_near_sum + branch_far_sum.astype(F32)).reshape(inputs.shape)
    block_out = (hidden + tanh_ffn * ffn_branch).astype(BF16)
    grad_mod_ffn_gate = jnp.sum(upstream * ffn_branch, axis=1) * (
        1.0 - tanh_ffn[:, 0] * tanh_ffn[:, 0]
    )
    for flow in (ffn, qkv, cap, down):
        for _ in range(5):
            flow.step(flow.waiting)
    vectors, at = [], 0
    for vector in parts:
        length = vector.shape[0] // place.shards
        vectors.append(lax.dynamic_slice_in_dim(summed, at + place.fsdp * length, length))
        at += vector.shape[0]
    modulation_grad = jnp.stack(
        [grad_mod_attn_scale, grad_mod_attn_gate, grad_mod_ffn_scale, grad_mod_ffn_gate], axis=1
    )
    return (
        block_out,
        input_grad,
        modulation_grad,
        vectors[0],
        qkv.result[0],
        qkv.result[1],
        qkv.result[2],
        vectors[2],
        vectors[3],
        cap.result[0],
        cap.result[1],
        vectors[4],
        vectors[5],
        down.result[w_down.shape[0] :],
        vectors[1],
        ffn.result[0],
        ffn.result[1],
        down.result[: w_down.shape[0]],
    )


def solution(mesh):
    def shards(*arrays):
        return layer(Place(mesh), *arrays)

    rows = P(("dp", "fsdp"), None, None)
    marks = P(("dp", "fsdp"), None)
    vector = P("fsdp")
    weight = P("fsdp", None)
    grad = P("fsdp", "dp")
    return jax.shard_map(
        shards,
        mesh=mesh,
        in_specs=(
            (rows, rows, rows, marks, marks, marks, P(("dp", "fsdp")), vector)
            + (weight, weight, weight, vector, vector, weight, weight, vector, vector, weight)
            + (vector, weight, weight, weight, rows)
        ),
        out_specs=(
            (rows, rows, rows, vector, grad, grad, grad, vector, vector, grad, grad, vector)
            + (vector, grad, vector, grad, grad, grad)
        ),
        check_vma=False,
    )
```
